32 devices in a mesh: dp: 8 (over z, y), tensor: 4 (over x, core).
Axes of the slice: x: 2, y: 2, z: 4, core: 2. Of those that a mesh axis runs over, the one named last changes fastest.
Arguments:
- token_ids: int32 [16, 512], P('dp'), may hold values from 0 to 30719
- labels: int32 [16, 512], P('dp'), may hold values 0 or 1
- lengths: int32 [16], P('dp'), may hold values from 128 to 512, as said below
- pair_index: int32 [16], replicated, may hold values from 0 to 15, each once
- embed_table: float32 [31232, 1024], P(('dp', 'tensor')), may hold values from -0.12 to 0.12
- table_first: float32 [31232, 1024], P(('dp', 'tensor')), may hold values from -9.1552734e-05 to 9.1552734e-05
- table_second: float32 [31232, 1024], P(('dp', 'tensor')), may hold values from 5.2470448e-11 to 2.0988179e-10
- vectors: float32 [27650], replicated
- vector_first: float32 [27650], replicated, may hold values from -0.0007324219 to 0.0007324219
- vector_second: float32 [27650], replicated, may hold values from 1.1193695e-09 to 4.477478e-09
- in_proj: float32 [2, 4, 3, 4, 256, 256], P(None, None, None, 'tensor', 'dp'), may hold values from -0.1875 to 0.1875
- out_proj: float32 [2, 4, 4, 256, 256], P(None, 'tensor', None, 'dp'), may hold values from -3 to 3
- up_proj: float32 [2, 4, 16, 256, 256], P(None, None, 'tensor', 'dp'), may hold values from -0.1875 to 0.1875
- down_proj: float32 [2, 16, 4, 256, 256], P(None, 'tensor', None, 'dp'), may hold values from -0.09375 to 0.09375
- stats_left: float32 [4, 8, 12, 256, 256], P('tensor', 'dp')
- stats_right: float32 [4, 8, 12, 256, 256], P('tensor', 'dp')
- root_left: float32 [4, 8, 12, 256, 256], P('tensor', 'dp')
- root_right: float32 [4, 8, 12, 256, 256], P('tensor', 'dp')
Outputs:
- loss: float32 [3], replicated
- grad_norm: float32 [], replicated
- new_in_proj: float32 [2, 4, 3, 4, 256, 256], P(None, None, None, 'tensor', 'dp')
- new_out_proj: float32 [2, 4, 4, 256, 256], P(None, 'tensor', None, 'dp')
- new_up_proj: float32 [2, 4, 16, 256, 256], P(None, None, 'tensor', 'dp')
- new_down_proj: float32 [2, 16, 4, 256, 256], P(None, 'tensor', None, 'dp')
- grad_in_proj: float32 [2, 4, 3, 4, 256, 256], P(None, None, None, 'tensor', 'dp')
- grad_out_proj: float32 [2, 4, 4, 256, 256], P(None, 'tensor', None, 'dp')
- grad_up_proj: float32 [2, 4, 16, 256, 256], P(None, None, 'tensor', 'dp')
- grad_down_proj: float32 [2, 16, 4, 256, 256], P(None, 'tensor', None, 'dp')
- new_stats_left: float32 [4, 8, 12, 256, 256], P('tensor', 'dp')
- new_stats_right: float32 [4, 8, 12, 256, 256], P('tensor', 'dp')
- new_table: float32 [31232, 1024], P(('dp', 'tensor'))
- new_table_first: float32 [31232, 1024], P(('dp', 'tensor'))
- new_table_second: float32 [31232, 1024], P(('dp', 'tensor'))
- new_vectors: float32 [27650], replicated
- new_vector_first: float32 [27650], replicated
- new_vector_second: float32 [27650], replicated
- grad_layer_vectors: float32 [24576], replicated
The draws below stay inside these ranges and needn't reach their ends.
Inputs may be any that keep to these rules, and one draw needn't show every extreme that they name: `lengths`: the last sequence uses all 512 slots.
All inputs are finite; a program needn't handle non-finite values. No bound on the sum of `labels` on one device may be relied on, other than what follows from the above.
Results may differ from the reference program's by a relative error of at most 0.0085.
Values may be sent and summed in bfloat16 or wider, within the bound.
No kernel may reach another device: no remote copies, remote signals or barrier semaphores. Data moves between devices by JAX's collectives and lax.ppermute only.
A program may use at most 320 MiB of HBM per device.

```python
import math
import jax
import jax.numpy as jnp
import numpy as np
from jax import lax

D = 1024
HD = 64
FF = 4096
VOCAB = 30720
SEQLEN = 512
MINLEN = 128
LAYERS = 2
BS = 256
STEP = 10
SEQ_DEV = 2
SEQS = 16
ROWS = 31232
RB = 4
FB = 16
BLOCKS = 96
SLOTS = 12
NVEC = 27650
PARAMS = 57175042
N_DP = 8
N_TENSOR = 4


def draw_lengths(key, part):
    position = jnp.arange(SEQS)
    device_at = position // SEQ_DEV
    reach_to = MINLEN + (SEQLEN - MINLEN) * (device_at + 1) // N_DP
    drawn_ints = jax.random.randint(key, (SEQS,), 0, 1 << 20)
    length = MINLEN + drawn_ints % (reach_to - MINLEN + 1)
    return jnp.where(position == SEQS - 1, SEQLEN, length).astype(jnp.int32)


def identity_like():
    return (jnp.arange(BS)[:, None] == jnp.arange(BS)[None, :]).astype(jnp.float32)


def symmetric_noise(key, full_shape):
    normal_draw = jax.random.normal(key, full_shape, jnp.float32)
    return 0.5 * (normal_draw + jnp.swapaxes(normal_draw, -1, -2))


def dominant(key, salt, lower, upper, scale_by):
    salted = jax.random.fold_in(key, salt)
    first_key, second_key = jax.random.split(salted)
    full_shape = (N_TENSOR, N_DP, SLOTS, BS, BS)
    diagonal = jax.random.uniform(first_key, full_shape[:-1], jnp.float32, lower, upper)
    return scale_by * (diagonal[..., None] * identity_like() + 0.6 / BS ** 0.5 * symmetric_noise(second_key, full_shape))


def draw_stats_left(key, part):
    return dominant(key, 11, 1.0, 4.0, 0.0526 * BS / PARAMS)


def draw_stats_right(key, part):
    return dominant(key, 12, 1.0, 4.0, 0.0526 * BS / PARAMS)


def draw_root_left(key, part):
    return dominant(key, 13, 1.0, 2.0, (PARAMS / BS) ** 0.25)


def draw_root_right(key, part):
    return dominant(key, 14, 1.0, 2.0, (PARAMS / BS) ** 0.25)


def draw_vectors(key, part):
    first_key, second_key, third_key, fourth_key = jax.random.split(key, 4)
    per_layer = 8 * D + FF
    position = jnp.arange(NVEC)
    inner_at = position % per_layer
    in_layers = position < LAYERS * per_layer
    tail_at = position - LAYERS * per_layer
    gain_one = (inner_at >= 4 * D + FF) & (inner_at < 5 * D + FF)
    gain_two = (inner_at >= 6 * D + FF) & (inner_at < 7 * D + FF)
    is_gain = in_layers & (gain_one | gain_two) | ~in_layers & (tail_at < D)
    is_head = ~in_layers & (tail_at >= 2 * D) & (tail_at < 3 * D)
    normal_draw = jax.random.normal(first_key, (NVEC,), jnp.float32)
    gain_draw = jax.random.uniform(second_key, (NVEC,), jnp.float32, 0.6, 1.4)
    scale_draw = jax.random.uniform(third_key, (NVEC,), jnp.float32, 2.3, 2.9)
    offset_draw = jax.random.uniform(fourth_key, (NVEC,), jnp.float32, -2.2, -1.8)
    result = jnp.where(is_gain, gain_draw, 0.1 * normal_draw)
    result = jnp.where(is_head, normal_draw / D ** 0.5, result)
    result = jnp.where(position == NVEC - 2, offset_draw, result)
    return jnp.where(position == NVEC - 1, scale_draw, result)


def plant(values, own_key, low, high):
    extent = values.shape
    place = [jax.random.randint(jax.random.fold_in(own_key, axis), (), 0, extent[axis]) for axis in range(len(extent))]
    values = values.at[tuple(place)].set(low)
    longest = extent.index(max(extent))
    place[longest] = (place[longest] + 1) % extent[longest]
    return values.at[tuple(place)].set(high)


def level_of(own_key, shape, cuts, low, high):
    level = 1.0
    for dim, shards_of in cuts:
        draws = jax.random.uniform(jax.random.fold_in(jax.random.fold_in(own_key, 6), dim), (shards_of,), jnp.float32, low / len(cuts), high / len(cuts))
        level = level * jnp.repeat(jnp.exp(draws), shape[dim] // shards_of).reshape((-1,) + (1,) * (len(shape) - 1 - dim))
    return level


def rank_table(number_of, lean):
    portions = [(1 << 20) // math.isqrt(grade ** lean) + 1 for grade in range(1, number_of + 1)]
    deviation = 1 + sum(portions) // (1 << 30)
    return np.cumsum(np.array([max(1, weight // deviation) for weight in portions]))


def ranked(key, extent, count, lean):
    grid = rank_table(count, lean)
    pick = jax.random.randint(jax.random.fold_in(key, 1), extent, 0, int(grid[count - 1]))
    rank = jnp.searchsorted(jnp.asarray(grid, jnp.int32), pick, side="right")
    return jax.random.permutation(jax.random.fold_in(key, 2), count)[rank].astype(jnp.int32)


def gaussian(key, extent, width, most, shards=(), held_as=jnp.bfloat16):
    factor_of = level_of(key, extent, shards, -0.22, 0.18) if shards else 1.0
    entries = jax.random.normal(key, extent, jnp.float32) * width * factor_of
    return jnp.minimum(jnp.maximum(entries, -most), most).astype(held_as)


def setup_inputs(seed: int = 0) -> dict:
    arg_keys = jax.random.split(jax.random.key(seed), 19)
    token_ids = plant(ranked(arg_keys[0], (SEQS, SEQLEN), VOCAB, 1), jax.random.fold_in(arg_keys[0], 3), 0, VOCAB - 1).astype(jnp.int32)
    labels = plant((jax.random.randint(arg_keys[1], (SEQS, SEQLEN), 0, 100) < 15).astype(jnp.int32), jax.random.fold_in(arg_keys[1], 1), 0, 1)
    lengths = draw_lengths(jax.random.fold_in(arg_keys[18], 71), 0)
    pair_index = jax.random.permutation(arg_keys[3], SEQS).astype(jnp.int32)
    embed_table = gaussian(arg_keys[4], (ROWS, D), 0.02, 0.12, ((0, 32),), jnp.float32)
    table_first = gaussian(arg_keys[5], (ROWS, D), (0.111 / PARAMS ** 0.5), 9.1552734375e-05, ((0, 32),), jnp.float32)
    table_second = jnp.clip(jnp.exp(math.log(2.0988179250114314e-10) - 1.3862944 * jax.random.uniform(arg_keys[6], (ROWS, D), jnp.float32) ** level_of(arg_keys[6], (ROWS, D), ((0, 32),), -0.2, 0.2)), 5.2470448125285785e-11, 2.0988179250114314e-10)
    vectors = draw_vectors(jax.random.fold_in(arg_keys[18], 71), 0)
    vector_first = gaussian(arg_keys[8], (NVEC,), (0.89 / PARAMS ** 0.5), 0.0007324219, (), jnp.float32)
    vector_second = jnp.clip(jnp.exp(jax.random.uniform(arg_keys[9], (NVEC,), jnp.float32, math.log(1.1193694859912284e-09), math.log(4.477477943964914e-09))), 1.1193694859912284e-09, 4.477477943964914e-09)
    in_proj = gaussian(arg_keys[10], (LAYERS, RB, 3, RB, BS, BS), D ** -0.5, 0.1875, ((3, 4), (4, 8)), jnp.float32)
    out_proj = gaussian(arg_keys[11], (LAYERS, RB, RB, BS, BS), (max(2 * D // SEQLEN, 1)) ** -0.5, 3.0, ((1, 4), (3, 8)), jnp.float32)
    up_proj = gaussian(arg_keys[12], (LAYERS, RB, FB, BS, BS), D ** -0.5, 0.1875, ((2, 4), (3, 8)), jnp.float32)
    down_proj = gaussian(arg_keys[13], (LAYERS, FB, RB, BS, BS), FF ** -0.5, 0.09375, ((1, 4), (3, 8)), jnp.float32)
    stats_left = draw_stats_left(jax.random.fold_in(arg_keys[18], 71), 0)
    stats_right = draw_stats_right(jax.random.fold_in(arg_keys[18], 71), 0)
    root_left = draw_root_left(jax.random.fold_in(arg_keys[18], 71), 0)
    root_right = draw_root_right(jax.random.fold_in(arg_keys[18], 71), 0)
    return {"token_ids": token_ids, "labels": labels, "lengths": lengths, "pair_index": pair_index, "embed_table": embed_table, "table_first": table_first, "table_second": table_second, "vectors": vectors, "vector_first": vector_first, "vector_second": vector_second, "in_proj": in_proj, "out_proj": out_proj, "up_proj": up_proj, "down_proj": down_proj, "stats_left": stats_left, "stats_right": stats_right, "root_left": root_left, "root_right": root_right}


PRECISE = lax.Precision.HIGHEST
EPS_NORM = 1e-05
EPS_UNIT = 1e-06
CLIP_NORM = 1.0
BETA_ONE = 0.9
BETA_TWO = 0.999
ADAM_EPS = 1e-08
STAT_DECAY = 0.95
RATE_TABLE = 0.06
RATE_VECTOR = 0.5
RATE_MATRIX = 0.5
RATE_OUT = 4.0
DECAY_TABLE = 0.01
DECAY_MATRIX = 0.01
CON_WEIGHT = 16.0
MASK_FILL = -1000000000.0

@jax.custom_vjp
def low(v):
    return lax.optimization_barrier(v.astype(jnp.bfloat16)).astype(jnp.float32)

@jax.custom_vjp
def low_back(v):
    return v

def low_keep(v):
    return (low(v), None)

def low_pass(kept, grad):
    return (grad,)

def back_keep(v):
    return (v, None)

def back_low(kept, grad):
    return (low(grad),)
low.defvjp(low_keep, low_pass)
low_back.defvjp(back_keep, back_low)

def layer_norm(values, gain, shift):
    centre = values - lax.optimization_barrier(jnp.mean(values, axis=-1, keepdims=True))
    spread_sq = lax.optimization_barrier(jnp.mean(centre * centre, axis=-1, keepdims=True))
    return centre * lax.rsqrt(spread_sq + EPS_NORM) * gain + shift

def contrast(pooled, log_scale, pair_index):
    unit_rows = pooled * lax.rsqrt(lax.optimization_barrier(jnp.sum(pooled * pooled, axis=-1, keepdims=True)) + EPS_UNIT)
    partner = jnp.take(unit_rows, pair_index, axis=0)
    logits = jnp.exp(log_scale) * jnp.dot(unit_rows, partner.T, precision=PRECISE)
    matched = jnp.diagonal(logits)
    by_rows = jax.nn.logsumexp(logits, axis=1) - matched
    by_cols = jax.nn.logsumexp(logits, axis=0) - matched
    return 0.5 * (jnp.mean(by_rows) + jnp.mean(by_cols))

def adamw(weight, first, second, grad, rate, decay):
    first = BETA_ONE * first + (1 - BETA_ONE) * grad
    second = BETA_TWO * second + (1 - BETA_TWO) * grad * grad
    fixed_first = first / (1 - BETA_ONE ** STEP)
    fixed_second = second / (1 - BETA_TWO ** STEP)
    return (weight - rate * (fixed_first / (jnp.sqrt(fixed_second) + ADAM_EPS) + decay * weight), first, second)

def layer_vectors(vectors, layer_no):
    base_at = layer_no * (8 * D + FF)
    others = vectors[base_at + 2 * D + FF:base_at + 8 * D + FF].reshape(6, D)
    return (vectors[base_at:base_at + D], vectors[base_at + D:base_at + 2 * D], vectors[base_at + 2 * D:base_at + 2 * D + FF]) + tuple(others)

def to_matrices(in_proj, out_proj, up_proj, down_proj):
    attend_in = in_proj.transpose(0, 1, 4, 2, 3, 5).reshape(LAYERS, D, 3, D)
    attend_out = out_proj.transpose(0, 1, 3, 2, 4).reshape(LAYERS, D, D)
    feed_up = up_proj.transpose(0, 1, 3, 2, 4).reshape(LAYERS, D, FF)
    feed_down = down_proj.transpose(0, 1, 3, 2, 4).reshape(LAYERS, FF, D)
    return (attend_in, attend_out, feed_up, feed_down)

def attention(queries, keys_in, values_in, keys_live):
    scores = jnp.einsum('gqhe,gkhe->ghqk', queries, keys_in, precision=PRECISE) * HD ** (-0.5)
    scores = jnp.where(keys_live[:, None, None, :], low_back(scores), MASK_FILL)
    weights = jax.nn.softmax(scores, axis=-1)
    return jnp.einsum('ghqk,gkhe->gqhe', low(weights), values_in, precision=PRECISE)

def encode(params, token_group, length_group):
    table_low, vectors, attend_in, attend_out, feed_up, feed_down = params
    members = token_group.shape[0]
    places = jnp.arange(SEQLEN)
    embed = low_back(table_low[token_group] + table_low[VOCAB + places][None])
    tail_at = LAYERS * (8 * D + FF)
    hidden = layer_norm(embed, vectors[tail_at:tail_at + D], vectors[tail_at + D:tail_at + 2 * D])
    keys_live = places[None, :] < length_group[:, None]
    head_shape = (members, SEQLEN, D // HD, HD)
    for layer_no in range(LAYERS):
        bias_q, bias_v, bias_up, bias_out, bias_down, gain_one, shift_one, gain_two, shift_two = layer_vectors(vectors, layer_no)
        projected = jnp.einsum('gsd,dje->gsje', low(hidden), attend_in[layer_no], precision=PRECISE)
        queries = low(low_back(projected[:, :, 0] + bias_q)).reshape(head_shape)
        keys_in = low(low_back(projected[:, :, 1])).reshape(head_shape)
        values_in = low(low_back(projected[:, :, 2] + bias_v)).reshape(head_shape)
        mixed = low(low_back(attention(queries, keys_in, values_in, keys_live).reshape(members, SEQLEN, D)))
        branch = low_back(jnp.matmul(mixed, attend_out[layer_no], precision=PRECISE) + bias_out)
        middle = layer_norm(hidden + branch, gain_one, shift_one)
        hidden_pre = low_back(jnp.matmul(low(middle), feed_up[layer_no], precision=PRECISE) + bias_up)
        hidden_act = low(jax.nn.gelu(hidden_pre, approximate=False))
        fed_out = low_back(jnp.matmul(hidden_act, feed_down[layer_no], precision=PRECISE) + bias_down)
        hidden = layer_norm(middle + fed_out, gain_two, shift_two)
    return hidden

def group_terms(params, token_group, label_group, length_group):
    hidden = encode(params, token_group, length_group)
    vectors = params[1]
    tail_at = LAYERS * (8 * D + FF)
    logits_tok = jnp.matmul(hidden, vectors[tail_at + 2 * D:tail_at + 3 * D], precision=PRECISE) + vectors[tail_at + 3 * D]
    counted = (jnp.arange(SEQLEN)[None, :] < length_group[:, None]).astype(jnp.float32)
    bce = jnp.sum(counted * (jax.nn.softplus(logits_tok) - label_group.astype(jnp.float32) * logits_tok))
    token_weight = counted / length_group[:, None].astype(jnp.float32)
    pooled = lax.optimization_barrier(jnp.sum(hidden * token_weight[:, :, None], axis=1))
    return (bce, jnp.sum(counted), pooled)

def objective(table_in, vectors, in_proj, out_proj, up_proj, down_proj, token_ids, labels, lengths, pair_index):
    matrices = to_matrices(in_proj, out_proj, up_proj, down_proj)
    params = (low(table_in), vectors) + tuple((low(member) for member in matrices))
    group = math.gcd(SEQS, max(1, 4096 // SEQLEN))

    def shaped(values):
        return values.reshape((SEQS // group, group) + values.shape[1:])

    def step_fn(carry, batch):
        bce, count, pooled = jax.checkpoint(group_terms)(params, batch[0], batch[1], batch[2])
        return ((carry[0] + bce, carry[1] + count), pooled)
    start = (jnp.zeros((), jnp.float32), jnp.zeros((), jnp.float32))
    sums, pooled = lax.scan(step_fn, start, (shaped(token_ids), shaped(labels), shaped(lengths)))
    weighted = CON_WEIGHT * SEQS * contrast(pooled.reshape(SEQS, D), vectors[-1], pair_index)
    return (sums[0] + weighted, (sums[0], sums[1], weighted))

def to_blocks(grads):
    grad_in, grad_out, grad_up, grad_down = grads
    attn_span = D // BS // N_TENSOR
    feed_span = FF // BS // N_TENSOR
    per_rank = []
    for rank_no in range(N_TENSOR):
        pieces = (grad_in[:, :, :, rank_no * attn_span:(rank_no + 1) * attn_span], grad_out[:, rank_no * attn_span:(rank_no + 1) * attn_span], grad_up[:, :, rank_no * feed_span:(rank_no + 1) * feed_span], grad_down[:, rank_no * feed_span:(rank_no + 1) * feed_span])
        per_rank.append(jnp.concatenate([member.reshape(-1, BS, BS) for member in pieces], axis=0))
    stacked = jnp.stack(per_rank)
    padding = jnp.zeros((N_TENSOR, SLOTS * N_DP - BLOCKS, BS, BS), jnp.float32)
    joined = jnp.concatenate([stacked, padding], axis=1)
    return joined.reshape(N_TENSOR, SLOTS, N_DP, BS, BS).transpose(0, 2, 1, 3, 4)

def from_blocks(updates):
    attn_span = D // BS // N_TENSOR
    feed_span = FF // BS // N_TENSOR
    row_blocks = D // BS
    feed_blocks = FF // BS
    flat = updates.transpose(0, 2, 1, 3, 4).reshape(N_TENSOR, SLOTS * N_DP, BS, BS)[:, :BLOCKS]
    counts = [LAYERS * row_blocks * 3 * attn_span, LAYERS * attn_span * row_blocks, LAYERS * row_blocks * feed_span, LAYERS * feed_span * row_blocks]
    starts = [0, counts[0], counts[0] + counts[1], counts[0] + counts[1] + counts[2]]
    pieces = [flat[:, begin_at:begin_at + span_of] for begin_at, span_of in zip(starts, counts)]
    attend_in = pieces[0].reshape(N_TENSOR, LAYERS, row_blocks, 3, attn_span, BS, BS).transpose(1, 2, 3, 0, 4, 5, 6).reshape(LAYERS, row_blocks, 3, row_blocks, BS, BS)
    attend_out = pieces[1].reshape(N_TENSOR, LAYERS, attn_span, row_blocks, BS, BS).transpose(1, 0, 2, 3, 4, 5).reshape(LAYERS, row_blocks, row_blocks, BS, BS)
    feed_up = pieces[2].reshape(N_TENSOR, LAYERS, row_blocks, feed_span, BS, BS).transpose(1, 2, 0, 3, 4, 5).reshape(LAYERS, row_blocks, feed_blocks, BS, BS)
    feed_down = pieces[3].reshape(N_TENSOR, LAYERS, feed_span, row_blocks, BS, BS).transpose(1, 0, 2, 3, 4, 5).reshape(LAYERS, feed_blocks, row_blocks, BS, BS)
    return (attend_in, attend_out, feed_up, feed_down)

def precondition(grads, stats_left, stats_right, root_left, root_right):
    dealt_blocks = to_blocks(grads)

    def one_block(members):
        block_grad, left_stat, right_stat, left_root, right_root = members
        new_left = STAT_DECAY * left_stat + (1 - STAT_DECAY) * jnp.dot(block_grad, block_grad.T, precision=PRECISE)
        new_right = STAT_DECAY * right_stat + (1 - STAT_DECAY) * jnp.dot(block_grad.T, block_grad, precision=PRECISE)
        direction = jnp.dot(jnp.dot(left_root, block_grad, precision=PRECISE), right_root, precision=PRECISE)
        return (new_left, new_right, direction)
    flat = tuple((member.reshape(-1, BS, BS) for member in (dealt_blocks, stats_left, stats_right, root_left, root_right)))
    new_left, new_right, directions = lax.map(one_block, flat)
    full_shape = stats_left.shape
    return (new_left.reshape(full_shape), new_right.reshape(full_shape), from_blocks(directions.reshape(full_shape)))

def reference(token_ids, labels, lengths, pair_index, embed_table, table_first, table_second, vectors, vector_first, vector_second, in_proj, out_proj, up_proj, down_proj, stats_left, stats_right, root_left, root_right):

    def loss_of(table_in, vectors_in, in_weight, out_weight, up_weight, down_weight):
        return objective(table_in, vectors_in, in_weight, out_weight, up_weight, down_weight, token_ids, labels, lengths, pair_index)
    total, pull, parts = jax.vjp(loss_of, embed_table, vectors, in_proj, out_proj, up_proj, down_proj, has_aux=True)
    grads = pull(jnp.ones_like(total))
    grad_norm = jnp.sqrt(sum((jnp.sum(member * member) for member in grads)))
    factor = CLIP_NORM / jnp.maximum(grad_norm, CLIP_NORM)
    clipped = tuple((member * factor for member in grads))
    new_left, new_right, updates = precondition(clipped[2:], stats_left, stats_right, root_left, root_right)
    matrices = (in_proj, out_proj, up_proj, down_proj)
    rates = (RATE_MATRIX, RATE_OUT, RATE_MATRIX, RATE_MATRIX)
    new_mats = tuple((weight - rate * (update + DECAY_MATRIX * weight) for weight, update, rate in zip(matrices, updates, rates)))
    new_table, table_one, table_two = adamw(embed_table, table_first, table_second, clipped[0], RATE_TABLE, DECAY_TABLE)
    new_vectors, vector_one, vector_two = adamw(vectors, vector_first, vector_second, clipped[1], RATE_VECTOR, 0.0)
    loss = jnp.stack([parts[0], parts[1], parts[2]])
    layer_grads = clipped[1][:LAYERS * (8 * D + FF)]
    return (loss, grad_norm, new_mats[0], new_mats[1], new_mats[2], new_mats[3], clipped[2], clipped[3], clipped[4], clipped[5], new_left, new_right, new_table, table_one, table_two, new_vectors, vector_one, vector_two, layer_grads)
```

```python
import math

import jax
import jax.numpy as jnp
from jax import lax
from jax.experimental import pallas as pl
from jax.experimental.pallas import tpu as pltpu
from jax.sharding import Mesh
from jax.sharding import PartitionSpec as P

D = 1024
HD = 64
FF = 4096
VOCAB = 30720
STEP = 10


PRECISE = lax.Precision.HIGHEST
EPS_NORM = 1e-05
EPS_UNIT = 1e-06
CLIP_NORM = 1.0
BETA_ONE = 0.9
BETA_TWO = 0.999
ADAM_EPS = 1e-08
STAT_DECAY = 0.95
RATE_TABLE = 0.06
RATE_VECTOR = 0.5
RATE_MATRIX = 0.5
RATE_OUT = 4.0
DECAY_TABLE = 0.01
DECAY_MATRIX = 0.01
CON_WEIGHT = 16.0
MASK_FILL = -1000000000.0

BF = jnp.bfloat16
F32 = jnp.float32
GROUP = ("dp", "x")
EVERY = ("dp", "x", "core")
ROW_SLOTS = 24


def layer_norm(values, gain, shift):
    centre = values - jnp.mean(values, axis=-1, keepdims=True)
    spread_sq = jnp.mean(centre * centre, axis=-1, keepdims=True)
    return centre * lax.rsqrt(spread_sq + EPS_NORM) * gain + shift


def norm_back(values, gain, shift, upstream):
    ignored, pull = jax.vjp(layer_norm, values, gain, shift)
    return pull(upstream)


def contrast(pooled, log_scale, pair_index):
    unit_rows = pooled * lax.rsqrt(jnp.sum(pooled * pooled, axis=-1, keepdims=True) + EPS_UNIT)
    partner = jnp.take(unit_rows, pair_index, axis=0)
    logits = jnp.exp(log_scale) * jnp.dot(unit_rows, partner.T, precision=PRECISE)
    matched = jnp.diagonal(logits)
    by_rows = jax.nn.logsumexp(logits, axis=1) - matched
    by_cols = jax.nn.logsumexp(logits, axis=0) - matched
    return 0.5 * (jnp.mean(by_rows) + jnp.mean(by_cols))


def adamw(weight, first, second, grad, rate, decay):
    first = BETA_ONE * first + (1 - BETA_ONE) * grad
    second = BETA_TWO * second + (1 - BETA_TWO) * grad * grad
    fixed_first = first / (1 - BETA_ONE**STEP)
    fixed_second = second / (1 - BETA_TWO**STEP)
    return (
        weight - rate * (fixed_first / (jnp.sqrt(fixed_second) + ADAM_EPS) + decay * weight),
        first,
        second,
    )


def from_peer(values, axis, mask=1):
    size = lax.axis_size(axis)
    return lax.ppermute(values, axis, [(at, at ^ mask) for at in range(size)])


def peers():
    found = []
    for axis in ("core", "x", "dp"):
        mask = 1
        while mask < lax.axis_size(axis):
            found.append((axis, mask))
            mask = mask * 2
    return found


def routes():
    masks = [1]
    while masks[-1] * 2 < lax.axis_size("dp"):
        masks.append(masks[-1] * 2)
    across = [("x", 1)]
    near = [("dp", masks[0])]
    far = [("dp", mask) for mask in masks[1:]]
    return (
        across + near + far,
        near + across + far,
        across + far + near,
        near + far + across,
    )


def scatter_sum(parts, route):
    masks = sorted((mask for axis, mask in route if axis == "dp"), reverse=True)
    left = [("dp", mask) for mask in masks] + [("x", 1)]
    parts = parts.reshape((2,) * len(left) + parts.shape[-2:])
    for axis, mask in route:
        dim = left.index((axis, mask))
        left.pop(dim)
        bit = lax.axis_index(axis) // mask % 2
        keep = lax.dynamic_index_in_dim(parts, bit, dim, keepdims=False)
        away = lax.dynamic_index_in_dim(parts, 1 - bit, dim, keepdims=False)
        parts = keep + from_peer(away, axis, mask)
    return parts


def sum_over_all(values):
    for axis, mask in peers():
        values = values + from_peer(values, axis, mask)
    return values


def gather_small(values, steps=()):
    mask = 1
    while mask < lax.axis_size("dp"):
        steps = steps + (("dp", mask),)
        mask = mask * 2
    for axis, mask in steps:
        other = from_peer(values, axis, mask)
        first = lax.axis_index(axis) // mask % 2 == 0
        values = jnp.where(
            first,
            jnp.concatenate([values, other], axis=0),
            jnp.concatenate([other, values], axis=0),
        )
    return values


def tree():
    count = lax.axis_size("dp") * lax.axis_size("x")
    holders = [count - 1]
    steps = []
    mask = 1
    while mask < count:
        steps.append([(at, at ^ mask) for at in holders])
        holders = holders + [at ^ mask for at in holders]
        mask = mask * 2
    return steps


def from_last(parts):
    at = lax.axis_index("dp") * lax.axis_size("x") + lax.axis_index("x")
    last = lax.axis_size("core") - 1
    value = jnp.where(lax.axis_index("core") == last, parts[last], from_peer(parts[0], "core"))
    for step in tree():
        found = lax.ppermute(value, GROUP, step)
        reached = jnp.any(at == jnp.array([there for here, there in step]))
        value = jnp.where(reached, found, value)
    return value


def to_last(value):
    total = value.astype(F32)
    for step in reversed(tree()):
        back = [(there, here) for here, there in step]
        total = total + lax.ppermute(total.astype(BF), GROUP, back).astype(F32)
    return jnp.concatenate([from_peer(total.astype(BF), "core").astype(F32), total], axis=0)


def collect(values):
    return jnp.concatenate([values, from_peer(values, "core")], axis=0)


def spread(values):
    half = values.shape[0] // 2
    return values[:half] + from_peer(values[half:].astype(BF), "core").astype(F32)


def column_sum(values):
    return jnp.sum(values.astype(F32), axis=0)


def fetch(pieces):
    low = pieces.astype(BF)
    whole = lax.all_gather(low, GROUP, axis=0, tiled=False)
    return whole.reshape((lax.axis_size("dp"), lax.axis_size("x")) + low.shape)


def fetch_layer(in_proj, out_proj, up_proj, down_proj, layer_no):
    rows, width = in_proj.shape[-2:]
    row_blocks = in_proj.shape[1]
    feed = up_proj.shape[2]
    pieces = [
        in_proj[layer_no].reshape(row_blocks, 3, rows, width).transpose(1, 0, 2, 3),
        out_proj[layer_no].reshape(1, row_blocks, rows, width),
        up_proj[layer_no].reshape(row_blocks, feed, rows, width),
        down_proj[layer_no].reshape(feed, row_blocks, rows, width),
    ]
    all_of = fetch(jnp.concatenate(pieces, axis=0))
    of_x = (1, all_of.shape[1], 0)
    second = (3, row_blocks, 0)
    return (
        (all_of, {"x": of_x, "low": (2, 3, 0), "high": second}),
        (all_of, {"x": of_x, "low": second, "high": (2, 1, 3)}),
        (all_of, {"x": of_x, "low": second, "high": (2, row_blocks, 4)}),
        (all_of, {"x": of_x, "low": second, "high": (2, feed, 4 + row_blocks)}),
    )


def wide():
    return pltpu.CompilerParams(vmem_limit_bytes=48 * 1024 * 1024)


def whole(shape):
    return pl.BlockSpec(shape, lambda step: (0,) * len(shape))


def columns_of(ref, at, width):
    if len(ref.shape) == 2:
        return ref[:, at * width : (at + 1) * width]
    per = ref.shape[2] // width
    return ref[at // per, :, at % per * width : (at % per + 1) * width]


def joined_rows(weights):
    if weights.shape[-2] % 16 == 0:
        return weights
    owners, ranks, first, second, rows, width = weights.shape
    moved = weights.transpose(1, 2, 3, 0, 4, 5)
    return moved.reshape(1, ranks, first, second, owners * rows, width)


def rows_product(left, weights, dims, over, across, outs, finish, by_column=()):
    weights = joined_rows(weights)
    owners, rows, width = weights.shape[0], weights.shape[4], weights.shape[5]
    side = owners * rows
    turned = "low" in over
    steps = 1
    for name in across:
        steps = steps * dims[name][1]
    tokens = left.shape[-2]
    block_sizes = [1] * 6
    block_sizes[0], block_sizes[4], block_sizes[5] = owners, rows, width
    for name in over:
        block_sizes[dims[name][0]] = dims[name][1]
    terms = [()]
    for name in over:
        terms = [term + (at,) for term in terms for at in range(dims[name][1])]

    def kernel(*refs):
        left_ref, weights_ref = refs[:2]
        total = None
        for number, term in enumerate(terms):
            at = [0] * 3
            for name, place in zip(over, term):
                at[dims[name][0] - 1] = place
            block = weights_ref[(slice(None),) + tuple(at)].reshape(side, width)
            part = columns_of(left_ref, number, side)
            contract = (((1,), (1 if turned else 0,)), ((), ()))
            term_out = lax.dot_general(part, block, contract, preferred_element_type=F32)
            total = term_out if total is None else total + term_out
        last_in = 2 + len(by_column)
        results = finish(total, *[ref[...] for ref in refs[2:last_in]])
        for ref, result in zip(refs[last_in:], results):
            ref[...] = result.astype(ref.dtype).reshape(ref.shape)

    def weights_at(step):
        place = [0] * 6
        for name in reversed(across):
            place[dims[name][0]] = dims[name][2] + lax.rem(step, dims[name][1])
            step = lax.div(step, dims[name][1])
        for name in over:
            place[dims[name][0]] = dims[name][2] // dims[name][1]
        return tuple(place)

    out_shapes = []
    out_specs = []
    for apart, dtype in outs:
        if apart == 1:
            out_shapes.append(jax.ShapeDtypeStruct((tokens, steps * side), dtype))
            out_specs.append(pl.BlockSpec((tokens, side), lambda step: (0, step)))
        else:
            per = steps // apart
            out_shapes.append(jax.ShapeDtypeStruct((apart, tokens, per * side), dtype))
            out_specs.append(
                pl.BlockSpec(
                    (1, tokens, side),
                    lambda step, per=per: (lax.div(step, per), 0, lax.rem(step, per)),
                )
            )
    work = steps * len(terms) * side * width
    return pl.pallas_call(
        kernel,
        grid=(steps,),
        in_specs=[whole(left.shape), pl.BlockSpec(tuple(block_sizes), weights_at)]
        + [
            pl.BlockSpec((member.shape[0], side), lambda step: (0, step)) for member in by_column
        ],
        out_specs=out_specs,
        out_shape=out_shapes,
        compiler_params=wide(),
        cost_estimate=pl.CostEstimate(
            flops=2 * tokens * work, bytes_accessed=2 * work + 2 * left.size, transcendentals=0
        ),
    )(left, weights, *by_column)


def block_grads(left, right, ranks, high, low, side, x_on_left):
    def kernel(left_ref, right_ref, out_ref):
        step = pl.program_id(0)
        for at in range(ranks if x_on_left else 1):
            begin = pl.multiple_of((at * high + step) * side, side)
            part = left_ref[:, pl.ds(begin, side)]
            for low_at in range(low):
                for rank in range(1 if x_on_left else ranks):
                    if x_on_left:
                        number, target = low_at, at
                    elif len(right_ref.shape) == 3:
                        number, target = low_at * ranks + rank, rank
                    else:
                        number, target = rank * low + low_at, rank
                    block = columns_of(right_ref, number, side)
                    out_ref[low_at, target] = lax.dot_general(
                        part, block, (((0,), (0,)), ((), ())), preferred_element_type=F32
                    ).astype(BF)

    return pl.pallas_call(
        kernel,
        grid=(high,),
        in_specs=[whole(left.shape), whole(right.shape)],
        out_specs=pl.BlockSpec((low, ranks, side, side), lambda step: (step, 0, 0, 0)),
        out_shape=jax.ShapeDtypeStruct((high * low, ranks, side, side), BF),
        compiler_params=wide(),
        cost_estimate=pl.CostEstimate(
            flops=2 * left.shape[-2] * high * low * ranks * side * side,
            bytes_accessed=2 * high * low * ranks * side * side,
            transcendentals=0,
        ),
    )(left, right)


PAIR = 2 * HD


def halves(values):
    lane = lax.broadcasted_iota(jnp.int32, values.shape, 1)
    nothing = jnp.zeros_like(values)
    return jnp.where(lane < HD, values, nothing), jnp.where(lane < HD, nothing, values)


def dot_nt(left, right):
    return lax.dot_general(left, right, (((1,), (1,)), ((), ())), preferred_element_type=F32)


def dot_nn(left, right):
    return lax.dot_general(left, right, (((1,), (0,)), ((), ())), preferred_element_type=F32)


def dot_tn(left, right):
    return lax.dot_general(left, right, (((0,), (0,)), ((), ())), preferred_element_type=F32)


def softmax_of(queries, keys_in, live):
    scores = dot_nt(queries, keys_in) * HD ** (-0.5)
    scores = jnp.where(live > 0, scores, MASK_FILL)
    grown = jnp.exp(scores - jnp.max(scores, axis=-1, keepdims=True))
    return grown / jnp.sum(grown, axis=-1, keepdims=True)


def attend_kernel(live_ref, qkv_ref, mixed_ref):
    live = live_ref[0]
    query_heads = halves(qkv_ref[0])
    value_heads = halves(qkv_ref[2])
    total = None
    for query, value in zip(query_heads, value_heads):
        weights = softmax_of(query, qkv_ref[1], live).astype(BF)
        part = dot_nn(weights, value)
        total = part if total is None else total + part
    mixed_ref[...] = total.astype(BF)


def attend_back_kernel(live_ref, qkv_ref, d_mixed_ref, d_qkv_ref):
    live = live_ref[0]
    query_heads = halves(qkv_ref[0])
    key_heads = halves(qkv_ref[1])
    d_heads = halves(d_mixed_ref[...])
    d_query = d_key = d_value = 0.0
    for query, key, d_out in zip(query_heads, key_heads, d_heads):
        weights = softmax_of(query, qkv_ref[1], live)
        d_value = d_value + dot_tn(weights.astype(BF), d_out)
        d_weights = dot_nt(d_out, qkv_ref[2])
        d_scores = weights * (
            d_weights - jnp.sum(weights * d_weights, axis=-1, keepdims=True)
        )
        d_scores = d_scores.astype(BF)
        d_query = d_query + dot_nn(d_scores, key)
        d_key = d_key + dot_tn(d_scores, query)
    scale_by = HD ** (-0.5)
    d_qkv_ref[0] = (d_query * scale_by).astype(BF)
    d_qkv_ref[1] = (d_key * scale_by).astype(BF)
    d_qkv_ref[2] = d_value.astype(BF)


def attend(qkv, live, d_mixed=None):
    seqs, slots = live.shape
    width = qkv.shape[2]
    pairs = width // PAIR
    mixed_spec = pl.BlockSpec((slots, PAIR), lambda seq, pair: (seq, pair))
    qkv_spec = pl.BlockSpec((3, slots, PAIR), lambda seq, pair: (0, seq, pair))
    specs = [pl.BlockSpec((1, 1, slots), lambda seq, pair: (seq, 0, 0)), qkv_spec]
    operands = [live.astype(F32).reshape(seqs, 1, slots), qkv]
    if d_mixed is None:
        out_spec, out_shape = mixed_spec, jax.ShapeDtypeStruct(qkv.shape[1:], BF)
        body, products = attend_kernel, 2
    else:
        specs.append(mixed_spec)
        operands.append(d_mixed)
        out_spec, out_shape = qkv_spec, jax.ShapeDtypeStruct(qkv.shape, BF)
        body, products = attend_back_kernel, 5
    return pl.pallas_call(
        body,
        grid=(seqs, pairs),
        in_specs=specs,
        out_specs=out_spec,
        out_shape=out_shape,
        compiler_params=wide(),
        cost_estimate=pl.CostEstimate(
            flops=2 * products * seqs * slots * slots * width * 2,
            bytes_accessed=2 * qkv.size * 2,
            transcendentals=seqs * slots * slots * width // HD,
        ),
    )(*operands)


def product(left, right):
    return jnp.dot(left, right, preferred_element_type=F32)


def product_tn(left, right):
    return lax.dot_general(left, right, (((0,), (0,)), ((), ())), preferred_element_type=F32)


def same(total):
    return (total,)


def plus(total, bias):
    return (total + bias,)


ROOT_HALF = 0.5**0.5
DENSITY = (2 * math.pi) ** (-0.5)


def plus_gelu(total, bias):
    total = total + bias
    return (total, total * (1.0 + lax.erf(total * ROOT_HALF)) * 0.5)


def times_gelu_slope(total, before):
    slope = 0.5 * (1.0 + lax.erf(before * ROOT_HALF)) + before * (
        DENSITY * jnp.exp(-0.5 * before * before)
    )
    return (total * slope,)


def layer_forward(residual, weights, pieces, keys_live):
    w_in, w_out, w_up, w_down = weights
    bias_q, bias_v, bias_up, bias_out, bias_down, gain_one, shift_one, gain_two, shift_two = pieces
    gathered = collect(residual.astype(BF))
    bias_in = jnp.concatenate([bias_q, jnp.zeros_like(bias_q), bias_v]).reshape(1, -1)
    (qkv,) = rows_product(
        gathered, *w_in, ("high",), ("low", "x"), [(3, BF)], plus, [bias_in]
    )
    mixed = attend(qkv, keys_live)
    (mixed_out,) = rows_product(mixed, *w_out, ("x", "high"), ("low",), [(1, F32)], same)
    first_in = residual + (spread(mixed_out) + bias_out)
    middle = layer_norm(first_in, gain_one, shift_one)
    spread_mid = collect(middle.astype(BF))
    hidden_pre, hidden_act = rows_product(
        spread_mid,
        *w_up,
        ("high",),
        ("x", "low"),
        [(1, F32), (1, BF)],
        plus_gelu,
        [bias_up.reshape(1, -1)],
    )
    (fed_out,) = rows_product(hidden_act, *w_down, ("x", "high"), ("low",), [(1, F32)], same)
    second_in = middle + (spread(fed_out) + bias_down)
    kept_values = (
        first_in,
        second_in,
        gathered,
        qkv,
        mixed,
        spread_mid,
        hidden_pre,
        hidden_act,
    )
    return (layer_norm(second_in, gain_two, shift_two), kept_values)


def layer_backward(upstream, kept_values, weights, pieces, keys_live):
    (
        first_in,
        second_in,
        gathered,
        qkv,
        mixed,
        spread_mid,
        hidden_pre,
        hidden_act,
    ) = kept_values
    w_in, w_out, w_up, w_down = weights
    gain_one, shift_one, gain_two, shift_two = pieces[5:]
    ranks, side = w_in[1]["x"][1], w_in[0].shape[-1]
    row_blocks, feed = w_in[1]["high"][1], w_up[1]["low"][1]
    d_second, d_gain_two, d_shift_two = norm_back(second_in, gain_two, shift_two, upstream)
    d_fed = d_second.astype(BF)
    d_fed_all = collect(d_fed)
    parts = block_grads(hidden_act, d_fed_all, ranks, feed, row_blocks, side, True)
    d_fed_all, parts = lax.optimization_barrier((d_fed_all, parts))
    yield "down", parts
    (d_pre,) = rows_product(
        d_fed_all, *w_down, ("low",), ("x", "high"), [(1, BF)], times_gelu_slope, [hidden_pre]
    )
    parts = block_grads(spread_mid, d_pre, ranks, row_blocks, feed, side, False)
    d_pre, parts = lax.optimization_barrier((d_pre, parts))
    yield "up", parts
    (d_up_in,) = rows_product(d_pre, *w_up, ("x", "low"), ("high",), [(1, F32)], same)
    d_middle = d_second + spread(d_up_in)
    d_first, d_gain_one, d_shift_one = norm_back(first_in, gain_one, shift_one, d_middle)
    d_branch = d_first.astype(BF)
    d_branch_all = collect(d_branch)
    parts = block_grads(mixed, d_branch_all, ranks, 1, row_blocks, side, True)
    d_branch_all, parts = lax.optimization_barrier((d_branch_all, parts))
    yield "out", parts
    (d_mixed,) = rows_product(d_branch_all, *w_out, ("low",), ("x", "high"), [(1, BF)], same)
    d_qkv = attend(qkv, keys_live, d_mixed)
    parts = block_grads(gathered, d_qkv, ranks, row_blocks, 3, side, False)
    d_qkv, parts = lax.optimization_barrier((d_qkv, parts))
    yield "in", parts
    (d_in,) = rows_product(d_qkv, *w_in, ("low", "x"), ("high",), [(1, F32)], same)
    d_residual = d_first + spread(d_in)
    bias_grads = (
        column_sum(d_qkv[0]),
        column_sum(d_qkv[2]),
        column_sum(d_pre),
        column_sum(d_branch),
        column_sum(d_fed),
        d_gain_one,
        d_shift_one,
        d_gain_two,
        d_shift_two,
    )
    yield "rest", (d_residual, bias_grads)


def shards(
    token_ids,
    labels,
    lengths,
    pair_index,
    embed_table,
    table_first,
    table_second,
    vectors,
    vector_first,
    vector_second,
    in_proj,
    out_proj,
    up_proj,
    down_proj,
    stats_left,
    stats_right,
    root_left,
    root_right,
):
    seq_dev, seq_slots = token_ids.shape
    layers = in_proj.shape[0]
    owners = lax.axis_size("dp")
    ranks = lax.axis_size("x")
    cores = lax.axis_size("core")
    devices = owners * ranks * cores
    owner_rank = lax.axis_index("dp")
    rank = lax.axis_index("x")
    core = lax.axis_index("core")
    device = (owner_rank * ranks + rank) * cores + core
    per_layer = 8 * D + FF
    tail_at = layers * per_layer
    block_size = in_proj.shape[-1]
    rows_per = in_proj.shape[-2]
    row_blocks = in_proj.shape[1]
    feed_blocks = up_proj.shape[2]
    slot_count = stats_left.shape[2]
    seqs = seq_dev // ranks
    group_rows = seqs * seq_slots
    local_rows = group_rows // cores

    def mine(values):
        return lax.dynamic_slice_in_dim(
            values.reshape(-1), rank * group_rows + core * local_rows, local_rows
        )

    my_rows = core * local_rows + jnp.arange(local_rows)
    my_sequence = rank * seqs + my_rows // seq_slots
    my_length = jnp.take(lengths, my_sequence)
    counted = (my_rows % seq_slots < my_length).astype(F32)
    my_labels = mine(labels).astype(F32)
    turned = (jnp.arange(group_rows) + core * local_rows) % group_rows
    keys_live = (turned % seq_slots < jnp.take(lengths, rank * seqs + turned // seq_slots)).reshape(
        seqs, seq_slots
    )

    shard_rows = embed_table.shape[0]
    all_ids = gather_small(token_ids).reshape(-1)
    last_base = VOCAB - (devices - 1) * shard_rows
    by_device = all_ids.reshape(devices, local_rows)
    holder = by_device // shard_rows
    earlier = jnp.arange(local_rows)[None, :] < jnp.arange(local_rows)[:, None]
    turn = jnp.sum(
        ((holder[:, :, None] == holder[:, None, :]) & earlier[None]).astype(jnp.int32), axis=2
    )
    rounds = jnp.max(turn) // ROW_SLOTS + 1
    own_index = by_device - device * shard_rows
    my_holder = lax.dynamic_index_in_dim(holder, device, 0, keepdims=False)
    my_turn = lax.dynamic_index_in_dim(turn, device, 0, keepdims=False)

    def plan(round_no):
        first = round_no * ROW_SLOTS
        here = (holder == device)[:, None, :] & (
            turn[:, None, :] - first == jnp.arange(ROW_SLOTS)[None, :, None]
        )
        row_of_slot = jnp.sum(jnp.where(here, own_index[:, None, :] + 1, 0), axis=2).reshape(-1)
        inside = (my_turn >= first) & (my_turn < first + ROW_SLOTS)
        my_slot = jnp.where(inside, my_holder * ROW_SLOTS + my_turn - first, -1)
        slot_of_token = (jnp.arange(devices * ROW_SLOTS)[:, None] == my_slot[None, :]).astype(BF)
        return row_of_slot, slot_of_token

    def exchange(filled):
        return lax.all_to_all(filled, EVERY, split_axis=0, concat_axis=0, tiled=True)

    def fetch_rows(round_no):
        row_of_slot, slot_of_token = plan(round_no)
        filled = jnp.take(embed_table, jnp.maximum(row_of_slot - 1, 0), axis=0).astype(BF)
        return product_tn(slot_of_token, exchange(filled))

    def return_rows(round_no, grads):
        row_of_slot, slot_of_token = plan(round_no)
        reached = exchange(product(slot_of_token, grads).astype(BF))
        picker = (row_of_slot[None, :] == 1 + jnp.arange(shard_rows)[:, None]).astype(BF)
        return product(picker, reached)

    def full_rows():
        table = lax.all_gather(embed_table.astype(BF), "dp", axis=0, tiled=True)
        tensor_ranks = ranks * cores

        def lookup(row_index):
            block_at = row_index // shard_rows
            inside = block_at % tensor_ranks == rank * cores + core
            at_row = block_at // tensor_ranks * shard_rows + row_index % shard_rows
            picked = jnp.take(table, jnp.where(inside, at_row, 0), axis=0)
            return jnp.where(inside[:, None], picked, jnp.zeros((), BF))

        rows = lookup(token_ids.reshape(-1))
        rows = rows + lookup(VOCAB + jnp.arange(rows.shape[0]) % seq_slots)
        return lax.psum_scatter(rows, ("x", "core"), scatter_dimension=0, tiled=True).astype(F32)

    places_last = last_base >= 0 and local_rows * cores == seq_slots
    if places_last:
        token_rows = lax.fori_loop(
            1, rounds, lambda at, rows: rows + fetch_rows(at), fetch_rows(0)
        )
        place_rows = from_last(
            [
                embed_table[last_base + at * local_rows : last_base + (at + 1) * local_rows].astype(BF)
                for at in range(cores)
            ]
        )
        embedded = token_rows + place_rows.astype(F32)
    else:
        embedded = full_rows()

    def by_rank(base_at, width):
        return jnp.concatenate(
            [
                lax.dynamic_slice_in_dim(vectors, base_at + (at * cores + core) * width, width)
                for at in range(ranks)
            ]
        )

    head_width = D // (ranks * cores)
    feed_width = FF // (ranks * cores)

    def pieces_of(layer_no):
        base_at = layer_no * per_layer
        others = vectors[base_at + 2 * D + FF : base_at + per_layer].reshape(6, D)
        return (
            by_rank(base_at, head_width),
            by_rank(base_at + D, head_width),
            by_rank(base_at + 2 * D, feed_width),
        ) + tuple(others)

    gain_embed = vectors[tail_at : tail_at + D]
    shift_embed = vectors[tail_at + D : tail_at + 2 * D]
    head_weight = vectors[tail_at + 2 * D : tail_at + 3 * D]
    residual = layer_norm(embedded, gain_embed, shift_embed)
    kept_all = []
    weights_all = []
    for layer_no in range(layers):
        weights = fetch_layer(in_proj, out_proj, up_proj, down_proj, layer_no)
        residual, kept_values = layer_forward(
            residual, weights, pieces_of(layer_no), keys_live
        )
        kept_all.append(kept_values)
        weights_all.append(weights)

    logits_tok = jnp.dot(residual, head_weight, precision=PRECISE) + vectors[tail_at + 3 * D]
    bce_part = jnp.sum(counted * (jax.nn.softplus(logits_tok) - my_labels * logits_tok))
    count_part = jnp.sum(counted)
    token_weight = counted / my_length.astype(F32)
    here_sequence = my_rows // seq_slots
    chooser = (here_sequence[None, :] == jnp.arange(seqs)[:, None]).astype(F32) * token_weight[None, :]
    pooled_here = jnp.dot(chooser, residual, precision=PRECISE)
    pooled = gather_small(pooled_here + from_peer(pooled_here, "core"), (("x", 1),))
    global_sequence = owner_rank * seq_dev + my_sequence

    def contrast_loss(pooled_in, log_scale):
        return CON_WEIGHT * pooled_in.shape[0] * contrast(pooled_in, log_scale, pair_index)

    scaled_con, con_pull = jax.vjp(contrast_loss, pooled, vectors[tail_at + 3 * D + 1])
    d_pooled, d_scale = con_pull(jnp.ones_like(scaled_con))
    d_logit = counted * (jax.nn.sigmoid(logits_tok) - my_labels)
    upstream = d_logit[:, None] * head_weight[None, :] + token_weight[:, None] * jnp.take(
        d_pooled, global_sequence, axis=0
    )
    d_head_weight = jnp.dot(d_logit, residual, precision=PRECISE)
    d_head_bias = jnp.sum(d_logit)
    leader = (device == 0).astype(F32)

    counts = {
        "in": row_blocks * 3,
        "out": row_blocks,
        "up": row_blocks * feed_blocks,
        "down": feed_blocks * row_blocks,
    }
    starts = {}
    begin_at = 0
    for name in ("in", "out", "up", "down"):
        starts[name] = begin_at
        begin_at = begin_at + layers * counts[name]
    block_count = begin_at
    ready = {}
    summed = {}

    def send_ready(offload):
        taken = []
        for slot in range(slot_count):
            numbers = range(slot * owners, min((slot + 1) * owners, block_count))
            if slot not in summed and all(number in ready for number in numbers):
                taken.append(slot)
        if offload and len(taken) > 0:
            array = ready[taken[0] * owners][0]
            array = array.reshape((len(taken), owners * ranks) + array.shape[2:])
            array = array.transpose(1, 0, 2, 3).reshape((-1,) + array.shape[2:])
            arrived = lax.psum_scatter(array, GROUP, scatter_dimension=0, tiled=True)
            for at, slot in enumerate(taken):
                summed[slot] = arrived[at]
            return
        for slot in taken:
            numbers = range(slot * owners, (slot + 1) * owners)
            members = []
            at = 0
            while at < owners:
                number = numbers[at]
                if number >= block_count:
                    members.append(jnp.zeros((owners - at, ranks, block_size, block_size), BF))
                    break
                array, offset = ready[number]
                span = 1
                while at + span < owners and ready.get(number + span, (None, 0))[0] is array:
                    span = span + 1
                members.append(array[offset : offset + span])
                at = at + span
            joined = jnp.concatenate(members, axis=0) if len(members) > 1 else members[0]
            summed[slot] = scatter_sum(joined, routes()[slot % 4])

    early = {("down", layers - 1), ("up", layers - 1), ("down", layers - 2)}
    bias_parts = [None] * layers
    for layer_no in reversed(range(layers)):
        for name, value in layer_backward(
            upstream,
            kept_all[layer_no],
            weights_all[layer_no],
            pieces_of(layer_no),
            keys_live,
        ):
            if name == "rest":
                upstream, bias_parts[layer_no] = value
                continue
            first = starts[name] + layer_no * counts[name]
            for at in range(counts[name]):
                ready[first + at] = (value, at)
            whole_slots = first % owners == 0 and counts[name] % owners == 0
            send_ready(whole_slots and (name, layer_no) in early)

    d_embed, d_gain_embed, d_shift_embed = norm_back(embedded, gain_embed, shift_embed, upstream)
    d_embed = d_embed.astype(BF)

    if places_last:
        table_shard = lax.fori_loop(
            1, rounds, lambda at, total: total + return_rows(at, d_embed), return_rows(0, d_embed)
        )
        place_grads = to_last(d_embed)
        table_shard = table_shard.at[last_base : last_base + seq_slots].add(
            jnp.where(device == devices - 1, place_grads, 0.0)
        )
    else:
        d_rows = lax.all_gather(d_embed, EVERY, axis=0, tiled=True)
        held = device * shard_rows + jnp.arange(shard_rows)
        all_places = VOCAB + jnp.arange(all_ids.shape[0]) % seq_slots
        picker = (all_ids[None, :] == held[:, None]).astype(BF) + (
            all_places[None, :] == held[:, None]
        ).astype(BF)
        table_shard = product(picker, d_rows)

    def placed(piece, base_at, width):
        row = jnp.zeros((ranks * cores * width,), F32)
        for at in range(ranks):
            row = lax.dynamic_update_slice(
                row, piece[at * width : (at + 1) * width], ((at * cores + core) * width,)
            )
        return row

    vector_rows = []
    for layer_no in range(layers):
        grad_items = bias_parts[layer_no]
        vector_rows.append(placed(grad_items[0], 0, head_width))
        vector_rows.append(placed(grad_items[1], 0, head_width))
        vector_rows.append(placed(grad_items[2], 0, feed_width))
        vector_rows.extend(grad_items[3:])
    vector_grad = jnp.concatenate(
        vector_rows
        + [d_gain_embed, d_shift_embed, d_head_weight, jnp.stack([d_head_bias, leader * d_scale])]
    )
    vector_total = sum_over_all(jnp.concatenate([vector_grad, jnp.stack([bce_part, count_part])]))
    offloaded = {
        starts[name] // owners + (layer_no * counts[name]) // owners + at
        for name, layer_no in early
        for at in range(counts[name] // owners)
    }
    order = [slot for slot in summed if slot not in offloaded] + [
        slot for slot in summed if slot in offloaded
    ]
    summed[order[0]], vector_total = lax.optimization_barrier((summed[order[0]], vector_total))
    bce_total, count_total = vector_total[-2], vector_total[-1]
    vector_total = vector_total[:-2]

    blocks_low = jnp.stack([summed[slot] for slot in range(slot_count)])
    blocks = blocks_low.astype(F32)
    squares = jnp.sum(table_shard * table_shard) + jnp.sum(blocks * blocks)
    square_total = sum_over_all(squares.reshape(1, 1))[0, 0]
    grad_norm = jnp.sqrt(square_total + jnp.sum(vector_total * vector_total))
    factor = CLIP_NORM / jnp.maximum(grad_norm, CLIP_NORM)

    left_root = root_left.reshape(blocks.shape)
    right_root = root_right.reshape(blocks.shape)
    returned = [None] * slot_count
    per_send = max(1, slot_count // 3)
    for begin_at in range(0, slot_count, per_send):
        taken = sorted(order[begin_at : begin_at + per_send])
        some = jnp.stack([summed[slot] for slot in taken])

        def roots(array):
            return jnp.stack([array[slot] for slot in taken])

        direction = jnp.einsum(
            "sij,sjk->sik",
            jnp.einsum(
                "sij,sjk->sik", roots(left_root), some.astype(F32), precision=lax.Precision.HIGH
            ),
            roots(right_root),
            precision=lax.Precision.HIGH,
        )
        both = jnp.stack([some, direction.astype(BF)])
        outgoing = both.reshape(2, len(taken), owners, rows_per, block_size).transpose(2, 0, 1, 3, 4)
        back = lax.all_to_all(outgoing, "dp", split_axis=0, concat_axis=0, tiled=True)
        for at, slot in enumerate(taken):
            returned[slot] = back[:, :, at]
    mine_back = (
        jnp.stack(returned)
        .transpose(2, 0, 1, 3, 4)
        .reshape(2, slot_count * owners, rows_per, block_size)[:, :block_count]
        .astype(F32)
        * factor
    )
    square_of = factor * factor * (1 - STAT_DECAY)
    new_left = STAT_DECAY * stats_left.reshape(blocks.shape) + square_of * jnp.einsum(
        "sij,skj->sik", blocks_low, blocks_low, preferred_element_type=F32
    )
    new_right = STAT_DECAY * stats_right.reshape(blocks.shape) + square_of * jnp.einsum(
        "sji,sjk->sik", blocks_low, blocks_low, preferred_element_type=F32
    )
    matrices = (in_proj, out_proj, up_proj, down_proj)
    new_weights = []
    clipped = []
    begin_at = 0
    rates = (RATE_MATRIX, RATE_OUT, RATE_MATRIX, RATE_MATRIX)
    for weight, rate in zip(matrices, rates):
        span_of = weight.size // (rows_per * block_size)
        part = mine_back[:, begin_at : begin_at + span_of].reshape((2,) + weight.shape)
        clipped.append(part[0])
        new_weights.append(weight - rate * (part[1] + DECAY_MATRIX * weight))
        begin_at = begin_at + span_of
    clipped_vectors = vector_total * factor
    new_table, table_one, table_two = adamw(
        embed_table, table_first, table_second, table_shard * factor, RATE_TABLE, DECAY_TABLE
    )
    new_vectors, vector_one, vector_two = adamw(
        vectors, vector_first, vector_second, clipped_vectors, RATE_VECTOR, 0.0
    )
    loss = jnp.stack([bce_total, count_total, scaled_con])
    return (
        loss,
        grad_norm,
        new_weights[0],
        new_weights[1],
        new_weights[2],
        new_weights[3],
        clipped[0],
        clipped[1],
        clipped[2],
        clipped[3],
        new_left.reshape(stats_left.shape),
        new_right.reshape(stats_right.shape),
        new_table,
        table_one,
        table_two,
        new_vectors,
        vector_one,
        vector_two,
        clipped_vectors[:tail_at],
    )


def solution(mesh):
    owners, tensor_ranks = mesh.shape["dp"], mesh.shape["tensor"]
    split = Mesh(mesh.devices.reshape(owners, tensor_ranks // 2, 2), EVERY)
    both = ("x", "core")
    placed = (
        P("dp", None),
        P("dp", None),
        P("dp"),
        P(),
        P(EVERY, None),
        P(EVERY, None),
        P(EVERY, None),
        P(),
        P(),
        P(),
        P(None, None, None, both, "dp", None),
        P(None, both, None, "dp", None),
        P(None, None, both, "dp", None),
        P(None, both, None, "dp", None),
        P(both, "dp", None, None, None),
        P(both, "dp", None, None, None),
        P(both, "dp", None, None, None),
        P(both, "dp", None, None, None),
    )
    matrices = placed[10:14]
    return jax.shard_map(
        shards,
        mesh=split,
        in_specs=placed,
        out_specs=(P(), P())
        + matrices
        + matrices
        + placed[14:16]
        + placed[4:7]
        + (P(), P(), P(), P()),
        check_vma=False,
    )
```

```python
import math

import jax
import jax.numpy as jnp
from jax import lax
from jax.experimental import pallas as pl
from jax.experimental.pallas import tpu as pltpu
from jax.sharding import Mesh
from jax.sharding import PartitionSpec as P

D = 1024
HD = 64
FF = 4096
VOCAB = 30720
STEP = 10


PRECISE = lax.Precision.HIGHEST
EPS_NORM = 1e-05
EPS_UNIT = 1e-06
CLIP_NORM = 1.0
BETA_ONE = 0.9
BETA_TWO = 0.999
ADAM_EPS = 1e-08
STAT_DECAY = 0.95
RATE_TABLE = 0.06
RATE_VECTOR = 0.5
RATE_MATRIX = 0.5
RATE_OUT = 4.0
DECAY_TABLE = 0.01
DECAY_MATRIX = 0.01
CON_WEIGHT = 16.0
MASK_FILL = -1000000000.0

BF = jnp.bfloat16
F32 = jnp.float32
GROUP = ("dp", "x")
EVERY = ("dp", "x", "core")
ROW_SLOTS = 24


def layer_norm(values, gain, shift):
    centre = values - jnp.mean(values, axis=-1, keepdims=True)
    spread_sq = jnp.mean(centre * centre, axis=-1, keepdims=True)
    return centre * lax.rsqrt(spread_sq + EPS_NORM) * gain + shift


def norm_back(values, gain, shift, upstream):
    ignored, pull = jax.vjp(layer_norm, values, gain, shift)
    return pull(upstream)


def contrast(pooled, log_scale, pair_index):
    unit_rows = pooled * lax.rsqrt(jnp.sum(pooled * pooled, axis=-1, keepdims=True) + EPS_UNIT)
    partner = jnp.take(unit_rows, pair_index, axis=0)
    logits = jnp.exp(log_scale) * jnp.dot(unit_rows, partner.T, precision=PRECISE)
    matched = jnp.diagonal(logits)
    by_rows = jax.nn.logsumexp(logits, axis=1) - matched
    by_cols = jax.nn.logsumexp(logits, axis=0) - matched
    return 0.5 * (jnp.mean(by_rows) + jnp.mean(by_cols))


def adamw(weight, first, second, grad, rate, decay):
    first = BETA_ONE * first + (1 - BETA_ONE) * grad
    second = BETA_TWO * second + (1 - BETA_TWO) * grad * grad
    fixed_first = first / (1 - BETA_ONE**STEP)
    fixed_second = second / (1 - BETA_TWO**STEP)
    return (
        weight - rate * (fixed_first / (jnp.sqrt(fixed_second) + ADAM_EPS) + decay * weight),
        first,
        second,
    )


def from_peer(values, axis, mask=1):
    size = lax.axis_size(axis)
    return lax.ppermute(values, axis, [(at, at ^ mask) for at in range(size)])


def peers():
    found = []
    for axis in ("core", "x", "dp"):
        mask = 1
        while mask < lax.axis_size(axis):
            found.append((axis, mask))
            mask = mask * 2
    return found


def scatter_sum(slots):
    masks = [1]
    while masks[-1] * 2 < lax.axis_size("dp"):
        masks.append(masks[-1] * 2)
    slots = slots.reshape((2,) * len(masks) + slots.shape[1:])
    for at, mask in enumerate(masks):
        bit = lax.axis_index("dp") // mask % 2
        dim = len(masks) - 1 - at
        away = lax.dynamic_index_in_dim(slots, 1 - bit, dim, keepdims=False)
        keep = lax.dynamic_index_in_dim(slots, bit, dim, keepdims=False)
        slots = keep + from_peer(away, "dp", mask)
    return slots


def sum_over_all(values):
    for axis, mask in peers():
        values = values + from_peer(values, axis, mask)
    return values


def gather_small(values, steps=()):
    mask = 1
    while mask < lax.axis_size("dp"):
        steps = steps + (("dp", mask),)
        mask = mask * 2
    for axis, mask in steps:
        other = from_peer(values, axis, mask)
        first = lax.axis_index(axis) // mask % 2 == 0
        values = jnp.where(
            first,
            jnp.concatenate([values, other], axis=0),
            jnp.concatenate([other, values], axis=0),
        )
    return values


def tree():
    count = lax.axis_size("dp") * lax.axis_size("x")
    holders = [count - 1]
    steps = []
    mask = count // 2
    while mask > 0:
        steps.append([(at, at ^ mask) for at in holders])
        holders = holders + [at ^ mask for at in holders]
        mask = mask // 2
    return steps


def from_last(parts):
    last = lax.axis_size("core") - 1
    return jnp.where(lax.axis_index("core") == last, parts[last], from_peer(parts[0], "core"))


def spread_from(value, step):
    at = lax.axis_index("dp") * lax.axis_size("x") + lax.axis_index("x")
    found = lax.ppermute(value, GROUP, step)
    reached = jnp.any(at == jnp.array([there for here, there in step]))
    return jnp.where(reached, found, value)


def to_last(value):
    total = value.astype(F32)
    for step in reversed(tree()):
        back = [(there, here) for here, there in step]
        total = total + lax.ppermute(total.astype(BF), GROUP, back).astype(F32)
    return jnp.concatenate([from_peer(total.astype(BF), "core").astype(F32), total], axis=0)


def after(values, *first):
    return lax.optimization_barrier((values,) + first)[0]


def collect(values):
    across = from_peer(values, "x")
    return jnp.concatenate([values, from_peer(values, "core")], axis=0), across


def complete(across):
    return jnp.concatenate([across, from_peer(across, "core")], axis=0)


def spread_first(other):
    rows = other.shape[0] // 2
    away = other[:rows] + from_peer(other[rows:].astype(BF), "core").astype(F32)
    return away.astype(BF)


def spread_last(own, away):
    rows = own.shape[0] // 2
    near = own[:rows] + from_peer(own[rows:].astype(BF), "core").astype(F32)
    return near + from_peer(away, "x").astype(F32)


def column_sum(*members):
    return sum(jnp.sum(values.astype(F32), axis=0) for values in members)


def fetch(pieces):
    return lax.all_gather(pieces, "dp", axis=0, tiled=False)[:, None]


def layer_rows(in_proj, out_proj, up_proj, down_proj, layer_no):
    rows, width = in_proj.shape[-2:]
    row_blocks = in_proj.shape[1]
    feed = up_proj.shape[2]
    attend_rows = [
        in_proj[layer_no].reshape(row_blocks, 3, rows, width).transpose(1, 0, 2, 3),
        out_proj[layer_no].reshape(1, row_blocks, rows, width),
    ]
    feed_rows = [
        up_proj[layer_no].reshape(row_blocks, feed, rows, width),
        down_proj[layer_no].reshape(feed, row_blocks, rows, width),
    ]
    return [jnp.concatenate(rows, axis=0).astype(BF) for rows in (attend_rows, feed_rows)]


def named_layer(attend_all, feed_all, row_blocks, feed):
    of_x = (1, attend_all.shape[1], 0)
    second = (3, row_blocks, 0)
    return (
        (attend_all, {"x": of_x, "low": (2, 3, 0), "high": second}),
        (attend_all, {"x": of_x, "low": second, "high": (2, 1, 3)}),
        (feed_all, {"x": of_x, "low": second, "high": (2, row_blocks, 0)}),
        (feed_all, {"x": of_x, "low": second, "high": (2, feed, row_blocks)}),
    )


def wide():
    return pltpu.CompilerParams(vmem_limit_bytes=48 * 1024 * 1024)


def whole(shape):
    return pl.BlockSpec(shape, lambda step: (0,) * len(shape))


def columns_of(ref, at, width):
    if len(ref.shape) == 2:
        return ref[:, at * width : (at + 1) * width]
    per = ref.shape[2] // width
    return ref[at // per, :, at % per * width : (at % per + 1) * width]


def joined_rows(weights):
    if weights.shape[-2] % 16 == 0:
        return weights
    owners, ranks, first, second, rows, width = weights.shape
    moved = weights.transpose(1, 2, 3, 0, 4, 5)
    return moved.reshape(1, ranks, first, second, owners * rows, width)


def rows_product(left, weights, dims, over, across, outs, finish, by_column=()):
    weights = joined_rows(weights)
    owners, rows, width = weights.shape[0], weights.shape[4], weights.shape[5]
    side = owners * rows
    turned = "low" in over
    steps = 1
    for name in across:
        steps = steps * dims[name][1]
    tokens = left.shape[-2]
    block_sizes = [1] * 6
    block_sizes[0], block_sizes[4], block_sizes[5] = owners, rows, width
    for name in over:
        block_sizes[dims[name][0]] = dims[name][1]
    terms = [()]
    for name in over:
        terms = [term + (at,) for term in terms for at in range(dims[name][1])]

    def kernel(*refs):
        left_ref, weights_ref = refs[:2]
        total = None
        for number, term in enumerate(terms):
            at = [0] * 3
            for name, place in zip(over, term):
                at[dims[name][0] - 1] = place
            block = weights_ref[(slice(None),) + tuple(at)].reshape(side, width)
            part = columns_of(left_ref, number, side)
            contract = (((1,), (1 if turned else 0,)), ((), ()))
            term_out = lax.dot_general(part, block, contract, preferred_element_type=F32)
            total = term_out if total is None else total + term_out
        last_in = 2 + len(by_column)
        results = finish(total, *[ref[...] for ref in refs[2:last_in]])
        for ref, result in zip(refs[last_in:], results):
            ref[...] = result.astype(ref.dtype).reshape(ref.shape)

    def weights_at(step):
        place = [0] * 6
        for name in reversed(across):
            place[dims[name][0]] = dims[name][2] + lax.rem(step, dims[name][1])
            step = lax.div(step, dims[name][1])
        for name in over:
            place[dims[name][0]] = dims[name][2] // dims[name][1]
        return tuple(place)

    out_shapes = []
    out_specs = []
    for apart, dtype in outs:
        if apart == 1:
            out_shapes.append(jax.ShapeDtypeStruct((tokens, steps * side), dtype))
            out_specs.append(pl.BlockSpec((tokens, side), lambda step: (0, step)))
        else:
            per = steps // apart
            out_shapes.append(jax.ShapeDtypeStruct((apart, tokens, per * side), dtype))
            out_specs.append(
                pl.BlockSpec(
                    (1, tokens, side),
                    lambda step, per=per: (lax.div(step, per), 0, lax.rem(step, per)),
                )
            )
    work = steps * len(terms) * side * width
    return pl.pallas_call(
        kernel,
        grid=(steps,),
        in_specs=[whole(left.shape), pl.BlockSpec(tuple(block_sizes), weights_at)]
        + [
            pl.BlockSpec((member.shape[0], side), lambda step: (0, step)) for member in by_column
        ],
        out_specs=out_specs,
        out_shape=out_shapes,
        compiler_params=wide(),
        cost_estimate=pl.CostEstimate(
            flops=2 * tokens * work, bytes_accessed=2 * work + 2 * left.size, transcendentals=0
        ),
    )(left, weights, *by_column)


def block_grads(lefts, rights, ranks, high, low, side, x_on_left, owners=None):
    count = len(lefts)

    def kernel(*refs):
        step = pl.program_id(0)
        out_ref = refs[2 * count]
        for at in range(ranks if x_on_left else 1):
            begin = pl.multiple_of((at * high + step) * side, side)
            parts = [ref[:, pl.ds(begin, side)] for ref in refs[:count]]
            for low_at in range(low):
                for rank in range(1 if x_on_left else ranks):
                    if x_on_left:
                        number, target = low_at, at
                    elif len(refs[count].shape) == 3:
                        number, target = low_at * ranks + rank, rank
                    else:
                        number, target = rank * low + low_at, rank
                    total = None
                    for part, right_ref in zip(parts, refs[count : 2 * count]):
                        block = columns_of(right_ref, number, side)
                        term = lax.dot_general(
                            part, block, (((0,), (0,)), ((), ())), preferred_element_type=F32
                        )
                        total = term if total is None else total + term
                    if owners is None:
                        out_ref[low_at, target] = total.astype(BF)
                    else:
                        out_ref[low_at, target, 0] = total.astype(BF)

    if owners is None:
        out_spec = pl.BlockSpec((low, ranks, side, side), lambda step: (step, 0, 0, 0))
        out_shape = (high * low, ranks, side, side)
    else:
        per = owners // low
        out_spec = pl.BlockSpec(
            (low, ranks, 1, side, side),
            lambda step: (lax.rem(step, per), 0, lax.div(step, per), 0, 0),
        )
        out_shape = (owners, ranks, high * low // owners, side, side)
    return pl.pallas_call(
        kernel,
        grid=(high,),
        in_specs=[whole(member.shape) for member in tuple(lefts) + tuple(rights)],
        out_specs=out_spec,
        out_shape=jax.ShapeDtypeStruct(out_shape, BF),
        compiler_params=wide(),
        cost_estimate=pl.CostEstimate(
            flops=2 * count * lefts[0].shape[-2] * high * low * ranks * side * side,
            bytes_accessed=2 * high * low * ranks * side * side,
            transcendentals=0,
        ),
    )(*lefts, *rights)


PAIR = 2 * HD


def halves(values):
    lane = lax.broadcasted_iota(jnp.int32, values.shape, 1)
    nothing = jnp.zeros_like(values)
    return jnp.where(lane < HD, values, nothing), jnp.where(lane < HD, nothing, values)


def dot_nt(left, right):
    return lax.dot_general(left, right, (((1,), (1,)), ((), ())), preferred_element_type=F32)


def dot_nn(left, right):
    return lax.dot_general(left, right, (((1,), (0,)), ((), ())), preferred_element_type=F32)


def dot_tn(left, right):
    return lax.dot_general(left, right, (((0,), (0,)), ((), ())), preferred_element_type=F32)


def softmax_of(queries, keys_in, live):
    scores = dot_nt(queries, keys_in) * HD ** (-0.5)
    scores = jnp.where(live > 0, scores, MASK_FILL)
    grown = jnp.exp(scores - jnp.max(scores, axis=-1, keepdims=True))
    return grown / jnp.sum(grown, axis=-1, keepdims=True)


def attend_kernel(live_ref, qkv_ref, mixed_ref):
    live = live_ref[0]
    query_heads = halves(qkv_ref[0])
    value_heads = halves(qkv_ref[2])
    total = None
    for query, value in zip(query_heads, value_heads):
        weights = softmax_of(query, qkv_ref[1], live).astype(BF)
        part = dot_nn(weights, value)
        total = part if total is None else total + part
    mixed_ref[...] = total.astype(BF)


def attend_back_kernel(live_ref, qkv_ref, d_mixed_ref, d_qkv_ref):
    live = live_ref[0]
    query_heads = halves(qkv_ref[0])
    key_heads = halves(qkv_ref[1])
    d_heads = halves(d_mixed_ref[...])
    d_query = d_key = d_value = 0.0
    for query, key, d_out in zip(query_heads, key_heads, d_heads):
        weights = softmax_of(query, qkv_ref[1], live)
        d_value = d_value + dot_tn(weights.astype(BF), d_out)
        d_weights = dot_nt(d_out, qkv_ref[2])
        d_scores = weights * (
            d_weights - jnp.sum(weights * d_weights, axis=-1, keepdims=True)
        )
        d_scores = d_scores.astype(BF)
        d_query = d_query + dot_nn(d_scores, key)
        d_key = d_key + dot_tn(d_scores, query)
    scale_by = HD ** (-0.5)
    d_qkv_ref[0] = (d_query * scale_by).astype(BF)
    d_qkv_ref[1] = (d_key * scale_by).astype(BF)
    d_qkv_ref[2] = d_value.astype(BF)


def attend(qkv, live, d_mixed=None):
    seqs, slots = live.shape
    width = qkv.shape[2]
    pairs = width // PAIR
    mixed_spec = pl.BlockSpec((slots, PAIR), lambda seq, pair: (seq, pair))
    qkv_spec = pl.BlockSpec((3, slots, PAIR), lambda seq, pair: (0, seq, pair))
    specs = [pl.BlockSpec((1, 1, slots), lambda seq, pair: (seq, 0, 0)), qkv_spec]
    operands = [live.astype(F32).reshape(seqs, 1, slots), qkv]
    if d_mixed is None:
        out_spec, out_shape = mixed_spec, jax.ShapeDtypeStruct(qkv.shape[1:], BF)
        body, products = attend_kernel, 2
    else:
        specs.append(mixed_spec)
        operands.append(d_mixed)
        out_spec, out_shape = qkv_spec, jax.ShapeDtypeStruct(qkv.shape, BF)
        body, products = attend_back_kernel, 5
    return pl.pallas_call(
        body,
        grid=(seqs, pairs),
        in_specs=specs,
        out_specs=out_spec,
        out_shape=out_shape,
        compiler_params=wide(),
        cost_estimate=pl.CostEstimate(
            flops=2 * products * seqs * slots * slots * width * 2,
            bytes_accessed=2 * qkv.size * 2,
            transcendentals=seqs * slots * slots * width // HD,
        ),
    )(*operands)


def product(left, right):
    return jnp.dot(left, right, preferred_element_type=F32)


def product_tn(left, right):
    return lax.dot_general(left, right, (((0,), (0,)), ((), ())), preferred_element_type=F32)


def same(total):
    return (total,)


def plus(total, bias):
    return (total + bias,)


ROOT_HALF = 0.5**0.5
DENSITY = (2 * math.pi) ** (-0.5)


def plus_gelu(total, bias):
    total = total + bias
    return (total, total * (1.0 + lax.erf(total * ROOT_HALF)) * 0.5)


def times_gelu_slope(total, before):
    slope = 0.5 * (1.0 + lax.erf(before * ROOT_HALF)) + before * (
        DENSITY * jnp.exp(-0.5 * before * before)
    )
    return (total * slope,)


def layer_forward(residual, weights, pieces, keys_live):
    w_in, w_out, w_up, w_down = weights
    bias_q, bias_v, bias_up, bias_out, bias_down, gain_one, shift_one, gain_two, shift_two = pieces
    bias_in = jnp.concatenate([bias_q, jnp.zeros_like(bias_q), bias_v]).reshape(1, -1)

    def mix(rows, live):
        (projected,) = rows_product(
            rows, *w_in, ("high",), ("low", "x"), [(3, BF)], plus, [bias_in]
        )
        return projected, attend(projected, live)

    def mix_out(mixed):
        return rows_product(mixed, *w_out, ("x", "high"), ("low",), [(1, F32)], same)[0]

    def feed(rows):
        return rows_product(
            rows,
            *w_up,
            ("high",),
            ("x", "low"),
            [(1, F32), (1, BF)],
            plus_gelu,
            [bias_up.reshape(1, -1)],
        )

    def feed_out(active):
        return rows_product(active, *w_down, ("x", "high"), ("low",), [(1, F32)], same)[0]

    own, across = collect(residual.astype(BF))
    own_qkv, own_mixed = mix(own, keys_live[0])
    other = complete(after(across, own_mixed))
    other_qkv, other_mixed = mix(other, keys_live[1])
    away = spread_first(mix_out(other_mixed))
    own_out = mix_out(after(own_mixed, away))
    first_in = residual + (spread_last(own_out, away) + bias_out)
    middle = layer_norm(first_in, gain_one, shift_one)
    own_mid, across = collect(middle.astype(BF))
    own_pre, own_act = feed(own_mid)
    other_mid = complete(after(across, own_act))
    other_pre, other_act = feed(other_mid)
    away = spread_first(feed_out(other_act))
    own_out = feed_out(after(own_act, away))
    second_in = middle + (spread_last(own_out, away) + bias_down)
    kept_values = (
        first_in,
        second_in,
        (own, other),
        (own_qkv, other_qkv),
        (own_mixed, other_mixed),
        (own_mid, other_mid),
        (own_pre, other_pre),
        (own_act, other_act),
    )
    return (layer_norm(second_in, gain_two, shift_two), kept_values)


def layer_backward(upstream, kept_values, weights, pieces, keys_live, dealt, emit):
    (
        first_in,
        second_in,
        gathered,
        qkv,
        mixed,
        spread_mid,
        hidden_pre,
        hidden_act,
    ) = kept_values
    w_in, w_out, w_up, w_down = weights
    gain_one, shift_one, gain_two, shift_two = pieces[5:]
    ranks, side = w_in[1]["x"][1], w_in[0].shape[-1]
    row_blocks, feed = w_in[1]["high"][1], w_up[1]["low"][1]
    d_second, d_gain_two, d_shift_two = norm_back(second_in, gain_two, shift_two, upstream)
    d_fed = d_second.astype(BF)

    def feed_back(rows, before):
        return rows_product(
            rows, *w_down, ("low",), ("x", "high"), [(1, BF)], times_gelu_slope, [before]
        )[0]

    def up_back(rows):
        return rows_product(rows, *w_up, ("x", "low"), ("high",), [(1, F32)], same)[0]

    own, across = collect(d_fed)
    own_pre = feed_back(own, hidden_pre[0])
    other = complete(after(across, own_pre))
    other_pre = feed_back(other, hidden_pre[1])
    away = spread_first(up_back(other_pre))
    own = after(own, away)
    parts = block_grads(hidden_act, (own, other), ranks, feed, row_blocks, side, True, dealt["down"])
    own_pre = emit("down", parts, own_pre)
    d_pre = (own_pre, other_pre)
    parts = block_grads(spread_mid, d_pre, ranks, row_blocks, feed, side, False, dealt["up"])
    own_pre = emit("up", parts, own_pre)
    d_middle = d_second + spread_last(up_back(own_pre), away)
    d_first, d_gain_one, d_shift_one = norm_back(first_in, gain_one, shift_one, d_middle)
    d_branch = d_first.astype(BF)

    def mix_back(rows, projected, live):
        (d_mixed,) = rows_product(rows, *w_out, ("low",), ("x", "high"), [(1, BF)], same)
        return attend(projected, live, d_mixed)

    def in_back(rows):
        return rows_product(rows, *w_in, ("low", "x"), ("high",), [(1, F32)], same)[0]

    own, across = collect(d_branch)
    own_qkv = mix_back(own, qkv[0], keys_live[0])
    other = complete(after(across, own_qkv))
    other_qkv = mix_back(other, qkv[1], keys_live[1])
    away = spread_first(in_back(other_qkv))
    own = after(own, away)
    parts = block_grads(mixed, (own, other), ranks, 1, row_blocks, side, True)
    own_qkv = emit("out", parts, own_qkv)
    d_qkv = (own_qkv, other_qkv)
    parts = block_grads(gathered, d_qkv, ranks, row_blocks, 3, side, False)
    own_qkv = emit("in", parts, own_qkv)
    d_residual = d_first + spread_last(in_back(own_qkv), away)
    bias_grads = (
        column_sum(*[member[0] for member in d_qkv]),
        column_sum(*[member[2] for member in d_qkv]),
        column_sum(*d_pre),
        column_sum(d_branch),
        column_sum(d_fed),
        d_gain_one,
        d_shift_one,
        d_gain_two,
        d_shift_two,
    )
    return d_residual, bias_grads


def shards(
    token_ids,
    labels,
    lengths,
    pair_index,
    embed_table,
    table_first,
    table_second,
    vectors,
    vector_first,
    vector_second,
    in_proj,
    out_proj,
    up_proj,
    down_proj,
    stats_left,
    stats_right,
    root_left,
    root_right,
):
    seq_dev, seq_slots = token_ids.shape
    layers = in_proj.shape[0]
    owners = lax.axis_size("dp")
    ranks = lax.axis_size("x")
    cores = lax.axis_size("core")
    devices = owners * ranks * cores
    owner_rank = lax.axis_index("dp")
    rank = lax.axis_index("x")
    core = lax.axis_index("core")
    device = (owner_rank * ranks + rank) * cores + core
    per_layer = 8 * D + FF
    tail_at = layers * per_layer
    block_size = in_proj.shape[-1]
    rows_per = in_proj.shape[-2]
    row_blocks = in_proj.shape[1]
    feed_blocks = up_proj.shape[2]
    slot_count = stats_left.shape[2]
    seqs = seq_dev // ranks
    group_rows = seqs * seq_slots
    local_rows = group_rows // cores

    def mine(values):
        return lax.dynamic_slice_in_dim(
            values.reshape(-1), rank * group_rows + core * local_rows, local_rows
        )

    my_rows = core * local_rows + jnp.arange(local_rows)
    my_sequence = rank * seqs + my_rows // seq_slots
    my_length = jnp.take(lengths, my_sequence)
    counted = (my_rows % seq_slots < my_length).astype(F32)
    my_labels = mine(labels).astype(F32)
    turned = (jnp.arange(seq_slots) + core * local_rows) % seq_slots
    keys_live = [
        (turned < lax.dynamic_index_in_dim(lengths, which, 0, keepdims=False))[None]
        for which in (rank, rank ^ 1)
    ]

    rows_here = [
        layer_rows(in_proj, out_proj, up_proj, down_proj, layer_no) for layer_no in range(layers)
    ]
    rows_here[0][0], token_ids = lax.optimization_barrier((rows_here[0][0], token_ids))

    shard_rows = embed_table.shape[0]
    last_base = VOCAB - (devices - 1) * shard_rows
    places_last = last_base >= 0 and local_rows * cores == seq_slots
    all_ids = gather_small(token_ids).reshape(-1)
    if places_last:
        place_rows = from_last(
            [
                embed_table[last_base + at * local_rows : last_base + (at + 1) * local_rows].astype(BF)
                for at in range(cores)
            ]
        )
        hops = tree()
        place_rows = spread_from(place_rows, hops[0])
        all_ids, place_rows = lax.optimization_barrier((all_ids, place_rows))
    by_device = all_ids.reshape(devices, local_rows)
    holder = by_device // shard_rows
    earlier = jnp.arange(local_rows)[None, :] < jnp.arange(local_rows)[:, None]
    turn = jnp.sum(
        ((holder[:, :, None] == holder[:, None, :]) & earlier[None]).astype(jnp.int32), axis=2
    )
    rounds = jnp.max(turn) // ROW_SLOTS + 1
    own_index = by_device - device * shard_rows
    my_holder = lax.dynamic_index_in_dim(holder, device, 0, keepdims=False)
    my_turn = lax.dynamic_index_in_dim(turn, device, 0, keepdims=False)

    def plan(round_no):
        first = round_no * ROW_SLOTS
        here = (holder == device)[:, None, :] & (
            turn[:, None, :] - first == jnp.arange(ROW_SLOTS)[None, :, None]
        )
        row_of_slot = jnp.sum(jnp.where(here, own_index[:, None, :] + 1, 0), axis=2).reshape(-1)
        inside = (my_turn >= first) & (my_turn < first + ROW_SLOTS)
        my_slot = jnp.where(inside, my_holder * ROW_SLOTS + my_turn - first, -1)
        slot_of_token = (jnp.arange(devices * ROW_SLOTS)[:, None] == my_slot[None, :]).astype(BF)
        return row_of_slot, slot_of_token

    def exchange(filled):
        return lax.all_to_all(filled, EVERY, split_axis=0, concat_axis=0, tiled=True)

    def rows_to_send(round_no):
        rows = jnp.maximum(plan(round_no)[0] - 1, 0)
        return jnp.take(embed_table, rows, axis=0).astype(BF)

    def rows_reached(round_no, reached):
        return product_tn(plan(round_no)[1], reached)

    def return_rows(round_no, grads):
        row_of_slot, slot_of_token = plan(round_no)
        reached = exchange(product(slot_of_token, grads).astype(BF))
        picker = (row_of_slot[None, :] == 1 + jnp.arange(shard_rows)[:, None]).astype(BF)
        return product(picker, reached)

    def full_rows():
        table = lax.all_gather(embed_table.astype(BF), "dp", axis=0, tiled=True)
        tensor_ranks = ranks * cores

        def lookup(row_index):
            block_at = row_index // shard_rows
            inside = block_at % tensor_ranks == rank * cores + core
            at_row = block_at // tensor_ranks * shard_rows + row_index % shard_rows
            picked = jnp.take(table, jnp.where(inside, at_row, 0), axis=0)
            return jnp.where(inside[:, None], picked, jnp.zeros((), BF))

        rows = lookup(token_ids.reshape(-1))
        rows = rows + lookup(VOCAB + jnp.arange(rows.shape[0]) % seq_slots)
        return lax.psum_scatter(rows, ("x", "core"), scatter_dimension=0, tiled=True).astype(F32)

    fetched = [[fetch(rows) for rows in of_layer] for of_layer in rows_here]
    if places_last:
        place_rows = spread_from(place_rows, hops[1])
        filled, place_rows = lax.optimization_barrier((rows_to_send(0), place_rows))
        for step in hops[2:]:
            place_rows = spread_from(place_rows, step)
        reached, fetched[0][0] = lax.optimization_barrier((exchange(filled), fetched[0][0]))
        token_rows = lax.fori_loop(
            1,
            rounds,
            lambda at, rows: rows + rows_reached(at, exchange(rows_to_send(at))),
            rows_reached(0, reached),
        )
        embedded = token_rows + place_rows.astype(F32)
    else:
        embedded = full_rows()

    def by_rank(base_at, width):
        return lax.dynamic_slice_in_dim(vectors, base_at + (rank * cores + core) * width, width)

    head_width = D // (ranks * cores)
    feed_width = FF // (ranks * cores)

    def pieces_of(layer_no):
        base_at = layer_no * per_layer
        others = vectors[base_at + 2 * D + FF : base_at + per_layer].reshape(6, D)
        return (
            by_rank(base_at, head_width),
            by_rank(base_at + D, head_width),
            by_rank(base_at + 2 * D, feed_width),
        ) + tuple(others)

    gain_embed = vectors[tail_at : tail_at + D]
    shift_embed = vectors[tail_at + D : tail_at + 2 * D]
    head_weight = vectors[tail_at + 2 * D : tail_at + 3 * D]
    residual = layer_norm(embedded, gain_embed, shift_embed)
    kept_all = []
    weights_all = []
    for layer_no in range(layers):
        weights = named_layer(*fetched[layer_no], row_blocks, feed_blocks)
        residual, kept_values = layer_forward(
            residual, weights, pieces_of(layer_no), keys_live
        )
        kept_all.append(kept_values)
        weights_all.append(weights)

    logits_tok = jnp.dot(residual, head_weight, precision=PRECISE) + vectors[tail_at + 3 * D]
    bce_part = jnp.sum(counted * (jax.nn.softplus(logits_tok) - my_labels * logits_tok))
    count_part = jnp.sum(counted)
    token_weight = counted / my_length.astype(F32)
    here_sequence = my_rows // seq_slots
    chooser = (here_sequence[None, :] == jnp.arange(seqs)[:, None]).astype(F32) * token_weight[None, :]
    pooled_here = jnp.dot(chooser, residual, precision=PRECISE)
    pooled = gather_small(pooled_here + from_peer(pooled_here, "core"), (("x", 1),))
    global_sequence = owner_rank * seq_dev + my_sequence

    def contrast_loss(pooled_in, log_scale):
        return CON_WEIGHT * pooled_in.shape[0] * contrast(pooled_in, log_scale, pair_index)

    scaled_con, con_pull = jax.vjp(contrast_loss, pooled, vectors[tail_at + 3 * D + 1])
    d_pooled, d_scale = con_pull(jnp.ones_like(scaled_con))
    d_logit = counted * (jax.nn.sigmoid(logits_tok) - my_labels)
    upstream = d_logit[:, None] * head_weight[None, :] + token_weight[:, None] * jnp.take(
        d_pooled, global_sequence, axis=0
    )
    d_head_weight = jnp.dot(d_logit, residual, precision=PRECISE)
    d_head_bias = jnp.sum(d_logit)
    leader = (device == 0).astype(F32)

    counts = {
        "in": row_blocks * 3,
        "out": row_blocks,
        "up": row_blocks * feed_blocks,
        "down": feed_blocks * row_blocks,
    }
    starts = {}
    begin_at = 0
    for name in ("in", "out", "up", "down"):
        starts[name] = begin_at
        begin_at = begin_at + layers * counts[name]
    block_count = begin_at
    dealt = {
        name: owners if counts[name] % owners == 0 and starts[name] % owners == 0 else None
        for name in counts
    }
    ready = {}
    ready_slots = {}
    summed = {}
    sends = []

    def slot_parts(slot):
        if slot in ready_slots:
            array, at = ready_slots[slot]
            return array[:, :, at]
        numbers = range(slot * owners, (slot + 1) * owners)
        members = []
        at = 0
        while at < owners:
            number = numbers[at]
            if number >= block_count:
                members.append(jnp.zeros((owners - at, 1, block_size, block_size), BF))
                break
            array, offset = ready[number]
            span = 1
            while at + span < owners and ready.get(number + span, (None, 0))[0] is array:
                span = span + 1
            members.append(array[offset : offset + span])
            at = at + span
        return jnp.concatenate(members, axis=0)

    def once_there(slots, values):
        sums = jnp.stack([summed[slot] for slot in slots])
        values, sums = lax.optimization_barrier((values, sums))
        for at, slot in enumerate(slots):
            summed[slot] = sums[at]
        return values

    def sum_ready(next_in):
        taken = []
        for slot in range(slot_count):
            numbers = range(slot * owners, min((slot + 1) * owners, block_count))
            if slot not in summed and (
                slot in ready_slots or all(number in ready for number in numbers)
            ):
                taken.append(slot)
        if not taken:
            return next_in
        outgoing = jnp.concatenate([slot_parts(slot) for slot in taken], axis=1)
        next_in, outgoing = lax.optimization_barrier((next_in, outgoing))
        if len(sends) < 2:
            arrived = lax.psum_scatter(
                outgoing.reshape((-1,) + outgoing.shape[2:]), "dp", scatter_dimension=0, tiled=True
            )
        else:
            arrived = once_there(sends[-1], scatter_sum(outgoing))
        for at, slot in enumerate(taken):
            summed[slot] = arrived[at]
        sends.append(taken)
        return next_in

    flat_stats = (slot_count, block_size, block_size)
    left_root = root_left.reshape(flat_stats)
    right_root = root_right.reshape(flat_stats)
    returned = [None] * slot_count

    def send_back(taken, next_in=None):
        some = jnp.stack([summed[slot] for slot in taken])

        def roots(array):
            return jnp.stack([array[slot] for slot in taken])

        direction = jnp.einsum(
            "sij,sjk->sik",
            jnp.einsum(
                "sij,sjk->sik", roots(left_root), some.astype(F32), precision=lax.Precision.HIGH
            ),
            roots(right_root),
            precision=lax.Precision.HIGH,
        )
        both = jnp.stack([some, direction.astype(BF)])
        outgoing = both.reshape(2, len(taken), owners, rows_per, block_size)
        back = lax.all_to_all(
            outgoing.transpose(2, 0, 1, 3, 4), "dp", split_axis=0, concat_axis=0, tiled=True
        )
        if next_in is not None:
            next_in, back = lax.optimization_barrier((next_in, back))
        for at, slot in enumerate(taken):
            returned[slot] = back[:, :, at]
        return next_in

    def emit_of(layer_no):
        def emit(name, value, next_in):
            next_in, value = lax.optimization_barrier((next_in, value))
            first = starts[name] + layer_no * counts[name]
            if dealt[name]:
                for at in range(counts[name] // owners):
                    ready_slots[first // owners + at] = (value, at)
            else:
                for at in range(counts[name]):
                    ready[first + at] = (value, at)
            if name == "down" and layer_no == 0 and sends:
                next_in = once_there(sends[0], next_in)
            if name == "up" or (name == "in" and layer_no == 0):
                next_in = sum_ready(next_in)
            if name == "out" and layer_no == 0 and len(sends) > 1:
                next_in = send_back(sends[0], next_in)
                if layers in early_vectors:
                    next_in, early_vectors[layers] = lax.optimization_barrier(
                        (next_in, early_vectors[layers])
                    )
            return next_in

        return emit

    def placed(piece, width):
        row = jnp.zeros((ranks * cores * width,), F32)
        return lax.dynamic_update_slice(row, piece, ((rank * cores + core) * width,))

    bias_parts = [None] * layers
    early_vectors = {}

    def vector_rows_of(layer_no):
        grad_items = bias_parts[layer_no]
        return [
            placed(grad_items[0], head_width),
            placed(grad_items[1], head_width),
            placed(grad_items[2], feed_width),
        ] + list(grad_items[3:])

    for layer_no in reversed(range(layers)):
        if layer_no == 0:
            rows = []
            for done_no in range(1, layers):
                rows = rows + vector_rows_of(done_no)
            others = jnp.stack([d_head_bias, leader * d_scale, bce_part, count_part])
            early_vectors[layers] = sum_over_all(jnp.concatenate(rows + [d_head_weight, others]))
        upstream, bias_parts[layer_no] = layer_backward(
            upstream,
            kept_all[layer_no],
            weights_all[layer_no],
            pieces_of(layer_no),
            keys_live,
            dealt,
            emit_of(layer_no),
        )

    d_embed, d_gain_embed, d_shift_embed = norm_back(embedded, gain_embed, shift_embed, upstream)
    d_embed = d_embed.astype(BF)

    if places_last:
        table_shard = lax.fori_loop(
            1, rounds, lambda at, total: total + return_rows(at, d_embed), return_rows(0, d_embed)
        )
        place_grads = to_last(d_embed)
        table_shard = table_shard.at[last_base : last_base + seq_slots].add(
            jnp.where(device == devices - 1, place_grads, 0.0)
        )
    else:
        d_rows = lax.all_gather(d_embed, EVERY, axis=0, tiled=True)
        held = device * shard_rows + jnp.arange(shard_rows)
        all_places = VOCAB + jnp.arange(all_ids.shape[0]) % seq_slots
        picker = (all_ids[None, :] == held[:, None]).astype(BF) + (
            all_places[None, :] == held[:, None]
        ).astype(BF)
        table_shard = product(picker, d_rows)

    for at, taken in enumerate(sends):
        if returned[taken[0]] is None:
            last = summed[sends[-1][0]] if at < len(sends) - 1 else None
            last = send_back(taken, last)
            if last is not None:
                summed[sends[-1][0]] = last

    blocks_low = jnp.stack([summed[slot] for slot in range(slot_count)])
    blocks = blocks_low.astype(F32)
    squares = jnp.sum(table_shard * table_shard) + jnp.sum(blocks * blocks)
    late = sum_over_all(
        jnp.concatenate(vector_rows_of(0) + [d_gain_embed, d_shift_embed, squares.reshape(1)])
    )
    early = early_vectors[layers]
    vector_total = jnp.concatenate(
        [late[:per_layer], early[: tail_at - per_layer], late[per_layer:-1], early[tail_at - per_layer : -2]]
    )
    bce_total, count_total, square_total = early[-2], early[-1], late[-1]
    grad_norm = jnp.sqrt(square_total + jnp.sum(vector_total * vector_total))
    factor = CLIP_NORM / jnp.maximum(grad_norm, CLIP_NORM)

    mine_back = (
        jnp.stack(returned)
        .transpose(2, 0, 1, 3, 4)
        .reshape(2, slot_count * owners, rows_per, block_size)[:, :block_count]
        .astype(F32)
        * factor
    )
    square_of = factor * factor * (1 - STAT_DECAY)
    new_left = STAT_DECAY * stats_left.reshape(blocks.shape) + square_of * jnp.einsum(
        "sij,skj->sik", blocks_low, blocks_low, preferred_element_type=F32
    )
    new_right = STAT_DECAY * stats_right.reshape(blocks.shape) + square_of * jnp.einsum(
        "sji,sjk->sik", blocks_low, blocks_low, preferred_element_type=F32
    )
    matrices = (in_proj, out_proj, up_proj, down_proj)
    new_weights = []
    clipped = []
    begin_at = 0
    rates = (RATE_MATRIX, RATE_OUT, RATE_MATRIX, RATE_MATRIX)
    for weight, rate in zip(matrices, rates):
        span_of = weight.size // (rows_per * block_size)
        part = mine_back[:, begin_at : begin_at + span_of].reshape((2,) + weight.shape)
        clipped.append(part[0])
        new_weights.append(weight - rate * (part[1] + DECAY_MATRIX * weight))
        begin_at = begin_at + span_of
    clipped_vectors = vector_total * factor
    new_table, table_one, table_two = adamw(
        embed_table, table_first, table_second, table_shard * factor, RATE_TABLE, DECAY_TABLE
    )
    new_vectors, vector_one, vector_two = adamw(
        vectors, vector_first, vector_second, clipped_vectors, RATE_VECTOR, 0.0
    )
    loss = jnp.stack([bce_total, count_total, scaled_con])
    return (
        loss,
        grad_norm,
        new_weights[0],
        new_weights[1],
        new_weights[2],
        new_weights[3],
        clipped[0],
        clipped[1],
        clipped[2],
        clipped[3],
        new_left.reshape(stats_left.shape),
        new_right.reshape(stats_right.shape),
        new_table,
        table_one,
        table_two,
        new_vectors,
        vector_one,
        vector_two,
        clipped_vectors[:tail_at],
    )


def solution(mesh):
    owners, tensor_ranks = mesh.shape["dp"], mesh.shape["tensor"]
    split = Mesh(mesh.devices.reshape(owners, tensor_ranks // 2, 2), EVERY)
    both = ("x", "core")
    placed = (
        P("dp", None),
        P("dp", None),
        P("dp"),
        P(),
        P(EVERY, None),
        P(EVERY, None),
        P(EVERY, None),
        P(),
        P(),
        P(),
        P(None, None, None, both, "dp", None),
        P(None, both, None, "dp", None),
        P(None, None, both, "dp", None),
        P(None, both, None, "dp", None),
        P(both, "dp", None, None, None),
        P(both, "dp", None, None, None),
        P(both, "dp", None, None, None),
        P(both, "dp", None, None, None),
    )
    matrices = placed[10:14]
    return jax.shard_map(
        shards,
        mesh=split,
        in_specs=placed,
        out_specs=(P(), P())
        + matrices
        + matrices
        + placed[14:16]
        + placed[4:7]
        + (P(), P(), P(), P()),
        check_vma=False,
    )
```

```python
import math

import jax
import jax.numpy as jnp
from jax import lax
from jax.experimental import pallas as pl
from jax.experimental.pallas import tpu as pltpu
from jax.sharding import Mesh
from jax.sharding import PartitionSpec as P

D = 1024
HD = 64
FF = 4096
VOCAB = 30720
STEP = 10


PRECISE = lax.Precision.HIGHEST
EPS_NORM = 1e-05
EPS_UNIT = 1e-06
CLIP_NORM = 1.0
BETA_ONE = 0.9
BETA_TWO = 0.999
ADAM_EPS = 1e-08
STAT_DECAY = 0.95
RATE_TABLE = 0.06
RATE_VECTOR = 0.5
RATE_MATRIX = 0.5
RATE_OUT = 4.0
DECAY_TABLE = 0.01
DECAY_MATRIX = 0.01
CON_WEIGHT = 16.0
MASK_FILL = -1000000000.0

BF = jnp.bfloat16
F32 = jnp.float32
GROUP = ("dp", "x")
EVERY = ("dp", "x", "core")
ROW_SLOTS = 24


def layer_norm(values, gain, shift):
    centre = values - jnp.mean(values, axis=-1, keepdims=True)
    spread_sq = jnp.mean(centre * centre, axis=-1, keepdims=True)
    return centre * lax.rsqrt(spread_sq + EPS_NORM) * gain + shift


def norm_back(values, gain, shift, upstream):
    ignored, pull = jax.vjp(layer_norm, values, gain, shift)
    return pull(upstream)


def adamw(weight, first, second, grad, rate, decay):
    first = BETA_ONE * first + (1 - BETA_ONE) * grad
    second = BETA_TWO * second + (1 - BETA_TWO) * grad * grad
    fixed_first = first / (1 - BETA_ONE**STEP)
    fixed_second = second / (1 - BETA_TWO**STEP)
    return (
        weight - rate * (fixed_first / (jnp.sqrt(fixed_second) + ADAM_EPS) + decay * weight),
        first,
        second,
    )


def from_peer(values, axis, mask=1):
    size = lax.axis_size(axis)
    return lax.ppermute(values, axis, [(at, at ^ mask) for at in range(size)])


def peers():
    found = []
    for axis in ("core", "x", "dp"):
        mask = 1
        while mask < lax.axis_size(axis):
            found.append((axis, mask))
            mask = mask * 2
    return found


def scatter_sum(slots, after_first):
    masks = [1]
    while masks[-1] * 2 < lax.axis_size("dp"):
        masks.append(masks[-1] * 2)
    slots = slots.reshape((2,) * len(masks) + slots.shape[1:])
    for at, mask in enumerate(masks):
        bit = lax.axis_index("dp") // mask % 2
        dim = len(masks) - 1 - at
        away = lax.dynamic_index_in_dim(slots, 1 - bit, dim, keepdims=False)
        keep = lax.dynamic_index_in_dim(slots, bit, dim, keepdims=False)
        slots = keep + from_peer(away, "dp", mask)
        if at == 0:
            slots = after_first(slots)
    return slots


def sum_over_all(values):
    for axis, mask in peers():
        values = values + from_peer(values, axis, mask)
    return values


def gather_small(values, steps=()):
    mask = 1
    while mask < lax.axis_size("dp"):
        steps = steps + (("dp", mask),)
        mask = mask * 2
    for axis, mask in steps:
        other = from_peer(values, axis, mask)
        first = lax.axis_index(axis) // mask % 2 == 0
        values = jnp.where(
            first,
            jnp.concatenate([values, other], axis=0),
            jnp.concatenate([other, values], axis=0),
        )
    return values


def tree():
    count = lax.axis_size("dp")
    holders = [count - 1]
    steps = []
    mask = count // 2
    while mask > 0:
        steps.append([(at, at ^ mask) for at in holders])
        holders = holders + [at ^ mask for at in holders]
        mask = mask // 2
    return steps


def last_to_near():
    count = lax.axis_size("dp") * lax.axis_size("x")
    return [(count - 1, count - 2)]


def from_last(parts):
    last = lax.axis_size("core") - 1
    value = jnp.where(lax.axis_index("core") == last, parts[last], from_peer(parts[0], "core"))
    half = value.shape[0] // 2
    near = lax.ppermute(value[:half], GROUP, last_to_near())
    return jnp.where(lax.axis_index("x") == 0, near, value[half:])


def spread_from(value, step):
    found = lax.ppermute(value, "dp", step)
    reached = jnp.any(lax.axis_index("dp") == jnp.array([there for here, there in step]))
    return jnp.where(reached, found, value)


def both_halves(value):
    other = from_peer(value, "x")
    first = lax.axis_index("x") == 0
    return jnp.where(
        first,
        jnp.concatenate([value, other], axis=0),
        jnp.concatenate([other, value], axis=0),
    )


def to_last(value):
    half = value.shape[0] // 2
    first = lax.axis_index("x") == 0
    away = jnp.where(first, value[half:], value[:half])
    total = jnp.where(first, value[:half], value[half:]).astype(F32)
    total = total + from_peer(away, "x").astype(F32)
    for step in reversed(tree()):
        back = [(there, here) for here, there in step]
        total = total + lax.ppermute(total.astype(BF), "dp", back).astype(F32)
    back = [(there, here) for here, there in last_to_near()]
    near = lax.ppermute(total.astype(BF), GROUP, back).astype(F32)
    total = jnp.concatenate([near, total], axis=0)
    return jnp.concatenate([from_peer(total.astype(BF), "core").astype(F32), total], axis=0)


def after(values, *first):
    return lax.optimization_barrier((values,) + first)[0]


def collect(values):
    across = from_peer(values, "x")
    return jnp.concatenate([values, from_peer(values, "core")], axis=0), across


def complete(across):
    return jnp.concatenate([across, from_peer(across, "core")], axis=0)


def spread_first(other):
    rows = other.shape[0] // 2
    away = other[:rows] + from_peer(other[rows:].astype(BF), "core").astype(F32)
    return away.astype(BF)


def spread_last(own, away):
    rows = own.shape[0] // 2
    near = own[:rows] + from_peer(own[rows:].astype(BF), "core").astype(F32)
    return near + from_peer(away, "x").astype(F32)


def column_sum(*members):
    return sum(jnp.sum(values.astype(F32), axis=0) for values in members)


def fetch(pieces):
    return lax.all_gather(pieces, "dp", axis=0, tiled=False)[:, None]


def layer_rows(in_proj, out_proj, up_proj, down_proj, layer_no):
    rows, width = in_proj.shape[-2:]
    row_blocks = in_proj.shape[1]
    feed = up_proj.shape[2]
    attend_rows = [
        in_proj[layer_no].reshape(row_blocks, 3, rows, width).transpose(1, 0, 2, 3),
        out_proj[layer_no].reshape(1, row_blocks, rows, width),
    ]
    feed_rows = [
        up_proj[layer_no].reshape(row_blocks, feed, rows, width),
        down_proj[layer_no].reshape(feed, row_blocks, rows, width),
    ]
    return [jnp.concatenate(rows, axis=0).astype(BF) for rows in (attend_rows, feed_rows)]


def named_layer(attend_all, feed_all, row_blocks, feed):
    of_x = (1, attend_all.shape[1], 0)
    second = (3, row_blocks, 0)
    return (
        (attend_all, {"x": of_x, "low": (2, 3, 0), "high": second}),
        (attend_all, {"x": of_x, "low": second, "high": (2, 1, 3)}),
        (feed_all, {"x": of_x, "low": second, "high": (2, row_blocks, 0)}),
        (feed_all, {"x": of_x, "low": second, "high": (2, feed, row_blocks)}),
    )


def wide():
    return pltpu.CompilerParams(vmem_limit_bytes=48 * 1024 * 1024)


def whole(shape):
    return pl.BlockSpec(shape, lambda step: (0,) * len(shape))


def columns_of(ref, at, width):
    if len(ref.shape) == 2:
        return ref[:, at * width : (at + 1) * width]
    per = ref.shape[2] // width
    return ref[at // per, :, at % per * width : (at % per + 1) * width]


def joined_rows(weights):
    if weights.shape[-2] % 16 == 0:
        return weights
    owners, ranks, first, second, rows, width = weights.shape
    moved = weights.transpose(1, 2, 3, 0, 4, 5)
    return moved.reshape(1, ranks, first, second, owners * rows, width)


def rows_product(left, weights, dims, over, across, outs, finish, by_column=()):
    weights = joined_rows(weights)
    owners, rows, width = weights.shape[0], weights.shape[4], weights.shape[5]
    side = owners * rows
    turned = "low" in over
    steps = 1
    for name in across:
        steps = steps * dims[name][1]
    tokens = left.shape[-2]
    block_sizes = [1] * 6
    block_sizes[0], block_sizes[4], block_sizes[5] = owners, rows, width
    for name in over:
        block_sizes[dims[name][0]] = dims[name][1]
    terms = [()]
    for name in over:
        terms = [term + (at,) for term in terms for at in range(dims[name][1])]

    def kernel(*refs):
        left_ref, weights_ref = refs[:2]
        total = None
        for number, term in enumerate(terms):
            at = [0] * 3
            for name, place in zip(over, term):
                at[dims[name][0] - 1] = place
            block = weights_ref[(slice(None),) + tuple(at)].reshape(side, width)
            part = columns_of(left_ref, number, side)
            contract = (((1,), (1 if turned else 0,)), ((), ()))
            term_out = lax.dot_general(part, block, contract, preferred_element_type=F32)
            total = term_out if total is None else total + term_out
        last_in = 2 + len(by_column)
        results = finish(total, *[ref[...] for ref in refs[2:last_in]])
        for ref, result in zip(refs[last_in:], results):
            ref[...] = result.astype(ref.dtype).reshape(ref.shape)

    def weights_at(step):
        place = [0] * 6
        for name in reversed(across):
            place[dims[name][0]] = dims[name][2] + lax.rem(step, dims[name][1])
            step = lax.div(step, dims[name][1])
        for name in over:
            place[dims[name][0]] = dims[name][2] // dims[name][1]
        return tuple(place)

    out_shapes = []
    out_specs = []
    for apart, dtype in outs:
        if apart == 1:
            out_shapes.append(jax.ShapeDtypeStruct((tokens, steps * side), dtype))
            out_specs.append(pl.BlockSpec((tokens, side), lambda step: (0, step)))
        else:
            per = steps // apart
            out_shapes.append(jax.ShapeDtypeStruct((apart, tokens, per * side), dtype))
            out_specs.append(
                pl.BlockSpec(
                    (1, tokens, side),
                    lambda step, per=per: (lax.div(step, per), 0, lax.rem(step, per)),
                )
            )
    work = steps * len(terms) * side * width
    return pl.pallas_call(
        kernel,
        grid=(steps,),
        in_specs=[whole(left.shape), pl.BlockSpec(tuple(block_sizes), weights_at)]
        + [
            pl.BlockSpec((member.shape[0], side), lambda step: (0, step)) for member in by_column
        ],
        out_specs=out_specs,
        out_shape=out_shapes,
        compiler_params=wide(),
        cost_estimate=pl.CostEstimate(
            flops=2 * tokens * work, bytes_accessed=2 * work + 2 * left.size, transcendentals=0
        ),
    )(left, weights, *by_column)


def block_grads(lefts, rights, ranks, high, low, side, x_on_left, owners=None):
    count = len(lefts)

    def kernel(*refs):
        step = pl.program_id(0)
        out_ref = refs[2 * count]
        for at in range(ranks if x_on_left else 1):
            begin = pl.multiple_of((at * high + step) * side, side)
            parts = [ref[:, pl.ds(begin, side)] for ref in refs[:count]]
            for low_at in range(low):
                for rank in range(1 if x_on_left else ranks):
                    if x_on_left:
                        number, target = low_at, at
                    elif len(refs[count].shape) == 3:
                        number, target = low_at * ranks + rank, rank
                    else:
                        number, target = rank * low + low_at, rank
                    total = None
                    for part, right_ref in zip(parts, refs[count : 2 * count]):
                        block = columns_of(right_ref, number, side)
                        term = lax.dot_general(
                            part, block, (((0,), (0,)), ((), ())), preferred_element_type=F32
                        )
                        total = term if total is None else total + term
                    if owners is None:
                        out_ref[low_at, target] = total.astype(BF)
                    else:
                        out_ref[low_at, target, 0] = total.astype(BF)

    if owners is None:
        out_spec = pl.BlockSpec((low, ranks, side, side), lambda step: (step, 0, 0, 0))
        out_shape = (high * low, ranks, side, side)
    else:
        per = owners // low
        out_spec = pl.BlockSpec(
            (low, ranks, 1, side, side),
            lambda step: (lax.rem(step, per), 0, lax.div(step, per), 0, 0),
        )
        out_shape = (owners, ranks, high * low // owners, side, side)
    return pl.pallas_call(
        kernel,
        grid=(high,),
        in_specs=[whole(member.shape) for member in tuple(lefts) + tuple(rights)],
        out_specs=out_spec,
        out_shape=jax.ShapeDtypeStruct(out_shape, BF),
        compiler_params=wide(),
        cost_estimate=pl.CostEstimate(
            flops=2 * count * lefts[0].shape[-2] * high * low * ranks * side * side,
            bytes_accessed=2 * high * low * ranks * side * side,
            transcendentals=0,
        ),
    )(*lefts, *rights)


PAIR = 2 * HD


def halves(values):
    lane = lax.broadcasted_iota(jnp.int32, values.shape, 1)
    nothing = jnp.zeros_like(values)
    return jnp.where(lane < HD, values, nothing), jnp.where(lane < HD, nothing, values)


def dot_nt(left, right):
    return lax.dot_general(left, right, (((1,), (1,)), ((), ())), preferred_element_type=F32)


def dot_nn(left, right):
    return lax.dot_general(left, right, (((1,), (0,)), ((), ())), preferred_element_type=F32)


def dot_tn(left, right):
    return lax.dot_general(left, right, (((0,), (0,)), ((), ())), preferred_element_type=F32)


def softmax_of(queries, keys_in, live):
    scores = dot_nt(queries, keys_in) * HD ** (-0.5)
    scores = jnp.where(live > 0, scores, MASK_FILL)
    grown = jnp.exp(scores - jnp.max(scores, axis=-1, keepdims=True))
    return grown / jnp.sum(grown, axis=-1, keepdims=True)


def attend_kernel(live_ref, qkv_ref, mixed_ref):
    live = live_ref[0]
    query_heads = halves(qkv_ref[0])
    value_heads = halves(qkv_ref[2])
    total = None
    for query, value in zip(query_heads, value_heads):
        weights = softmax_of(query, qkv_ref[1], live).astype(BF)
        part = dot_nn(weights, value)
        total = part if total is None else total + part
    mixed_ref[...] = total.astype(BF)


def attend_back_kernel(live_ref, qkv_ref, d_mixed_ref, d_qkv_ref):
    live = live_ref[0]
    query_heads = halves(qkv_ref[0])
    key_heads = halves(qkv_ref[1])
    d_heads = halves(d_mixed_ref[...])
    d_query = d_key = d_value = 0.0
    for query, key, d_out in zip(query_heads, key_heads, d_heads):
        weights = softmax_of(query, qkv_ref[1], live)
        d_value = d_value + dot_tn(weights.astype(BF), d_out)
        d_weights = dot_nt(d_out, qkv_ref[2])
        d_scores = weights * (
            d_weights - jnp.sum(weights * d_weights, axis=-1, keepdims=True)
        )
        d_scores = d_scores.astype(BF)
        d_query = d_query + dot_nn(d_scores, key)
        d_key = d_key + dot_tn(d_scores, query)
    scale_by = HD ** (-0.5)
    d_qkv_ref[0] = (d_query * scale_by).astype(BF)
    d_qkv_ref[1] = (d_key * scale_by).astype(BF)
    d_qkv_ref[2] = d_value.astype(BF)


def attend(qkv, live, d_mixed=None):
    seqs, slots = live.shape
    width = qkv.shape[2]
    pairs = width // PAIR
    mixed_spec = pl.BlockSpec((slots, PAIR), lambda seq, pair: (seq, pair))
    qkv_spec = pl.BlockSpec((3, slots, PAIR), lambda seq, pair: (0, seq, pair))
    specs = [pl.BlockSpec((1, 1, slots), lambda seq, pair: (seq, 0, 0)), qkv_spec]
    operands = [live.astype(F32).reshape(seqs, 1, slots), qkv]
    if d_mixed is None:
        out_spec, out_shape = mixed_spec, jax.ShapeDtypeStruct(qkv.shape[1:], BF)
        body, products = attend_kernel, 2
    else:
        specs.append(mixed_spec)
        operands.append(d_mixed)
        out_spec, out_shape = qkv_spec, jax.ShapeDtypeStruct(qkv.shape, BF)
        body, products = attend_back_kernel, 5
    return pl.pallas_call(
        body,
        grid=(seqs, pairs),
        in_specs=specs,
        out_specs=out_spec,
        out_shape=out_shape,
        compiler_params=wide(),
        cost_estimate=pl.CostEstimate(
            flops=2 * products * seqs * slots * slots * width * 2,
            bytes_accessed=2 * qkv.size * 2,
            transcendentals=seqs * slots * slots * width // HD,
        ),
    )(*operands)


def product(left, right):
    return jnp.dot(left, right, preferred_element_type=F32)


def product_tn(left, right):
    return lax.dot_general(left, right, (((0,), (0,)), ((), ())), preferred_element_type=F32)


def same(total):
    return (total,)


def plus(total, bias):
    return (total + bias,)


ROOT_HALF = 0.5**0.5
DENSITY = (2 * math.pi) ** (-0.5)


def plus_gelu(total, bias):
    total = total + bias
    return (total, total * (1.0 + lax.erf(total * ROOT_HALF)) * 0.5)


def times_gelu_slope(total, before):
    slope = 0.5 * (1.0 + lax.erf(before * ROOT_HALF)) + before * (
        DENSITY * jnp.exp(-0.5 * before * before)
    )
    return (total * slope,)


def layer_forward(residual, weights, pieces, keys_live):
    w_in, w_out, w_up, w_down = weights
    bias_q, bias_v, bias_up, bias_out, bias_down, gain_one, shift_one, gain_two, shift_two = pieces
    bias_in = jnp.concatenate([bias_q, jnp.zeros_like(bias_q), bias_v]).reshape(1, -1)

    def mix(rows, live):
        (projected,) = rows_product(
            rows, *w_in, ("high",), ("low", "x"), [(3, BF)], plus, [bias_in]
        )
        return projected, attend(projected, live)

    def mix_out(mixed):
        return rows_product(mixed, *w_out, ("x", "high"), ("low",), [(1, F32)], same)[0]

    def feed(rows):
        return rows_product(
            rows,
            *w_up,
            ("high",),
            ("x", "low"),
            [(1, F32), (1, BF)],
            plus_gelu,
            [bias_up.reshape(1, -1)],
        )

    def feed_out(active):
        return rows_product(active, *w_down, ("x", "high"), ("low",), [(1, F32)], same)[0]

    own, across = collect(residual.astype(BF))
    own_qkv, own_mixed = mix(own, keys_live[0])
    other = complete(after(across, own_mixed))
    other_qkv, other_mixed = mix(other, keys_live[1])
    away = spread_first(mix_out(other_mixed))
    own_out = mix_out(after(own_mixed, away))
    first_in = residual + (spread_last(own_out, away) + bias_out)
    middle = layer_norm(first_in, gain_one, shift_one)
    own_mid, across = collect(middle.astype(BF))
    own_pre, own_act = feed(own_mid)
    other_mid = complete(after(across, own_act))
    other_pre, other_act = feed(other_mid)
    away = spread_first(feed_out(other_act))
    own_out = feed_out(after(own_act, away))
    second_in = middle + (spread_last(own_out, away) + bias_down)
    kept_values = (
        first_in,
        second_in,
        (own, other),
        (own_qkv, other_qkv),
        (own_mixed, other_mixed),
        (own_mid, other_mid),
        (own_pre, other_pre),
        (own_act, other_act),
    )
    return (layer_norm(second_in, gain_two, shift_two), kept_values)


def layer_backward(upstream, kept_values, weights, pieces, keys_live, dealt, emit):
    (
        first_in,
        second_in,
        gathered,
        qkv,
        mixed,
        spread_mid,
        hidden_pre,
        hidden_act,
    ) = kept_values
    w_in, w_out, w_up, w_down = weights
    gain_one, shift_one, gain_two, shift_two = pieces[5:]
    ranks, side = w_in[1]["x"][1], w_in[0].shape[-1]
    row_blocks, feed = w_in[1]["high"][1], w_up[1]["low"][1]
    d_second, d_gain_two, d_shift_two = norm_back(second_in, gain_two, shift_two, upstream)
    d_fed = d_second.astype(BF)

    def feed_back(rows, before):
        return rows_product(
            rows, *w_down, ("low",), ("x", "high"), [(1, BF)], times_gelu_slope, [before]
        )[0]

    def up_back(rows):
        return rows_product(rows, *w_up, ("x", "low"), ("high",), [(1, F32)], same)[0]

    own, across = collect(d_fed)
    own_pre = feed_back(own, hidden_pre[0])
    other = complete(after(across, own_pre))
    other_pre = feed_back(other, hidden_pre[1])
    away = spread_first(up_back(other_pre))
    own = after(own, away)
    parts = block_grads(hidden_act, (own, other), ranks, feed, row_blocks, side, True, dealt["down"])
    own_pre = emit("down", parts, own_pre)
    d_pre = (own_pre, other_pre)
    parts = block_grads(spread_mid, d_pre, ranks, row_blocks, feed, side, False, dealt["up"])
    own_pre = emit("up", parts, own_pre)
    d_middle = d_second + spread_last(up_back(own_pre), away)
    d_first, d_gain_one, d_shift_one = norm_back(first_in, gain_one, shift_one, d_middle)
    d_branch = d_first.astype(BF)

    def mix_back(rows, projected, live):
        (d_mixed,) = rows_product(rows, *w_out, ("low",), ("x", "high"), [(1, BF)], same)
        return attend(projected, live, d_mixed)

    def in_back(rows):
        return rows_product(rows, *w_in, ("low", "x"), ("high",), [(1, F32)], same)[0]

    own, across = collect(d_branch)
    own_qkv = mix_back(own, qkv[0], keys_live[0])
    other = complete(after(across, own_qkv))
    other_qkv = mix_back(other, qkv[1], keys_live[1])
    away = spread_first(in_back(other_qkv))
    own = after(own, away)
    parts = block_grads(mixed, (own, other), ranks, 1, row_blocks, side, True)
    own_qkv = emit("out", parts, own_qkv)
    d_qkv = (own_qkv, other_qkv)
    parts = block_grads(gathered, d_qkv, ranks, row_blocks, 3, side, False)
    own_qkv = emit("in", parts, own_qkv)
    d_residual = d_first + spread_last(in_back(own_qkv), away)
    bias_grads = (
        column_sum(*[member[0] for member in d_qkv]),
        column_sum(*[member[2] for member in d_qkv]),
        column_sum(*d_pre),
        column_sum(d_branch),
        column_sum(d_fed),
        d_gain_one,
        d_shift_one,
        d_gain_two,
        d_shift_two,
    )
    return d_residual, bias_grads


def precise(left, right, dims):
    return lax.dot_general(
        left, right, (dims, ((), ())), precision=PRECISE, preferred_element_type=F32
    )


def contrast_kernel(scale_ref, pairs_ref, pooled_ref, loss_ref, d_scale_ref, d_pooled_ref):
    pooled = pooled_ref[...]
    count = pooled.shape[0]
    norm = lax.rsqrt(jnp.sum(pooled * pooled, axis=-1, keepdims=True) + EPS_UNIT)
    unit = pooled * norm
    row_at = lax.broadcasted_iota(jnp.int32, (count, count), 0)
    column_at = lax.broadcasted_iota(jnp.int32, (count, count), 1)
    picks = (pairs_ref[...] == column_at).astype(F32)
    same_at = (row_at == column_at).astype(F32)
    scale = jnp.exp(scale_ref[...])
    partner = precise(picks, unit, ((1,), (0,)))
    logits = scale * precise(unit, partner, ((1,), (1,)))
    total = 0.0
    slope = -2.0 * same_at
    for axis in (1, 0):
        highest = jnp.max(logits, axis=axis, keepdims=True)
        grown = jnp.exp(logits - highest)
        each = jnp.sum(grown, axis=axis, keepdims=True)
        total = total + jnp.sum(highest + jnp.log(each), keepdims=True)
        slope = slope + grown / each
    total = total - 2.0 * jnp.sum(logits * same_at, keepdims=True)
    weight = 0.5 * CON_WEIGHT
    loss_ref[...] = weight * total
    slope = weight * slope
    d_scale_ref[...] = jnp.sum(slope * logits, keepdims=True)
    slope = slope * scale
    d_partner = precise(slope, unit, ((0,), (0,)))
    d_unit = precise(slope, partner, ((1,), (0,))) + precise(picks, d_partner, ((0,), (0,)))
    along = jnp.sum(d_unit * pooled, axis=-1, keepdims=True)
    d_pooled_ref[...] = norm * d_unit - pooled * (norm * norm * norm * along)


def contrast(pooled, log_scale, pair_index):
    loss, d_scale, d_pooled = pl.pallas_call(
        contrast_kernel,
        out_shape=[
            jax.ShapeDtypeStruct((1, 1), F32),
            jax.ShapeDtypeStruct((1, 1), F32),
            jax.ShapeDtypeStruct(pooled.shape, F32),
        ],
        compiler_params=wide(),
    )(log_scale.reshape(1, 1), pair_index.reshape(-1, 1), pooled)
    return loss[0, 0], d_scale[0, 0], d_pooled


def split_dot(left, right):
    total = None
    parts = []
    for operand in (left, right):
        if operand.dtype == BF:
            parts.append((operand,))
        else:
            high = operand.astype(BF)
            parts.append((high, (operand - high.astype(F32)).astype(BF)))
    for at, first in enumerate(parts[0]):
        for second in parts[1][: 2 - at]:
            term = dot_nn(first, second)
            total = term if total is None else total + term
    return total


def precondition(blocks, left_roots, right_roots, taken, owners):
    count, side = blocks.shape[0], blocks.shape[-1]
    rows = side // owners

    def kernel(slots_ref, block_ref, left_ref, right_ref, out_ref):
        block = block_ref[0]
        result = split_dot(split_dot(left_ref[0], block), right_ref[0])
        out_ref[:, 0, 0] = block.reshape(owners, rows, side)
        out_ref[:, 1, 0] = result.astype(BF).reshape(owners, rows, side)

    root_spec = pl.BlockSpec((1, side, side), lambda step, slots_ref: (slots_ref[step], 0, 0))
    return pl.pallas_call(
        kernel,
        grid_spec=pltpu.PrefetchScalarGridSpec(
            num_scalar_prefetch=1,
            grid=(count,),
            in_specs=[
                pl.BlockSpec((1, side, side), lambda step, slots_ref: (step, 0, 0)),
                root_spec,
                root_spec,
            ],
            out_specs=pl.BlockSpec(
                (owners, 2, 1, rows, side), lambda step, slots_ref: (0, 0, step, 0, 0)
            ),
        ),
        out_shape=jax.ShapeDtypeStruct((owners, 2, count, rows, side), BF),
        compiler_params=wide(),
        cost_estimate=pl.CostEstimate(
            flops=10 * count * side**3, bytes_accessed=14 * blocks.size, transcendentals=0
        ),
    )(jnp.array(taken, jnp.int32), blocks, left_roots, right_roots)


def shards(
    token_ids,
    labels,
    lengths,
    pair_index,
    embed_table,
    table_first,
    table_second,
    vectors,
    vector_first,
    vector_second,
    in_proj,
    out_proj,
    up_proj,
    down_proj,
    stats_left,
    stats_right,
    root_left,
    root_right,
):
    seq_dev, seq_slots = token_ids.shape
    layers = in_proj.shape[0]
    owners = lax.axis_size("dp")
    ranks = lax.axis_size("x")
    cores = lax.axis_size("core")
    devices = owners * ranks * cores
    owner_rank = lax.axis_index("dp")
    rank = lax.axis_index("x")
    core = lax.axis_index("core")
    device = (owner_rank * ranks + rank) * cores + core
    per_layer = 8 * D + FF
    tail_at = layers * per_layer
    block_size = in_proj.shape[-1]
    rows_per = in_proj.shape[-2]
    row_blocks = in_proj.shape[1]
    feed_blocks = up_proj.shape[2]
    slot_count = stats_left.shape[2]
    seqs = seq_dev // ranks
    group_rows = seqs * seq_slots
    local_rows = group_rows // cores

    def mine(values):
        return lax.dynamic_slice_in_dim(
            values.reshape(-1), rank * group_rows + core * local_rows, local_rows
        )

    my_rows = core * local_rows + jnp.arange(local_rows)
    my_sequence = rank * seqs + my_rows // seq_slots
    my_length = jnp.take(lengths, my_sequence)
    counted = (my_rows % seq_slots < my_length).astype(F32)
    my_labels = mine(labels).astype(F32)
    turned = (jnp.arange(seq_slots) + core * local_rows) % seq_slots
    keys_live = [
        (turned < lax.dynamic_index_in_dim(lengths, which, 0, keepdims=False))[None]
        for which in (rank, rank ^ 1)
    ]

    rows_here = [
        layer_rows(in_proj, out_proj, up_proj, down_proj, layer_no) for layer_no in range(layers)
    ]
    rows_here[0][0], token_ids = lax.optimization_barrier((rows_here[0][0], token_ids))

    shard_rows = embed_table.shape[0]
    last_base = VOCAB - (devices - 1) * shard_rows
    places_last = last_base >= 0 and local_rows * cores == seq_slots
    all_ids = gather_small(token_ids).reshape(-1)
    if places_last:
        place_rows = from_last(
            [
                embed_table[last_base + at * local_rows : last_base + (at + 1) * local_rows].astype(BF)
                for at in range(cores)
            ]
        )
        hops = tree()
        all_ids, place_rows = lax.optimization_barrier((all_ids, place_rows))
    by_device = all_ids.reshape(devices, local_rows)
    holder = by_device // shard_rows
    earlier = jnp.arange(local_rows)[None, :] < jnp.arange(local_rows)[:, None]
    turn = jnp.sum(
        ((holder[:, :, None] == holder[:, None, :]) & earlier[None]).astype(jnp.int32), axis=2
    )
    rounds = jnp.max(turn) // ROW_SLOTS + 1
    own_index = by_device - device * shard_rows
    my_holder = lax.dynamic_index_in_dim(holder, device, 0, keepdims=False)
    my_turn = lax.dynamic_index_in_dim(turn, device, 0, keepdims=False)

    def plan(round_no):
        first = round_no * ROW_SLOTS
        here = (holder == device)[:, None, :] & (
            turn[:, None, :] - first == jnp.arange(ROW_SLOTS)[None, :, None]
        )
        row_of_slot = jnp.sum(jnp.where(here, own_index[:, None, :] + 1, 0), axis=2).reshape(-1)
        inside = (my_turn >= first) & (my_turn < first + ROW_SLOTS)
        my_slot = jnp.where(inside, my_holder * ROW_SLOTS + my_turn - first, -1)
        slot_of_token = (jnp.arange(devices * ROW_SLOTS)[:, None] == my_slot[None, :]).astype(BF)
        return row_of_slot, slot_of_token

    def exchange(filled):
        return lax.all_to_all(filled, EVERY, split_axis=0, concat_axis=0, tiled=True)

    def rows_to_send(round_no):
        rows = jnp.maximum(plan(round_no)[0] - 1, 0)
        return jnp.take(embed_table, rows, axis=0).astype(BF)

    def rows_reached(round_no, reached):
        return product_tn(plan(round_no)[1], reached)

    def return_rows(round_no, grads):
        row_of_slot, slot_of_token = plan(round_no)
        reached = exchange(product(slot_of_token, grads).astype(BF))
        picker = (row_of_slot[None, :] == 1 + jnp.arange(shard_rows)[:, None]).astype(BF)
        return product(picker, reached)

    def full_rows():
        table = lax.all_gather(embed_table.astype(BF), "dp", axis=0, tiled=True)
        tensor_ranks = ranks * cores

        def lookup(row_index):
            block_at = row_index // shard_rows
            inside = block_at % tensor_ranks == rank * cores + core
            at_row = block_at // tensor_ranks * shard_rows + row_index % shard_rows
            picked = jnp.take(table, jnp.where(inside, at_row, 0), axis=0)
            return jnp.where(inside[:, None], picked, jnp.zeros((), BF))

        rows = lookup(token_ids.reshape(-1))
        rows = rows + lookup(VOCAB + jnp.arange(rows.shape[0]) % seq_slots)
        return lax.psum_scatter(rows, ("x", "core"), scatter_dimension=0, tiled=True).astype(F32)

    fetched = [[fetch(rows) for rows in of_layer] for of_layer in rows_here]
    if places_last:
        place_rows = spread_from(place_rows, hops[0])
        filled, place_rows = lax.optimization_barrier((rows_to_send(0), place_rows))
        for step in hops[1:]:
            place_rows = spread_from(place_rows, step)
        reached, fetched[0][0] = lax.optimization_barrier((exchange(filled), fetched[0][0]))
        token_rows = lax.fori_loop(
            1,
            rounds,
            lambda at, rows: rows + rows_reached(at, exchange(rows_to_send(at))),
            rows_reached(0, reached),
        )
        embedded = token_rows + both_halves(place_rows).astype(F32)
    else:
        embedded = full_rows()

    def by_rank(base_at, width):
        return lax.dynamic_slice_in_dim(vectors, base_at + (rank * cores + core) * width, width)

    head_width = D // (ranks * cores)
    feed_width = FF // (ranks * cores)

    def pieces_of(layer_no):
        base_at = layer_no * per_layer
        others = vectors[base_at + 2 * D + FF : base_at + per_layer].reshape(6, D)
        return (
            by_rank(base_at, head_width),
            by_rank(base_at + D, head_width),
            by_rank(base_at + 2 * D, feed_width),
        ) + tuple(others)

    gain_embed = vectors[tail_at : tail_at + D]
    shift_embed = vectors[tail_at + D : tail_at + 2 * D]
    head_weight = vectors[tail_at + 2 * D : tail_at + 3 * D]
    residual = layer_norm(embedded, gain_embed, shift_embed)
    kept_all = []
    weights_all = []
    for layer_no in range(layers):
        weights = named_layer(*fetched[layer_no], row_blocks, feed_blocks)
        residual, kept_values = layer_forward(
            residual, weights, pieces_of(layer_no), keys_live
        )
        kept_all.append(kept_values)
        weights_all.append(weights)

    logits_tok = jnp.dot(residual, head_weight, precision=PRECISE) + vectors[tail_at + 3 * D]
    bce_part = jnp.sum(counted * (jax.nn.softplus(logits_tok) - my_labels * logits_tok))
    count_part = jnp.sum(counted)
    token_weight = counted / my_length.astype(F32)
    here_sequence = my_rows // seq_slots
    chooser = (here_sequence[None, :] == jnp.arange(seqs)[:, None]).astype(F32) * token_weight[None, :]
    pooled_here = jnp.dot(chooser, residual, precision=PRECISE)
    pooled = gather_small(pooled_here + from_peer(pooled_here, "core"), (("x", 1),))
    global_sequence = owner_rank * seq_dev + my_sequence

    scaled_con, d_scale, d_pooled = contrast(pooled, vectors[tail_at + 3 * D + 1], pair_index)
    d_logit = counted * (jax.nn.sigmoid(logits_tok) - my_labels)
    if seqs == 1:
        d_rows = lax.dynamic_slice_in_dim(d_pooled, owner_rank * seq_dev + rank, 1, axis=0)
    else:
        d_rows = jnp.take(d_pooled, global_sequence, axis=0)
    upstream = d_logit[:, None] * head_weight[None, :] + token_weight[:, None] * d_rows
    d_head_weight = jnp.dot(d_logit, residual, precision=PRECISE)
    d_head_bias = jnp.sum(d_logit)
    leader = (device == 0).astype(F32)

    counts = {
        "in": row_blocks * 3,
        "out": row_blocks,
        "up": row_blocks * feed_blocks,
        "down": feed_blocks * row_blocks,
    }
    starts = {}
    begin_at = 0
    for name in ("in", "out", "up", "down"):
        starts[name] = begin_at
        begin_at = begin_at + layers * counts[name]
    block_count = begin_at
    dealt = {
        name: owners if counts[name] % owners == 0 and starts[name] % owners == 0 else None
        for name in counts
    }
    ready = {}
    ready_slots = {}
    summed = {}
    sends = []

    def slot_parts(slot):
        if slot in ready_slots:
            array, at = ready_slots[slot]
            return array[:, :, at]
        numbers = range(slot * owners, (slot + 1) * owners)
        members = []
        at = 0
        while at < owners:
            number = numbers[at]
            if number >= block_count:
                members.append(jnp.zeros((owners - at, 1, block_size, block_size), BF))
                break
            array, offset = ready[number]
            span = 1
            while at + span < owners and ready.get(number + span, (None, 0))[0] is array:
                span = span + 1
            members.append(array[offset : offset + span])
            at = at + span
        return jnp.concatenate(members, axis=0)

    def once_there(slots, values):
        sums = jnp.stack([summed[slot] for slot in slots])
        values, sums = lax.optimization_barrier((values, sums))
        for at, slot in enumerate(slots):
            summed[slot] = sums[at]
        return values

    def sum_ready(next_in):
        taken = []
        for slot in range(slot_count):
            numbers = range(slot * owners, min((slot + 1) * owners, block_count))
            if slot not in summed and (
                slot in ready_slots or all(number in ready for number in numbers)
            ):
                taken.append(slot)
        if not taken:
            return next_in
        outgoing = jnp.concatenate([slot_parts(slot) for slot in taken], axis=1)
        next_in, outgoing = lax.optimization_barrier((next_in, outgoing))
        if len(sends) < 2:
            arrived = lax.psum_scatter(
                outgoing.reshape((-1,) + outgoing.shape[2:]), "dp", scatter_dimension=0, tiled=True
            )
        else:
            before = sends[-1]
            arrived = scatter_sum(
                outgoing, lambda slots: send_back(before, once_there(before, slots), False)
            )
            back = returned[before[0]][0]
            arrived, back = lax.optimization_barrier((arrived, back))
            for at, slot in enumerate(before):
                returned[slot] = (back, at)
        for at, slot in enumerate(taken):
            summed[slot] = arrived[at]
        sends.append(taken)
        return next_in

    flat_stats = (slot_count, block_size, block_size)
    left_root = root_left.reshape(flat_stats)
    right_root = root_right.reshape(flat_stats)
    returned = [None] * slot_count

    def send_back(taken, next_in=None, wait=True):
        some = jnp.stack([summed[slot] for slot in taken])
        if rows_per % 16 == 0:
            outgoing = precondition(some, left_root, right_root, taken, owners)
        else:

            def roots(array):
                return jnp.stack([array[slot] for slot in taken])

            direction = jnp.einsum(
                "sij,sjk->sik",
                jnp.einsum(
                    "sij,sjk->sik", roots(left_root), some.astype(F32), precision=lax.Precision.HIGH
                ),
                roots(right_root),
                precision=lax.Precision.HIGH,
            )
            both = jnp.stack([some, direction.astype(BF)])
            outgoing = both.reshape(2, len(taken), owners, rows_per, block_size).transpose(
                2, 0, 1, 3, 4
            )
        if not wait:
            next_in, outgoing = lax.optimization_barrier((next_in, outgoing))
        back = lax.all_to_all(outgoing, "dp", split_axis=0, concat_axis=0, tiled=True)
        if next_in is not None and wait:
            next_in, back = lax.optimization_barrier((next_in, back))
        for at, slot in enumerate(taken):
            returned[slot] = (back, at)
        return next_in

    def emit_of(layer_no):
        def emit(name, value, next_in):
            next_in, value = lax.optimization_barrier((next_in, value))
            first = starts[name] + layer_no * counts[name]
            if dealt[name]:
                for at in range(counts[name] // owners):
                    ready_slots[first // owners + at] = (value, at)
            else:
                for at in range(counts[name]):
                    ready[first + at] = (value, at)
            if name == "down" and layer_no == 0 and sends:
                next_in = once_there(sends[0], next_in)
            if name == "up" or (name == "in" and layer_no == 0):
                next_in = sum_ready(next_in)
            if name == "out" and layer_no == 0 and len(sends) > 1:
                next_in = send_back(sends[0], next_in, False)
            return next_in

        return emit

    def placed(piece, width):
        row = jnp.zeros((ranks * cores * width,), F32)
        return lax.dynamic_update_slice(row, piece, ((rank * cores + core) * width,))

    bias_parts = [None] * layers

    def vector_rows_of(layer_no):
        grad_items = bias_parts[layer_no]
        return [
            placed(grad_items[0], head_width),
            placed(grad_items[1], head_width),
            placed(grad_items[2], feed_width),
        ] + list(grad_items[3:])

    for layer_no in reversed(range(layers)):
        upstream, bias_parts[layer_no] = layer_backward(
            upstream,
            kept_all[layer_no],
            weights_all[layer_no],
            pieces_of(layer_no),
            keys_live,
            dealt,
            emit_of(layer_no),
        )

    d_embed, d_gain_embed, d_shift_embed = norm_back(embedded, gain_embed, shift_embed, upstream)
    d_embed = d_embed.astype(BF)
    if returned[sends[0][0]] is not None:
        d_embed, back = lax.optimization_barrier((d_embed, returned[sends[0][0]][0]))
        for at, slot in enumerate(sends[0]):
            returned[slot] = (back, at)
    if places_last:
        table_shard = lax.fori_loop(
            1, rounds, lambda at, total: total + return_rows(at, d_embed), return_rows(0, d_embed)
        )
        place_grads = to_last(d_embed)
        table_shard = table_shard.at[last_base : last_base + seq_slots].add(
            jnp.where(device == devices - 1, place_grads, 0.0)
        )
    else:
        d_rows = lax.all_gather(d_embed, EVERY, axis=0, tiled=True)
        held = device * shard_rows + jnp.arange(shard_rows)
        all_places = VOCAB + jnp.arange(all_ids.shape[0]) % seq_slots
        picker = (all_ids[None, :] == held[:, None]).astype(BF) + (
            all_places[None, :] == held[:, None]
        ).astype(BF)
        table_shard = product(picker, d_rows)

    blocks_low = jnp.stack([summed[slot] for slot in range(slot_count)])
    blocks = blocks_low.astype(F32)
    squares = jnp.sum(table_shard * table_shard) + jnp.sum(blocks * blocks)
    for taken in sends:
        if returned[taken[0]] is None:
            squares = send_back(taken, squares, False)
    vector_rows = []
    for layer_no in range(layers):
        vector_rows = vector_rows + vector_rows_of(layer_no)
    scalars = jnp.stack([d_head_bias, leader * d_scale, bce_part, count_part, squares])
    totals = sum_over_all(
        jnp.concatenate(vector_rows + [d_gain_embed, d_shift_embed, d_head_weight, scalars])
    )
    vector_total = totals[:-3]
    bce_total, count_total, square_total = totals[-3], totals[-2], totals[-1]
    grad_norm = jnp.sqrt(square_total + jnp.sum(vector_total * vector_total))
    factor = CLIP_NORM / jnp.maximum(grad_norm, CLIP_NORM)

    square_of = factor * factor * (1 - STAT_DECAY)
    new_left = STAT_DECAY * stats_left.reshape(blocks.shape) + square_of * jnp.einsum(
        "sij,skj->sik", blocks_low, blocks_low, preferred_element_type=F32
    )
    new_right = STAT_DECAY * stats_right.reshape(blocks.shape) + square_of * jnp.einsum(
        "sji,sjk->sik", blocks_low, blocks_low, preferred_element_type=F32
    )
    matrices = (in_proj, out_proj, up_proj, down_proj)
    new_weights = []
    clipped = []
    begin_at = 0
    rates = (RATE_MATRIX, RATE_OUT, RATE_MATRIX, RATE_MATRIX)
    for weight, rate in zip(matrices, rates):
        span_of = weight.size // (rows_per * block_size)
        numbers = range(begin_at, begin_at + span_of)
        both = []
        for kind in range(2):
            pieces = []
            for slot in range(numbers[0] // owners, numbers[-1] // owners + 1):
                back, at = returned[slot]
                low = max(numbers[0] - slot * owners, 0)
                high = min(numbers[-1] + 1 - slot * owners, owners)
                pieces.append(back[low:high, kind, at])
            both.append(jnp.concatenate(pieces, axis=0).reshape(weight.shape).astype(F32) * factor)
        clipped.append(both[0])
        new_weights.append(weight - rate * (both[1] + DECAY_MATRIX * weight))
        begin_at = begin_at + span_of
    clipped_vectors = vector_total * factor
    new_table, table_one, table_two = adamw(
        embed_table, table_first, table_second, table_shard * factor, RATE_TABLE, DECAY_TABLE
    )
    new_vectors, vector_one, vector_two = adamw(
        vectors, vector_first, vector_second, clipped_vectors, RATE_VECTOR, 0.0
    )
    loss = jnp.stack([bce_total, count_total, scaled_con])
    return (
        loss,
        grad_norm,
        new_weights[0],
        new_weights[1],
        new_weights[2],
        new_weights[3],
        clipped[0],
        clipped[1],
        clipped[2],
        clipped[3],
        new_left.reshape(stats_left.shape),
        new_right.reshape(stats_right.shape),
        new_table,
        table_one,
        table_two,
        new_vectors,
        vector_one,
        vector_two,
        clipped_vectors[:tail_at],
    )


def solution(mesh):
    owners, tensor_ranks = mesh.shape["dp"], mesh.shape["tensor"]
    split = Mesh(mesh.devices.reshape(owners, tensor_ranks // 2, 2), EVERY)
    both = ("x", "core")
    placed = (
        P("dp", None),
        P("dp", None),
        P("dp"),
        P(),
        P(EVERY, None),
        P(EVERY, None),
        P(EVERY, None),
        P(),
        P(),
        P(),
        P(None, None, None, both, "dp", None),
        P(None, both, None, "dp", None),
        P(None, None, both, "dp", None),
        P(None, both, None, "dp", None),
        P(both, "dp", None, None, None),
        P(both, "dp", None, None, None),
        P(both, "dp", None, None, None),
        P(both, "dp", None, None, None),
    )
    matrices = placed[10:14]
    return jax.shard_map(
        shards,
        mesh=split,
        in_specs=placed,
        out_specs=(P(), P())
        + matrices
        + matrices
        + placed[14:16]
        + placed[4:7]
        + (P(), P(), P(), P()),
        check_vma=False,
    )
```

```python
import math

import jax
import jax.numpy as jnp
from jax import lax
from jax.experimental import pallas as pl
from jax.experimental.pallas import tpu as pltpu
from jax.sharding import Mesh
from jax.sharding import PartitionSpec as P

D = 1024
HD = 64
FF = 4096
VOCAB = 30720
STEP = 10


PRECISE = lax.Precision.HIGHEST
EPS_NORM = 1e-05
EPS_UNIT = 1e-06
CLIP_NORM = 1.0
BETA_ONE = 0.9
BETA_TWO = 0.999
ADAM_EPS = 1e-08
STAT_DECAY = 0.95
RATE_TABLE = 0.06
RATE_VECTOR = 0.5
RATE_MATRIX = 0.5
RATE_OUT = 4.0
DECAY_TABLE = 0.01
DECAY_MATRIX = 0.01
CON_WEIGHT = 16.0
MASK_FILL = -1000000000.0

BF = jnp.bfloat16
F32 = jnp.float32
GROUP = ("dp", "x")
EVERY = ("dp", "x", "core")
ROW_SLOTS = 24


def layer_norm(values, gain, shift):
    centre = values - jnp.mean(values, axis=-1, keepdims=True)
    spread_sq = jnp.mean(centre * centre, axis=-1, keepdims=True)
    return centre * lax.rsqrt(spread_sq + EPS_NORM) * gain + shift


def norm_back(values, gain, shift, upstream):
    ignored, pull = jax.vjp(layer_norm, values, gain, shift)
    return pull(upstream)


def adamw(weight, first, second, grad, rate, decay):
    first = BETA_ONE * first + (1 - BETA_ONE) * grad
    second = BETA_TWO * second + (1 - BETA_TWO) * grad * grad
    fixed_first = first / (1 - BETA_ONE**STEP)
    fixed_second = second / (1 - BETA_TWO**STEP)
    return (
        weight - rate * (fixed_first / (jnp.sqrt(fixed_second) + ADAM_EPS) + decay * weight),
        first,
        second,
    )


def from_peer(values, axis, mask=1):
    size = lax.axis_size(axis)
    return lax.ppermute(values, axis, [(at, at ^ mask) for at in range(size)])


def peers():
    found = []
    for axis in ("core", "x", "dp"):
        mask = 1
        while mask < lax.axis_size(axis):
            found.append((axis, mask))
            mask = mask * 2
    return found


def halving_steps():
    masks = [1]
    while masks[-1] * 2 < lax.axis_size("dp"):
        masks.append(masks[-1] * 2)
    return masks


def halve(slots, step):
    mask = halving_steps()[step]
    dim = len(halving_steps()) - 1 - step
    bit = lax.axis_index("dp") // mask % 2
    away = lax.dynamic_index_in_dim(slots, 1 - bit, dim, keepdims=False)
    keep = lax.dynamic_index_in_dim(slots, bit, dim, keepdims=False)
    return keep + from_peer(away, "dp", mask)


def sum_over_all(values):
    for axis, mask in peers():
        values = values + from_peer(values, axis, mask)
    return values


def gather_small(values, steps=()):
    mask = 1
    while mask < lax.axis_size("dp"):
        steps = steps + (("dp", mask),)
        mask = mask * 2
    for axis, mask in steps:
        other = from_peer(values, axis, mask)
        first = lax.axis_index(axis) // mask % 2 == 0
        values = jnp.where(
            first,
            jnp.concatenate([values, other], axis=0),
            jnp.concatenate([other, values], axis=0),
        )
    return values


def tree():
    count = lax.axis_size("dp")
    holders = [count - 1]
    steps = []
    mask = count // 2
    while mask > 0:
        steps.append([(at, at ^ mask) for at in holders])
        holders = holders + [at ^ mask for at in holders]
        mask = mask // 2
    return steps


def last_to_near():
    count = lax.axis_size("dp") * lax.axis_size("x")
    return [(count - 1, count - 2)]


def from_last(parts):
    last = lax.axis_size("core") - 1
    value = jnp.where(lax.axis_index("core") == last, parts[last], from_peer(parts[0], "core"))
    half = value.shape[0] // 2
    near = lax.ppermute(value[:half], GROUP, last_to_near())
    return jnp.where(lax.axis_index("x") == 0, near, value[half:])


def spread_from(value, step):
    found = lax.ppermute(value, "dp", step)
    reached = jnp.any(lax.axis_index("dp") == jnp.array([there for here, there in step]))
    return jnp.where(reached, found, value)


def both_halves(value):
    other = from_peer(value, "x")
    first = lax.axis_index("x") == 0
    return jnp.where(
        first,
        jnp.concatenate([value, other], axis=0),
        jnp.concatenate([other, value], axis=0),
    )


def to_last(value):
    half = value.shape[0] // 2
    first = lax.axis_index("x") == 0
    away = jnp.where(first, value[half:], value[:half])
    total = jnp.where(first, value[:half], value[half:]).astype(F32)
    total = total + from_peer(away, "x").astype(F32)
    for step in reversed(tree()):
        back = [(there, here) for here, there in step]
        total = total + lax.ppermute(total.astype(BF), "dp", back).astype(F32)
    back = [(there, here) for here, there in last_to_near()]
    near = lax.ppermute(total.astype(BF), GROUP, back).astype(F32)
    total = jnp.concatenate([near, total], axis=0)
    return jnp.concatenate([from_peer(total.astype(BF), "core").astype(F32), total], axis=0)


def after(values, *first):
    return lax.optimization_barrier((values,) + first)[0]


def collect(values):
    across = from_peer(values, "x")
    return jnp.concatenate([values, from_peer(values, "core")], axis=0), across


def complete(across):
    return jnp.concatenate([across, from_peer(across, "core")], axis=0)


def spread_first(other):
    rows = other.shape[0] // 2
    away = other[:rows] + from_peer(other[rows:].astype(BF), "core").astype(F32)
    return away.astype(BF)


def spread_last(own, away):
    rows = own.shape[0] // 2
    near = own[:rows] + from_peer(own[rows:].astype(BF), "core").astype(F32)
    return near + from_peer(away, "x").astype(F32)


def column_sum(*members):
    return sum(jnp.sum(values.astype(F32), axis=0) for values in members)


def fetch(pieces):
    return lax.all_gather(pieces, "dp", axis=0, tiled=False)[:, None]


def layer_rows(in_proj, out_proj, up_proj, down_proj, layer_no):
    rows, width = in_proj.shape[-2:]
    row_blocks = in_proj.shape[1]
    feed = up_proj.shape[2]
    attend_rows = [
        in_proj[layer_no].reshape(row_blocks, 3, rows, width).transpose(1, 0, 2, 3),
        out_proj[layer_no].reshape(1, row_blocks, rows, width),
    ]
    feed_rows = [
        up_proj[layer_no].reshape(row_blocks, feed, rows, width),
        down_proj[layer_no].reshape(feed, row_blocks, rows, width),
    ]
    return [jnp.concatenate(rows, axis=0).astype(BF) for rows in (attend_rows, feed_rows)]


def named_layer(attend_all, feed_all, row_blocks, feed):
    of_x = (1, attend_all.shape[1], 0)
    second = (3, row_blocks, 0)
    return (
        (attend_all, {"x": of_x, "low": (2, 3, 0), "high": second}),
        (attend_all, {"x": of_x, "low": second, "high": (2, 1, 3)}),
        (feed_all, {"x": of_x, "low": second, "high": (2, row_blocks, 0)}),
        (feed_all, {"x": of_x, "low": second, "high": (2, feed, row_blocks)}),
    )


def wide():
    return pltpu.CompilerParams(vmem_limit_bytes=48 * 1024 * 1024)


def whole(shape):
    return pl.BlockSpec(shape, lambda step: (0,) * len(shape))


def columns_of(ref, at, width):
    if len(ref.shape) == 2:
        return ref[:, at * width : (at + 1) * width]
    per = ref.shape[2] // width
    return ref[at // per, :, at % per * width : (at % per + 1) * width]


def joined_rows(weights):
    if weights.shape[-2] % 16 == 0:
        return weights
    owners, ranks, first, second, rows, width = weights.shape
    moved = weights.transpose(1, 2, 3, 0, 4, 5)
    return moved.reshape(1, ranks, first, second, owners * rows, width)


def rows_product(left, weights, dims, over, across, outs, finish, by_column=()):
    weights = joined_rows(weights)
    owners, rows, width = weights.shape[0], weights.shape[4], weights.shape[5]
    side = owners * rows
    turned = "low" in over
    steps = 1
    for name in across:
        steps = steps * dims[name][1]
    tokens = left.shape[-2]
    block_sizes = [1] * 6
    block_sizes[0], block_sizes[4], block_sizes[5] = owners, rows, width
    for name in over:
        block_sizes[dims[name][0]] = dims[name][1]
    terms = [()]
    for name in over:
        terms = [term + (at,) for term in terms for at in range(dims[name][1])]

    def kernel(*refs):
        left_ref, weights_ref = refs[:2]
        total = None
        for number, term in enumerate(terms):
            at = [0] * 3
            for name, place in zip(over, term):
                at[dims[name][0] - 1] = place
            block = weights_ref[(slice(None),) + tuple(at)].reshape(side, width)
            part = columns_of(left_ref, number, side)
            contract = (((1,), (1 if turned else 0,)), ((), ()))
            term_out = lax.dot_general(part, block, contract, preferred_element_type=F32)
            total = term_out if total is None else total + term_out
        last_in = 2 + len(by_column)
        results = finish(total, *[ref[...] for ref in refs[2:last_in]])
        for ref, result in zip(refs[last_in:], results):
            ref[...] = result.astype(ref.dtype).reshape(ref.shape)

    def weights_at(step):
        place = [0] * 6
        for name in reversed(across):
            place[dims[name][0]] = dims[name][2] + lax.rem(step, dims[name][1])
            step = lax.div(step, dims[name][1])
        for name in over:
            place[dims[name][0]] = dims[name][2] // dims[name][1]
        return tuple(place)

    out_shapes = []
    out_specs = []
    for apart, dtype in outs:
        if apart == 1:
            out_shapes.append(jax.ShapeDtypeStruct((tokens, steps * side), dtype))
            out_specs.append(pl.BlockSpec((tokens, side), lambda step: (0, step)))
        else:
            per = steps // apart
            out_shapes.append(jax.ShapeDtypeStruct((apart, tokens, per * side), dtype))
            out_specs.append(
                pl.BlockSpec(
                    (1, tokens, side),
                    lambda step, per=per: (lax.div(step, per), 0, lax.rem(step, per)),
                )
            )
    work = steps * len(terms) * side * width
    return pl.pallas_call(
        kernel,
        grid=(steps,),
        in_specs=[whole(left.shape), pl.BlockSpec(tuple(block_sizes), weights_at)]
        + [
            pl.BlockSpec((member.shape[0], side), lambda step: (0, step)) for member in by_column
        ],
        out_specs=out_specs,
        out_shape=out_shapes,
        compiler_params=wide(),
        cost_estimate=pl.CostEstimate(
            flops=2 * tokens * work, bytes_accessed=2 * work + 2 * left.size, transcendentals=0
        ),
    )(left, weights, *by_column)


def block_grads(lefts, rights, ranks, high, low, side, x_on_left, owners=None):
    count = len(lefts)

    def kernel(*refs):
        step = pl.program_id(0)
        out_ref = refs[2 * count]
        for at in range(ranks if x_on_left else 1):
            begin = pl.multiple_of((at * high + step) * side, side)
            parts = [ref[:, pl.ds(begin, side)] for ref in refs[:count]]
            for low_at in range(low):
                for rank in range(1 if x_on_left else ranks):
                    if x_on_left:
                        number, target = low_at, at
                    elif len(refs[count].shape) == 3:
                        number, target = low_at * ranks + rank, rank
                    else:
                        number, target = rank * low + low_at, rank
                    total = None
                    for part, right_ref in zip(parts, refs[count : 2 * count]):
                        block = columns_of(right_ref, number, side)
                        term = lax.dot_general(
                            part, block, (((0,), (0,)), ((), ())), preferred_element_type=F32
                        )
                        total = term if total is None else total + term
                    if owners is None:
                        out_ref[low_at, target] = total.astype(BF)
                    else:
                        out_ref[low_at, target, 0] = total.astype(BF)

    if owners is None:
        out_spec = pl.BlockSpec((low, ranks, side, side), lambda step: (step, 0, 0, 0))
        out_shape = (high * low, ranks, side, side)
    else:
        per = owners // low
        out_spec = pl.BlockSpec(
            (low, ranks, 1, side, side),
            lambda step: (lax.rem(step, per), 0, lax.div(step, per), 0, 0),
        )
        out_shape = (owners, ranks, high * low // owners, side, side)
    return pl.pallas_call(
        kernel,
        grid=(high,),
        in_specs=[whole(member.shape) for member in tuple(lefts) + tuple(rights)],
        out_specs=out_spec,
        out_shape=jax.ShapeDtypeStruct(out_shape, BF),
        compiler_params=wide(),
        cost_estimate=pl.CostEstimate(
            flops=2 * count * lefts[0].shape[-2] * high * low * ranks * side * side,
            bytes_accessed=2 * high * low * ranks * side * side,
            transcendentals=0,
        ),
    )(*lefts, *rights)


PAIR = 2 * HD


def halves(values):
    lane = lax.broadcasted_iota(jnp.int32, values.shape, 1)
    nothing = jnp.zeros_like(values)
    return jnp.where(lane < HD, values, nothing), jnp.where(lane < HD, nothing, values)


def dot_nt(left, right):
    return lax.dot_general(left, right, (((1,), (1,)), ((), ())), preferred_element_type=F32)


def dot_nn(left, right):
    return lax.dot_general(left, right, (((1,), (0,)), ((), ())), preferred_element_type=F32)


def dot_tn(left, right):
    return lax.dot_general(left, right, (((0,), (0,)), ((), ())), preferred_element_type=F32)


def softmax_of(queries, keys_in, live):
    scores = dot_nt(queries, keys_in) * HD ** (-0.5)
    scores = jnp.where(live > 0, scores, MASK_FILL)
    grown = jnp.exp(scores - jnp.max(scores, axis=-1, keepdims=True))
    return grown / jnp.sum(grown, axis=-1, keepdims=True)


def attend_kernel(live_ref, qkv_ref, mixed_ref):
    live = live_ref[0]
    query_heads = halves(qkv_ref[0])
    value_heads = halves(qkv_ref[2])
    total = None
    for query, value in zip(query_heads, value_heads):
        weights = softmax_of(query, qkv_ref[1], live).astype(BF)
        part = dot_nn(weights, value)
        total = part if total is None else total + part
    mixed_ref[...] = total.astype(BF)


def attend_back_kernel(live_ref, qkv_ref, d_mixed_ref, d_qkv_ref):
    live = live_ref[0]
    query_heads = halves(qkv_ref[0])
    key_heads = halves(qkv_ref[1])
    d_heads = halves(d_mixed_ref[...])
    d_query = d_key = d_value = 0.0
    for query, key, d_out in zip(query_heads, key_heads, d_heads):
        weights = softmax_of(query, qkv_ref[1], live)
        d_value = d_value + dot_tn(weights.astype(BF), d_out)
        d_weights = dot_nt(d_out, qkv_ref[2])
        d_scores = weights * (
            d_weights - jnp.sum(weights * d_weights, axis=-1, keepdims=True)
        )
        d_scores = d_scores.astype(BF)
        d_query = d_query + dot_nn(d_scores, key)
        d_key = d_key + dot_tn(d_scores, query)
    scale_by = HD ** (-0.5)
    d_qkv_ref[0] = (d_query * scale_by).astype(BF)
    d_qkv_ref[1] = (d_key * scale_by).astype(BF)
    d_qkv_ref[2] = d_value.astype(BF)


def attend(qkv, live, d_mixed=None):
    seqs, slots = live.shape
    width = qkv.shape[2]
    pairs = width // PAIR
    mixed_spec = pl.BlockSpec((slots, PAIR), lambda seq, pair: (seq, pair))
    qkv_spec = pl.BlockSpec((3, slots, PAIR), lambda seq, pair: (0, seq, pair))
    specs = [pl.BlockSpec((1, 1, slots), lambda seq, pair: (seq, 0, 0)), qkv_spec]
    operands = [live.astype(F32).reshape(seqs, 1, slots), qkv]
    if d_mixed is None:
        out_spec, out_shape = mixed_spec, jax.ShapeDtypeStruct(qkv.shape[1:], BF)
        body, products = attend_kernel, 2
    else:
        specs.append(mixed_spec)
        operands.append(d_mixed)
        out_spec, out_shape = qkv_spec, jax.ShapeDtypeStruct(qkv.shape, BF)
        body, products = attend_back_kernel, 5
    return pl.pallas_call(
        body,
        grid=(seqs, pairs),
        in_specs=specs,
        out_specs=out_spec,
        out_shape=out_shape,
        compiler_params=wide(),
        cost_estimate=pl.CostEstimate(
            flops=2 * products * seqs * slots * slots * width * 2,
            bytes_accessed=2 * qkv.size * 2,
            transcendentals=seqs * slots * slots * width // HD,
        ),
    )(*operands)


def product(left, right):
    return jnp.dot(left, right, preferred_element_type=F32)


def product_tn(left, right):
    return lax.dot_general(left, right, (((0,), (0,)), ((), ())), preferred_element_type=F32)


def same(total):
    return (total,)


def plus(total, bias):
    return (total + bias,)


ROOT_HALF = 0.5**0.5
DENSITY = (2 * math.pi) ** (-0.5)


def plus_gelu(total, bias):
    total = total + bias
    return (total, total * (1.0 + lax.erf(total * ROOT_HALF)) * 0.5)


def times_gelu_slope(total, before):
    slope = 0.5 * (1.0 + lax.erf(before * ROOT_HALF)) + before * (
        DENSITY * jnp.exp(-0.5 * before * before)
    )
    return (total * slope,)


def layer_forward(residual, weights, pieces, keys_live):
    w_in, w_out, w_up, w_down = weights
    bias_q, bias_v, bias_up, bias_out, bias_down, gain_one, shift_one, gain_two, shift_two = pieces
    bias_in = jnp.concatenate([bias_q, jnp.zeros_like(bias_q), bias_v]).reshape(1, -1)

    def mix(rows, live):
        (projected,) = rows_product(
            rows, *w_in, ("high",), ("low", "x"), [(3, BF)], plus, [bias_in]
        )
        return projected, attend(projected, live)

    def mix_out(mixed):
        return rows_product(mixed, *w_out, ("x", "high"), ("low",), [(1, F32)], same)[0]

    def feed(rows):
        return rows_product(
            rows,
            *w_up,
            ("high",),
            ("x", "low"),
            [(1, F32), (1, BF)],
            plus_gelu,
            [bias_up.reshape(1, -1)],
        )

    def feed_out(active):
        return rows_product(active, *w_down, ("x", "high"), ("low",), [(1, F32)], same)[0]

    own, across = collect(residual.astype(BF))
    own_qkv, own_mixed = mix(own, keys_live[0])
    other = complete(after(across, own_mixed))
    other_qkv, other_mixed = mix(other, keys_live[1])
    away = spread_first(mix_out(other_mixed))
    own_out = mix_out(after(own_mixed, away))
    first_in = residual + (spread_last(own_out, away) + bias_out)
    middle = layer_norm(first_in, gain_one, shift_one)
    own_mid, across = collect(middle.astype(BF))
    own_pre, own_act = feed(own_mid)
    other_mid = complete(after(across, own_act))
    other_pre, other_act = feed(other_mid)
    away = spread_first(feed_out(other_act))
    own_out = feed_out(after(own_act, away))
    second_in = middle + (spread_last(own_out, away) + bias_down)
    kept_values = (
        first_in,
        second_in,
        (own, other),
        (own_qkv, other_qkv),
        (own_mixed, other_mixed),
        (own_mid, other_mid),
        (own_pre, other_pre),
        (own_act, other_act),
    )
    return (layer_norm(second_in, gain_two, shift_two), kept_values)


def layer_backward(upstream, kept_values, weights, pieces, keys_live, dealt, emit):
    (
        first_in,
        second_in,
        gathered,
        qkv,
        mixed,
        spread_mid,
        hidden_pre,
        hidden_act,
    ) = kept_values
    w_in, w_out, w_up, w_down = weights
    gain_one, shift_one, gain_two, shift_two = pieces[5:]
    ranks, side = w_in[1]["x"][1], w_in[0].shape[-1]
    row_blocks, feed = w_in[1]["high"][1], w_up[1]["low"][1]
    d_second, d_gain_two, d_shift_two = norm_back(second_in, gain_two, shift_two, upstream)
    d_fed = d_second.astype(BF)

    def feed_back(rows, before):
        return rows_product(
            rows, *w_down, ("low",), ("x", "high"), [(1, BF)], times_gelu_slope, [before]
        )[0]

    def up_back(rows):
        return rows_product(rows, *w_up, ("x", "low"), ("high",), [(1, F32)], same)[0]

    own, across = collect(d_fed)
    own_pre = feed_back(own, hidden_pre[0])
    other = complete(after(across, own_pre))
    other_pre = feed_back(other, hidden_pre[1])
    away = spread_first(up_back(other_pre))
    own = after(own, away)
    parts = block_grads(hidden_act, (own, other), ranks, feed, row_blocks, side, True, dealt["down"])
    own_pre = emit("down", parts, own_pre)
    d_pre = (own_pre, other_pre)
    parts = block_grads(spread_mid, d_pre, ranks, row_blocks, feed, side, False, dealt["up"])
    own_pre = emit("up", parts, own_pre)
    d_middle = d_second + spread_last(up_back(own_pre), away)
    d_first, d_gain_one, d_shift_one = norm_back(first_in, gain_one, shift_one, d_middle)
    d_branch = d_first.astype(BF)

    def mix_back(rows, projected, live):
        (d_mixed,) = rows_product(rows, *w_out, ("low",), ("x", "high"), [(1, BF)], same)
        return attend(projected, live, d_mixed)

    def in_back(rows):
        return rows_product(rows, *w_in, ("low", "x"), ("high",), [(1, F32)], same)[0]

    own, across = collect(d_branch)
    own_qkv = mix_back(own, qkv[0], keys_live[0])
    other = complete(after(across, own_qkv))
    other_qkv = mix_back(other, qkv[1], keys_live[1])
    away = spread_first(in_back(other_qkv))
    own = after(own, away)
    parts = block_grads(mixed, (own, other), ranks, 1, row_blocks, side, True)
    own_qkv = emit("out", parts, own_qkv)
    d_qkv = (own_qkv, other_qkv)
    parts = block_grads(gathered, d_qkv, ranks, row_blocks, 3, side, False)
    own_qkv = emit("in", parts, own_qkv)
    d_residual = d_first + spread_last(in_back(own_qkv), away)
    bias_grads = (
        column_sum(*[member[0] for member in d_qkv]),
        column_sum(*[member[2] for member in d_qkv]),
        column_sum(*d_pre),
        column_sum(d_branch),
        column_sum(d_fed),
        d_gain_one,
        d_shift_one,
        d_gain_two,
        d_shift_two,
    )
    return d_residual, bias_grads


def precise(left, right, dims):
    return lax.dot_general(
        left, right, (dims, ((), ())), precision=PRECISE, preferred_element_type=F32
    )


def contrast_kernel(scale_ref, pairs_ref, pooled_ref, loss_ref, d_scale_ref, d_pooled_ref):
    pooled = pooled_ref[...]
    count = pooled.shape[0]
    norm = lax.rsqrt(jnp.sum(pooled * pooled, axis=-1, keepdims=True) + EPS_UNIT)
    unit = pooled * norm
    row_at = lax.broadcasted_iota(jnp.int32, (count, count), 0)
    column_at = lax.broadcasted_iota(jnp.int32, (count, count), 1)
    picks = (pairs_ref[...] == column_at).astype(F32)
    same_at = (row_at == column_at).astype(F32)
    scale = jnp.exp(scale_ref[...])
    partner = precise(picks, unit, ((1,), (0,)))
    logits = scale * precise(unit, partner, ((1,), (1,)))
    total = 0.0
    slope = -2.0 * same_at
    for axis in (1, 0):
        highest = jnp.max(logits, axis=axis, keepdims=True)
        grown = jnp.exp(logits - highest)
        each = jnp.sum(grown, axis=axis, keepdims=True)
        total = total + jnp.sum(highest + jnp.log(each), keepdims=True)
        slope = slope + grown / each
    total = total - 2.0 * jnp.sum(logits * same_at, keepdims=True)
    weight = 0.5 * CON_WEIGHT
    loss_ref[...] = weight * total
    slope = weight * slope
    d_scale_ref[...] = jnp.sum(slope * logits, keepdims=True)
    slope = slope * scale
    d_partner = precise(slope, unit, ((0,), (0,)))
    d_unit = precise(slope, partner, ((1,), (0,))) + precise(picks, d_partner, ((0,), (0,)))
    along = jnp.sum(d_unit * pooled, axis=-1, keepdims=True)
    d_pooled_ref[...] = norm * d_unit - pooled * (norm * norm * norm * along)


def contrast(pooled, log_scale, pair_index):
    loss, d_scale, d_pooled = pl.pallas_call(
        contrast_kernel,
        out_shape=[
            jax.ShapeDtypeStruct((1, 1), F32),
            jax.ShapeDtypeStruct((1, 1), F32),
            jax.ShapeDtypeStruct(pooled.shape, F32),
        ],
        compiler_params=wide(),
    )(log_scale.reshape(1, 1), pair_index.reshape(-1, 1), pooled)
    return loss[0, 0], d_scale[0, 0], d_pooled


def split_dot(left, right):
    total = None
    parts = []
    for operand in (left, right):
        if operand.dtype == BF:
            parts.append((operand,))
        else:
            high = operand.astype(BF)
            parts.append((high, (operand - high.astype(F32)).astype(BF)))
    for at, first in enumerate(parts[0]):
        for second in parts[1][: 2 - at]:
            term = dot_nn(first, second)
            total = term if total is None else total + term
    return total


def precondition(blocks, left_roots, right_roots, taken, owners):
    count, side = blocks.shape[0], blocks.shape[-1]
    rows = side // owners

    def kernel(slots_ref, block_ref, left_ref, right_ref, out_ref):
        block = block_ref[0]
        result = split_dot(split_dot(left_ref[0], block), right_ref[0])
        out_ref[:, 0, 0] = block.reshape(owners, rows, side)
        out_ref[:, 1, 0] = result.astype(BF).reshape(owners, rows, side)

    root_spec = pl.BlockSpec((1, side, side), lambda step, slots_ref: (slots_ref[step], 0, 0))
    return pl.pallas_call(
        kernel,
        grid_spec=pltpu.PrefetchScalarGridSpec(
            num_scalar_prefetch=1,
            grid=(count,),
            in_specs=[
                pl.BlockSpec((1, side, side), lambda step, slots_ref: (step, 0, 0)),
                root_spec,
                root_spec,
            ],
            out_specs=pl.BlockSpec(
                (owners, 2, 1, rows, side), lambda step, slots_ref: (0, 0, step, 0, 0)
            ),
        ),
        out_shape=jax.ShapeDtypeStruct((owners, 2, count, rows, side), BF),
        compiler_params=wide(),
        cost_estimate=pl.CostEstimate(
            flops=10 * count * side**3, bytes_accessed=14 * blocks.size, transcendentals=0
        ),
    )(jnp.array(taken, jnp.int32), blocks, left_roots, right_roots)


def shards(
    token_ids,
    labels,
    lengths,
    pair_index,
    embed_table,
    table_first,
    table_second,
    vectors,
    vector_first,
    vector_second,
    in_proj,
    out_proj,
    up_proj,
    down_proj,
    stats_left,
    stats_right,
    root_left,
    root_right,
):
    seq_dev, seq_slots = token_ids.shape
    layers = in_proj.shape[0]
    owners = lax.axis_size("dp")
    ranks = lax.axis_size("x")
    cores = lax.axis_size("core")
    devices = owners * ranks * cores
    owner_rank = lax.axis_index("dp")
    rank = lax.axis_index("x")
    core = lax.axis_index("core")
    device = (owner_rank * ranks + rank) * cores + core
    per_layer = 8 * D + FF
    tail_at = layers * per_layer
    block_size = in_proj.shape[-1]
    rows_per = in_proj.shape[-2]
    row_blocks = in_proj.shape[1]
    feed_blocks = up_proj.shape[2]
    slot_count = stats_left.shape[2]
    seqs = seq_dev // ranks
    group_rows = seqs * seq_slots
    local_rows = group_rows // cores

    def mine(values):
        return lax.dynamic_slice_in_dim(
            values.reshape(-1), rank * group_rows + core * local_rows, local_rows
        )

    my_rows = core * local_rows + jnp.arange(local_rows)
    my_sequence = rank * seqs + my_rows // seq_slots
    my_length = jnp.take(lengths, my_sequence)
    counted = (my_rows % seq_slots < my_length).astype(F32)
    my_labels = mine(labels).astype(F32)
    turned = (jnp.arange(seq_slots) + core * local_rows) % seq_slots
    keys_live = [
        (turned < lax.dynamic_index_in_dim(lengths, which, 0, keepdims=False))[None]
        for which in (rank, rank ^ 1)
    ]

    rows_here = [
        layer_rows(in_proj, out_proj, up_proj, down_proj, layer_no) for layer_no in range(layers)
    ]
    rows_here[0][0], token_ids = lax.optimization_barrier((rows_here[0][0], token_ids))

    shard_rows = embed_table.shape[0]
    last_base = VOCAB - (devices - 1) * shard_rows
    places_last = last_base >= 0 and local_rows * cores == seq_slots
    all_ids = gather_small(token_ids).reshape(-1)
    if places_last:
        place_rows = from_last(
            [
                embed_table[last_base + at * local_rows : last_base + (at + 1) * local_rows].astype(BF)
                for at in range(cores)
            ]
        )
        hops = tree()
        all_ids, place_rows = lax.optimization_barrier((all_ids, place_rows))
    by_device = all_ids.reshape(devices, local_rows)
    holder = by_device // shard_rows
    earlier = jnp.arange(local_rows)[None, :] < jnp.arange(local_rows)[:, None]
    turn = jnp.sum(
        ((holder[:, :, None] == holder[:, None, :]) & earlier[None]).astype(jnp.int32), axis=2
    )
    rounds = jnp.max(turn) // ROW_SLOTS + 1
    own_index = by_device - device * shard_rows
    my_holder = lax.dynamic_index_in_dim(holder, device, 0, keepdims=False)
    my_turn = lax.dynamic_index_in_dim(turn, device, 0, keepdims=False)

    def plan(round_no):
        first = round_no * ROW_SLOTS
        here = (holder == device)[:, None, :] & (
            turn[:, None, :] - first == jnp.arange(ROW_SLOTS)[None, :, None]
        )
        row_of_slot = jnp.sum(jnp.where(here, own_index[:, None, :] + 1, 0), axis=2).reshape(-1)
        inside = (my_turn >= first) & (my_turn < first + ROW_SLOTS)
        my_slot = jnp.where(inside, my_holder * ROW_SLOTS + my_turn - first, -1)
        slot_of_token = (jnp.arange(devices * ROW_SLOTS)[:, None] == my_slot[None, :]).astype(BF)
        return row_of_slot, slot_of_token

    def exchange(filled):
        return lax.all_to_all(filled, EVERY, split_axis=0, concat_axis=0, tiled=True)

    def rows_to_send(round_no):
        rows = jnp.maximum(plan(round_no)[0] - 1, 0)
        return jnp.take(embed_table, rows, axis=0).astype(BF)

    def rows_reached(round_no, reached):
        return product_tn(plan(round_no)[1], reached)

    def rows_to_return(round_no, grads):
        return product(plan(round_no)[1], grads).astype(BF)

    def rows_returned(round_no, reached):
        row_of_slot = plan(round_no)[0]
        picker = (row_of_slot[None, :] == 1 + jnp.arange(shard_rows)[:, None]).astype(BF)
        return product(picker, reached)

    def full_rows():
        table = lax.all_gather(embed_table.astype(BF), "dp", axis=0, tiled=True)
        tensor_ranks = ranks * cores

        def lookup(row_index):
            block_at = row_index // shard_rows
            inside = block_at % tensor_ranks == rank * cores + core
            at_row = block_at // tensor_ranks * shard_rows + row_index % shard_rows
            picked = jnp.take(table, jnp.where(inside, at_row, 0), axis=0)
            return jnp.where(inside[:, None], picked, jnp.zeros((), BF))

        rows = lookup(token_ids.reshape(-1))
        rows = rows + lookup(VOCAB + jnp.arange(rows.shape[0]) % seq_slots)
        return lax.psum_scatter(rows, ("x", "core"), scatter_dimension=0, tiled=True).astype(F32)

    fetched = [[fetch(rows) for rows in of_layer] for of_layer in rows_here]
    if places_last:
        place_rows = spread_from(place_rows, hops[0])
        filled, place_rows = lax.optimization_barrier((rows_to_send(0), place_rows))
        for step in hops[1:]:
            place_rows = spread_from(place_rows, step)
        reached, fetched[0][0] = lax.optimization_barrier((exchange(filled), fetched[0][0]))
        token_rows = lax.fori_loop(
            1,
            rounds,
            lambda at, rows: rows + rows_reached(at, exchange(rows_to_send(at))),
            rows_reached(0, reached),
        )
        embedded = token_rows + both_halves(place_rows).astype(F32)
    else:
        embedded = full_rows()

    def by_rank(base_at, width):
        return lax.dynamic_slice_in_dim(vectors, base_at + (rank * cores + core) * width, width)

    head_width = D // (ranks * cores)
    feed_width = FF // (ranks * cores)

    def pieces_of(layer_no):
        base_at = layer_no * per_layer
        others = vectors[base_at + 2 * D + FF : base_at + per_layer].reshape(6, D)
        return (
            by_rank(base_at, head_width),
            by_rank(base_at + D, head_width),
            by_rank(base_at + 2 * D, feed_width),
        ) + tuple(others)

    gain_embed = vectors[tail_at : tail_at + D]
    shift_embed = vectors[tail_at + D : tail_at + 2 * D]
    head_weight = vectors[tail_at + 2 * D : tail_at + 3 * D]
    residual = layer_norm(embedded, gain_embed, shift_embed)
    kept_all = []
    weights_all = []
    for layer_no in range(layers):
        weights = named_layer(*fetched[layer_no], row_blocks, feed_blocks)
        residual, kept_values = layer_forward(
            residual, weights, pieces_of(layer_no), keys_live
        )
        kept_all.append(kept_values)
        weights_all.append(weights)

    logits_tok = jnp.dot(residual, head_weight, precision=PRECISE) + vectors[tail_at + 3 * D]
    bce_part = jnp.sum(counted * (jax.nn.softplus(logits_tok) - my_labels * logits_tok))
    count_part = jnp.sum(counted)
    token_weight = counted / my_length.astype(F32)
    here_sequence = my_rows // seq_slots
    chooser = (here_sequence[None, :] == jnp.arange(seqs)[:, None]).astype(F32) * token_weight[None, :]
    pooled_here = jnp.dot(chooser, residual, precision=PRECISE)
    pooled = gather_small(pooled_here + from_peer(pooled_here, "core"), (("x", 1),))
    global_sequence = owner_rank * seq_dev + my_sequence

    scaled_con, d_scale, d_pooled = contrast(pooled, vectors[tail_at + 3 * D + 1], pair_index)
    d_logit = counted * (jax.nn.sigmoid(logits_tok) - my_labels)
    if seqs == 1:
        d_rows = lax.dynamic_slice_in_dim(d_pooled, owner_rank * seq_dev + rank, 1, axis=0)
    else:
        d_rows = jnp.take(d_pooled, global_sequence, axis=0)
    upstream = d_logit[:, None] * head_weight[None, :] + token_weight[:, None] * d_rows
    d_head_weight = jnp.dot(d_logit, residual, precision=PRECISE)
    d_head_bias = jnp.sum(d_logit)
    leader = (device == 0).astype(F32)

    counts = {
        "in": row_blocks * 3,
        "out": row_blocks,
        "up": row_blocks * feed_blocks,
        "down": feed_blocks * row_blocks,
    }
    starts = {}
    begin_at = 0
    for name in ("in", "out", "up", "down"):
        starts[name] = begin_at
        begin_at = begin_at + layers * counts[name]
    block_count = begin_at
    dealt = {
        name: owners if counts[name] % owners == 0 and starts[name] % owners == 0 else None
        for name in counts
    }
    ready = {}
    ready_slots = {}
    summed = {}
    sends = []
    halved = []

    def slot_parts(slot):
        if slot in ready_slots:
            array, at = ready_slots[slot]
            return array[:, :, at]
        numbers = range(slot * owners, (slot + 1) * owners)
        members = []
        at = 0
        while at < owners:
            number = numbers[at]
            if number >= block_count:
                members.append(jnp.zeros((owners - at, 1, block_size, block_size), BF))
                break
            array, offset = ready[number]
            span = 1
            while at + span < owners and ready.get(number + span, (None, 0))[0] is array:
                span = span + 1
            members.append(array[offset : offset + span])
            at = at + span
        return jnp.concatenate(members, axis=0)

    def once_there(slots, values):
        sums = jnp.stack([summed[slot] for slot in slots])
        values, sums = lax.optimization_barrier((values, sums))
        for at, slot in enumerate(slots):
            summed[slot] = sums[at]
        return values

    def sum_ready(next_in):
        taken = []
        for slot in range(slot_count):
            numbers = range(slot * owners, min((slot + 1) * owners, block_count))
            if slot not in summed and (
                slot in ready_slots or all(number in ready for number in numbers)
            ):
                taken.append(slot)
        if not taken:
            return next_in
        outgoing = jnp.concatenate([slot_parts(slot) for slot in taken], axis=1)
        next_in, outgoing = lax.optimization_barrier((next_in, outgoing))
        if len(sends) < 2:
            arrived = lax.psum_scatter(
                outgoing.reshape((-1,) + outgoing.shape[2:]), "dp", scatter_dimension=0, tiled=True
            )
        else:
            bits = (2,) * len(halving_steps())
            halved.append(halve(outgoing.reshape(bits + outgoing.shape[1:]), 0))
            sends.append(taken)
            return next_in
        for at, slot in enumerate(taken):
            summed[slot] = arrived[at]
        sends.append(taken)
        return next_in

    flat_stats = (slot_count, block_size, block_size)
    left_root = root_left.reshape(flat_stats)
    right_root = root_right.reshape(flat_stats)
    returned = [None] * slot_count

    def send_back(taken, next_in=None, wait=True):
        some = jnp.stack([summed[slot] for slot in taken])
        if rows_per % 16 == 0:
            outgoing = precondition(some, left_root, right_root, taken, owners)
        else:

            def roots(array):
                return jnp.stack([array[slot] for slot in taken])

            direction = jnp.einsum(
                "sij,sjk->sik",
                jnp.einsum(
                    "sij,sjk->sik", roots(left_root), some.astype(F32), precision=lax.Precision.HIGH
                ),
                roots(right_root),
                precision=lax.Precision.HIGH,
            )
            both = jnp.stack([some, direction.astype(BF)])
            outgoing = both.reshape(2, len(taken), owners, rows_per, block_size).transpose(
                2, 0, 1, 3, 4
            )
        if not wait:
            next_in, outgoing = lax.optimization_barrier((next_in, outgoing))
        back = lax.all_to_all(outgoing, "dp", split_axis=0, concat_axis=0, tiled=True)
        if next_in is not None and wait:
            next_in, back = lax.optimization_barrier((next_in, back))
        for at, slot in enumerate(taken):
            returned[slot] = (back, at)
        return next_in

    def emit_of(layer_no):
        def emit(name, value, next_in):
            next_in, value = lax.optimization_barrier((next_in, value))
            first = starts[name] + layer_no * counts[name]
            if dealt[name]:
                for at in range(counts[name] // owners):
                    ready_slots[first // owners + at] = (value, at)
            else:
                for at in range(counts[name]):
                    ready[first + at] = (value, at)
            if name == "down" and layer_no == 0 and sends:
                next_in = once_there(sends[0], next_in)
            if name == "up" or (name == "in" and layer_no == 0):
                next_in = sum_ready(next_in)
            if name == "out" and layer_no == 0 and len(sends) > 1:
                next_in = send_back(sends[0], next_in, False)
            return next_in

        return emit

    def placed(piece, width):
        row = jnp.zeros((ranks * cores * width,), F32)
        return lax.dynamic_update_slice(row, piece, ((rank * cores + core) * width,))

    bias_parts = [None] * layers

    def vector_rows_of(layer_no):
        grad_items = bias_parts[layer_no]
        return [
            placed(grad_items[0], head_width),
            placed(grad_items[1], head_width),
            placed(grad_items[2], feed_width),
        ] + list(grad_items[3:])

    for layer_no in reversed(range(layers)):
        upstream, bias_parts[layer_no] = layer_backward(
            upstream,
            kept_all[layer_no],
            weights_all[layer_no],
            pieces_of(layer_no),
            keys_live,
            dealt,
            emit_of(layer_no),
        )

    d_embed, d_gain_embed, d_shift_embed = norm_back(embedded, gain_embed, shift_embed, upstream)
    d_embed = d_embed.astype(BF)
    if returned[sends[0][0]] is not None:
        d_embed, back, halved = lax.optimization_barrier(
            (d_embed, returned[sends[0][0]][0], halved)
        )
        for at, slot in enumerate(sends[0]):
            returned[slot] = (back, at)
    last_step = len(halving_steps()) - 1
    halved = [halve(slots, 1) for slots in halved]
    if places_last:
        reached = exchange(rows_to_return(0, d_embed))
        if halved:
            before = sends[-2]
            sums = jnp.stack([summed[slot] for slot in before])
            reached, halved, sums = lax.optimization_barrier((reached, halved, sums))
            for at, slot in enumerate(before):
                summed[slot] = sums[at]
        table_shard = lax.fori_loop(
            1,
            rounds,
            lambda at, total: total + rows_returned(at, exchange(rows_to_return(at, d_embed))),
            rows_returned(0, reached),
        )
        place_grads = to_last(d_embed)
        table_shard = table_shard.at[last_base : last_base + seq_slots].add(
            jnp.where(device == devices - 1, place_grads, 0.0)
        )
    else:
        d_rows = lax.all_gather(d_embed, EVERY, axis=0, tiled=True)
        held = device * shard_rows + jnp.arange(shard_rows)
        all_places = VOCAB + jnp.arange(all_ids.shape[0]) % seq_slots
        picker = (all_ids[None, :] == held[:, None]).astype(BF) + (
            all_places[None, :] == held[:, None]
        ).astype(BF)
        table_shard = product(picker, d_rows)

    for slots in halved:
        for step in range(2, last_step + 1):
            slots = halve(slots, step)
        slots = send_back(sends[-2], slots, False)
        for at, slot in enumerate(sends[-1]):
            summed[slot] = slots[at]

    blocks_low = jnp.stack([summed[slot] for slot in range(slot_count)])
    blocks = blocks_low.astype(F32)
    squares = jnp.sum(table_shard * table_shard) + jnp.sum(blocks * blocks)
    for taken in sends:
        if returned[taken[0]] is None:
            squares = send_back(taken, squares, False)
    vector_rows = []
    for layer_no in range(layers):
        vector_rows = vector_rows + vector_rows_of(layer_no)
    scalars = jnp.stack([d_head_bias, leader * d_scale, bce_part, count_part, squares])
    totals = jnp.concatenate(vector_rows + [d_gain_embed, d_shift_embed, d_head_weight, scalars])
    totals = sum_over_all(totals)
    vector_total = totals[:-3]
    bce_total, count_total, square_total = totals[-3], totals[-2], totals[-1]
    grad_norm = jnp.sqrt(square_total + jnp.sum(vector_total * vector_total))
    factor = CLIP_NORM / jnp.maximum(grad_norm, CLIP_NORM)

    square_of = factor * factor * (1 - STAT_DECAY)
    new_left = STAT_DECAY * stats_left.reshape(blocks.shape) + square_of * jnp.einsum(
        "sij,skj->sik", blocks_low, blocks_low, preferred_element_type=F32
    )
    new_right = STAT_DECAY * stats_right.reshape(blocks.shape) + square_of * jnp.einsum(
        "sji,sjk->sik", blocks_low, blocks_low, preferred_element_type=F32
    )
    matrices = (in_proj, out_proj, up_proj, down_proj)
    new_weights = []
    clipped = []
    begin_at = 0
    rates = (RATE_MATRIX, RATE_OUT, RATE_MATRIX, RATE_MATRIX)
    for weight, rate in zip(matrices, rates):
        span_of = weight.size // (rows_per * block_size)
        numbers = range(begin_at, begin_at + span_of)
        both = []
        for kind in range(2):
            pieces = []
            for slot in range(numbers[0] // owners, numbers[-1] // owners + 1):
                back, at = returned[slot]
                low = max(numbers[0] - slot * owners, 0)
                high = min(numbers[-1] + 1 - slot * owners, owners)
                pieces.append(back[low:high, kind, at])
            both.append(jnp.concatenate(pieces, axis=0).reshape(weight.shape).astype(F32) * factor)
        clipped.append(both[0])
        new_weights.append(weight - rate * (both[1] + DECAY_MATRIX * weight))
        begin_at = begin_at + span_of
    clipped_vectors = vector_total * factor
    new_table, table_one, table_two = adamw(
        embed_table, table_first, table_second, table_shard * factor, RATE_TABLE, DECAY_TABLE
    )
    new_vectors, vector_one, vector_two = adamw(
        vectors, vector_first, vector_second, clipped_vectors, RATE_VECTOR, 0.0
    )
    loss = jnp.stack([bce_total, count_total, scaled_con])
    return (
        loss,
        grad_norm,
        new_weights[0],
        new_weights[1],
        new_weights[2],
        new_weights[3],
        clipped[0],
        clipped[1],
        clipped[2],
        clipped[3],
        new_left.reshape(stats_left.shape),
        new_right.reshape(stats_right.shape),
        new_table,
        table_one,
        table_two,
        new_vectors,
        vector_one,
        vector_two,
        clipped_vectors[:tail_at],
    )


def solution(mesh):
    owners, tensor_ranks = mesh.shape["dp"], mesh.shape["tensor"]
    split = Mesh(mesh.devices.reshape(owners, tensor_ranks // 2, 2), EVERY)
    both = ("x", "core")
    placed = (
        P("dp", None),
        P("dp", None),
        P("dp"),
        P(),
        P(EVERY, None),
        P(EVERY, None),
        P(EVERY, None),
        P(),
        P(),
        P(),
        P(None, None, None, both, "dp", None),
        P(None, both, None, "dp", None),
        P(None, None, both, "dp", None),
        P(None, both, None, "dp", None),
        P(both, "dp", None, None, None),
        P(both, "dp", None, None, None),
        P(both, "dp", None, None, None),
        P(both, "dp", None, None, None),
    )
    matrices = placed[10:14]
    return jax.shard_map(
        shards,
        mesh=split,
        in_specs=placed,
        out_specs=(P(), P())
        + matrices
        + matrices
        + placed[14:16]
        + placed[4:7]
        + (P(), P(), P(), P()),
        check_vma=False,
    )
```

```python
import math

import jax
import jax.numpy as jnp
from jax import lax
from jax.experimental import pallas as pl
from jax.experimental.pallas import tpu as pltpu
from jax.sharding import Mesh
from jax.sharding import PartitionSpec as P

D = 1024
HD = 64
FF = 4096
VOCAB = 30720
STEP = 10


PRECISE = lax.Precision.HIGHEST
EPS_NORM = 1e-05
EPS_UNIT = 1e-06
CLIP_NORM = 1.0
BETA_ONE = 0.9
BETA_TWO = 0.999
ADAM_EPS = 1e-08
STAT_DECAY = 0.95
RATE_TABLE = 0.06
RATE_VECTOR = 0.5
RATE_MATRIX = 0.5
RATE_OUT = 4.0
DECAY_TABLE = 0.01
DECAY_MATRIX = 0.01
CON_WEIGHT = 16.0
MASK_FILL = -1000000000.0

BF = jnp.bfloat16
F32 = jnp.float32
GROUP = ("dp", "x")
EVERY = ("dp", "x", "core")
ROW_SLOTS = 24


def layer_norm(values, gain, shift):
    centre = values - jnp.mean(values, axis=-1, keepdims=True)
    spread_sq = jnp.mean(centre * centre, axis=-1, keepdims=True)
    return centre * lax.rsqrt(spread_sq + EPS_NORM) * gain + shift


def norm_back(values, gain, shift, upstream):
    ignored, pull = jax.vjp(layer_norm, values, gain, shift)
    return pull(upstream)


def adamw(weight, first, second, grad, rate, decay):
    first = BETA_ONE * first + (1 - BETA_ONE) * grad
    second = BETA_TWO * second + (1 - BETA_TWO) * grad * grad
    fixed_first = first / (1 - BETA_ONE**STEP)
    fixed_second = second / (1 - BETA_TWO**STEP)
    return (
        weight - rate * (fixed_first / (jnp.sqrt(fixed_second) + ADAM_EPS) + decay * weight),
        first,
        second,
    )


def from_peer(values, axis, mask=1):
    size = lax.axis_size(axis)
    return lax.ppermute(values, axis, [(at, at ^ mask) for at in range(size)])


def peers():
    found = []
    for axis in ("core", "x", "dp"):
        mask = 1
        while mask < lax.axis_size(axis):
            found.append((axis, mask))
            mask = mask * 2
    return found


def halving_steps():
    masks = [1]
    while masks[-1] * 2 < lax.axis_size("dp"):
        masks.append(masks[-1] * 2)
    return masks


def halve(slots, step):
    mask = halving_steps()[step]
    dim = len(halving_steps()) - 1 - step
    bit = lax.axis_index("dp") // mask % 2
    away = lax.dynamic_index_in_dim(slots, 1 - bit, dim, keepdims=False)
    keep = lax.dynamic_index_in_dim(slots, bit, dim, keepdims=False)
    return keep + from_peer(away, "dp", mask)


def sum_over_all(values):
    for axis, mask in peers():
        values = values + from_peer(values, axis, mask)
    return values


def gather_small(values, steps=()):
    mask = 1
    while mask < lax.axis_size("dp"):
        steps = steps + (("dp", mask),)
        mask = mask * 2
    for axis, mask in steps:
        other = from_peer(values, axis, mask)
        first = lax.axis_index(axis) // mask % 2 == 0
        values = jnp.where(
            first,
            jnp.concatenate([values, other], axis=0),
            jnp.concatenate([other, values], axis=0),
        )
    return values


def tree():
    count = lax.axis_size("dp")
    holders = [count - 1]
    steps = []
    mask = count // 2
    while mask > 0:
        steps.append([(at, at ^ mask) for at in holders])
        holders = holders + [at ^ mask for at in holders]
        mask = mask // 2
    return steps


def last_to_near():
    count = lax.axis_size("dp") * lax.axis_size("x")
    return [(count - 1, count - 2)]


def from_last(parts):
    last = lax.axis_size("core") - 1
    value = jnp.where(lax.axis_index("core") == last, parts[last], from_peer(parts[0], "core"))
    half = value.shape[0] // 2
    near = lax.ppermute(value[:half], GROUP, last_to_near())
    return jnp.where(lax.axis_index("x") == 0, near, value[half:])


def spread_from(value, step):
    found = lax.ppermute(value, "dp", step)
    reached = jnp.any(lax.axis_index("dp") == jnp.array([there for here, there in step]))
    return jnp.where(reached, found, value)


def both_halves(value):
    other = from_peer(value, "x")
    first = lax.axis_index("x") == 0
    return jnp.where(
        first,
        jnp.concatenate([value, other], axis=0),
        jnp.concatenate([other, value], axis=0),
    )


def to_last(value):
    half = value.shape[0] // 2
    first = lax.axis_index("x") == 0
    away = jnp.where(first, value[half:], value[:half])
    total = jnp.where(first, value[:half], value[half:]).astype(F32)
    total = total + from_peer(away, "x").astype(F32)
    for step in reversed(tree()):
        back = [(there, here) for here, there in step]
        total = total + lax.ppermute(total.astype(BF), "dp", back).astype(F32)
    back = [(there, here) for here, there in last_to_near()]
    near = lax.ppermute(total.astype(BF), GROUP, back).astype(F32)
    total = jnp.concatenate([near, total], axis=0)
    return jnp.concatenate([from_peer(total.astype(BF), "core").astype(F32), total], axis=0)


def after(values, *first):
    return lax.optimization_barrier((values,) + first)[0]


def collect(values):
    across = from_peer(values, "x")
    return jnp.concatenate([values, from_peer(values, "core")], axis=0), across


def complete(across):
    return jnp.concatenate([across, from_peer(across, "core")], axis=0)


def spread_first(other):
    rows = other.shape[0] // 2
    away = other[:rows] + from_peer(other[rows:].astype(BF), "core").astype(F32)
    return away.astype(BF)


def spread_last(own, away):
    rows = own.shape[0] // 2
    near = own[:rows] + from_peer(own[rows:].astype(BF), "core").astype(F32)
    return near + from_peer(away, "x").astype(F32)


def column_sum(*members):
    return sum(jnp.sum(values.astype(F32), axis=0) for values in members)


def fetch(pieces):
    return lax.all_gather(pieces, "dp", axis=0, tiled=False)[:, None]


def layer_rows(in_proj, out_proj, up_proj, down_proj, layer_no):
    rows, width = in_proj.shape[-2:]
    row_blocks = in_proj.shape[1]
    feed = up_proj.shape[2]
    attend_rows = [
        in_proj[layer_no].reshape(row_blocks, 3, rows, width).transpose(1, 0, 2, 3),
        out_proj[layer_no].reshape(1, row_blocks, rows, width),
    ]
    return [
        jnp.concatenate(attend_rows, axis=0).astype(BF),
        up_proj[layer_no].reshape(row_blocks, feed, rows, width).astype(BF),
        down_proj[layer_no].reshape(feed, row_blocks, rows, width).astype(BF),
    ]


def named_layer(attend_all, up_all, down_all, row_blocks, feed):
    of_x = (1, attend_all.shape[1], 0)
    second = (3, row_blocks, 0)
    return (
        (attend_all, {"x": of_x, "low": (2, 3, 0), "high": second}),
        (attend_all, {"x": of_x, "low": second, "high": (2, 1, 3)}),
        (up_all[0], {"x": of_x, "low": second, "high": (2, row_blocks, up_all[1])}),
        (down_all[0], {"x": of_x, "low": second, "high": (2, feed, down_all[1])}),
    )


def wide():
    return pltpu.CompilerParams(vmem_limit_bytes=48 * 1024 * 1024)


def whole(shape):
    return pl.BlockSpec(shape, lambda step: (0,) * len(shape))


def columns_of(ref, at, width):
    if len(ref.shape) == 2:
        return ref[:, at * width : (at + 1) * width]
    per = ref.shape[2] // width
    return ref[at // per, :, at % per * width : (at % per + 1) * width]


def joined_rows(weights):
    if weights.shape[-2] % 16 == 0:
        return weights
    owners, ranks, first, second, rows, width = weights.shape
    moved = weights.transpose(1, 2, 3, 0, 4, 5)
    return moved.reshape(1, ranks, first, second, owners * rows, width)


def rows_product(left, weights, dims, over, across, outs, finish, by_column=()):
    weights = joined_rows(weights)
    owners, rows, width = weights.shape[0], weights.shape[4], weights.shape[5]
    side = owners * rows
    turned = "low" in over
    steps = 1
    for name in across:
        steps = steps * dims[name][1]
    tokens = left.shape[-2]
    block_sizes = [1] * 6
    block_sizes[0], block_sizes[4], block_sizes[5] = owners, rows, width
    for name in over:
        block_sizes[dims[name][0]] = dims[name][1]
    terms = [()]
    for name in over:
        terms = [term + (at,) for term in terms for at in range(dims[name][1])]

    def kernel(*refs):
        left_ref, weights_ref = refs[:2]
        total = None
        for number, term in enumerate(terms):
            at = [0] * 3
            for name, place in zip(over, term):
                at[dims[name][0] - 1] = place
            block = weights_ref[(slice(None),) + tuple(at)].reshape(side, width)
            part = columns_of(left_ref, number, side)
            contract = (((1,), (1 if turned else 0,)), ((), ()))
            term_out = lax.dot_general(part, block, contract, preferred_element_type=F32)
            total = term_out if total is None else total + term_out
        last_in = 2 + len(by_column)
        results = finish(total, *[ref[...] for ref in refs[2:last_in]])
        for ref, result in zip(refs[last_in:], results):
            ref[...] = result.astype(ref.dtype).reshape(ref.shape)

    def weights_at(step):
        place = [0] * 6
        for name in reversed(across):
            place[dims[name][0]] = dims[name][2] + lax.rem(step, dims[name][1])
            step = lax.div(step, dims[name][1])
        for name in over:
            place[dims[name][0]] = dims[name][2] // dims[name][1]
        return tuple(place)

    out_shapes = []
    out_specs = []
    for apart, dtype in outs:
        if apart == 1:
            out_shapes.append(jax.ShapeDtypeStruct((tokens, steps * side), dtype))
            out_specs.append(pl.BlockSpec((tokens, side), lambda step: (0, step)))
        else:
            per = steps // apart
            out_shapes.append(jax.ShapeDtypeStruct((apart, tokens, per * side), dtype))
            out_specs.append(
                pl.BlockSpec(
                    (1, tokens, side),
                    lambda step, per=per: (lax.div(step, per), 0, lax.rem(step, per)),
                )
            )
    work = steps * len(terms) * side * width
    return pl.pallas_call(
        kernel,
        grid=(steps,),
        in_specs=[whole(left.shape), pl.BlockSpec(tuple(block_sizes), weights_at)]
        + [
            pl.BlockSpec((member.shape[0], side), lambda step: (0, step)) for member in by_column
        ],
        out_specs=out_specs,
        out_shape=out_shapes,
        compiler_params=wide(),
        cost_estimate=pl.CostEstimate(
            flops=2 * tokens * work, bytes_accessed=2 * work + 2 * left.size, transcendentals=0
        ),
    )(left, weights, *by_column)


def block_grads(lefts, rights, ranks, high, low, side, x_on_left, owners=None):
    count = len(lefts)

    def kernel(*refs):
        step = pl.program_id(0)
        out_ref = refs[2 * count]
        for at in range(ranks if x_on_left else 1):
            begin = pl.multiple_of((at * high + step) * side, side)
            parts = [ref[:, pl.ds(begin, side)] for ref in refs[:count]]
            for low_at in range(low):
                for rank in range(1 if x_on_left else ranks):
                    if x_on_left:
                        number, target = low_at, at
                    elif len(refs[count].shape) == 3:
                        number, target = low_at * ranks + rank, rank
                    else:
                        number, target = rank * low + low_at, rank
                    total = None
                    for part, right_ref in zip(parts, refs[count : 2 * count]):
                        block = columns_of(right_ref, number, side)
                        term = lax.dot_general(
                            part, block, (((0,), (0,)), ((), ())), preferred_element_type=F32
                        )
                        total = term if total is None else total + term
                    if owners is None:
                        out_ref[low_at, target] = total.astype(BF)
                    else:
                        out_ref[low_at, target, 0] = total.astype(BF)

    if owners is None:
        out_spec = pl.BlockSpec((low, ranks, side, side), lambda step: (step, 0, 0, 0))
        out_shape = (high * low, ranks, side, side)
    else:
        per = owners // low
        out_spec = pl.BlockSpec(
            (low, ranks, 1, side, side),
            lambda step: (lax.rem(step, per), 0, lax.div(step, per), 0, 0),
        )
        out_shape = (owners, ranks, high * low // owners, side, side)
    return pl.pallas_call(
        kernel,
        grid=(high,),
        in_specs=[whole(member.shape) for member in tuple(lefts) + tuple(rights)],
        out_specs=out_spec,
        out_shape=jax.ShapeDtypeStruct(out_shape, BF),
        compiler_params=wide(),
        cost_estimate=pl.CostEstimate(
            flops=2 * count * lefts[0].shape[-2] * high * low * ranks * side * side,
            bytes_accessed=2 * high * low * ranks * side * side,
            transcendentals=0,
        ),
    )(*lefts, *rights)


PAIR = 2 * HD


def halves(values):
    lane = lax.broadcasted_iota(jnp.int32, values.shape, 1)
    nothing = jnp.zeros_like(values)
    return jnp.where(lane < HD, values, nothing), jnp.where(lane < HD, nothing, values)


def dot_nt(left, right):
    return lax.dot_general(left, right, (((1,), (1,)), ((), ())), preferred_element_type=F32)


def dot_nn(left, right):
    return lax.dot_general(left, right, (((1,), (0,)), ((), ())), preferred_element_type=F32)


def dot_tn(left, right):
    return lax.dot_general(left, right, (((0,), (0,)), ((), ())), preferred_element_type=F32)


def softmax_of(queries, keys_in, live):
    scores = dot_nt(queries, keys_in) * HD ** (-0.5)
    scores = jnp.where(live > 0, scores, MASK_FILL)
    grown = jnp.exp(scores - jnp.max(scores, axis=-1, keepdims=True))
    return grown / jnp.sum(grown, axis=-1, keepdims=True)


def attend_kernel(live_ref, qkv_ref, mixed_ref):
    live = live_ref[0]
    query_heads = halves(qkv_ref[0])
    value_heads = halves(qkv_ref[2])
    total = None
    for query, value in zip(query_heads, value_heads):
        weights = softmax_of(query, qkv_ref[1], live).astype(BF)
        part = dot_nn(weights, value)
        total = part if total is None else total + part
    mixed_ref[...] = total.astype(BF)


def attend_back_kernel(live_ref, qkv_ref, d_mixed_ref, d_qkv_ref):
    live = live_ref[0]
    query_heads = halves(qkv_ref[0])
    key_heads = halves(qkv_ref[1])
    d_heads = halves(d_mixed_ref[...])
    d_query = d_key = d_value = 0.0
    for query, key, d_out in zip(query_heads, key_heads, d_heads):
        weights = softmax_of(query, qkv_ref[1], live)
        d_value = d_value + dot_tn(weights.astype(BF), d_out)
        d_weights = dot_nt(d_out, qkv_ref[2])
        d_scores = weights * (
            d_weights - jnp.sum(weights * d_weights, axis=-1, keepdims=True)
        )
        d_scores = d_scores.astype(BF)
        d_query = d_query + dot_nn(d_scores, key)
        d_key = d_key + dot_tn(d_scores, query)
    scale_by = HD ** (-0.5)
    d_qkv_ref[0] = (d_query * scale_by).astype(BF)
    d_qkv_ref[1] = (d_key * scale_by).astype(BF)
    d_qkv_ref[2] = d_value.astype(BF)


def attend(qkv, live, d_mixed=None):
    seqs, slots = live.shape
    width = qkv.shape[2]
    pairs = width // PAIR
    mixed_spec = pl.BlockSpec((slots, PAIR), lambda seq, pair: (seq, pair))
    qkv_spec = pl.BlockSpec((3, slots, PAIR), lambda seq, pair: (0, seq, pair))
    specs = [pl.BlockSpec((1, 1, slots), lambda seq, pair: (seq, 0, 0)), qkv_spec]
    operands = [live.astype(F32).reshape(seqs, 1, slots), qkv]
    if d_mixed is None:
        out_spec, out_shape = mixed_spec, jax.ShapeDtypeStruct(qkv.shape[1:], BF)
        body, products = attend_kernel, 2
    else:
        specs.append(mixed_spec)
        operands.append(d_mixed)
        out_spec, out_shape = qkv_spec, jax.ShapeDtypeStruct(qkv.shape, BF)
        body, products = attend_back_kernel, 5
    return pl.pallas_call(
        body,
        grid=(seqs, pairs),
        in_specs=specs,
        out_specs=out_spec,
        out_shape=out_shape,
        compiler_params=wide(),
        cost_estimate=pl.CostEstimate(
            flops=2 * products * seqs * slots * slots * width * 2,
            bytes_accessed=2 * qkv.size * 2,
            transcendentals=seqs * slots * slots * width // HD,
        ),
    )(*operands)


def product(left, right):
    return jnp.dot(left, right, preferred_element_type=F32)


def product_tn(left, right):
    return lax.dot_general(left, right, (((0,), (0,)), ((), ())), preferred_element_type=F32)


def same(total):
    return (total,)


def plus(total, bias):
    return (total + bias,)


ROOT_HALF = 0.5**0.5
DENSITY = (2 * math.pi) ** (-0.5)


def plus_gelu(total, bias):
    total = total + bias
    return (total, total * (1.0 + lax.erf(total * ROOT_HALF)) * 0.5)


def times_gelu_slope(total, before):
    slope = 0.5 * (1.0 + lax.erf(before * ROOT_HALF)) + before * (
        DENSITY * jnp.exp(-0.5 * before * before)
    )
    return (total * slope,)


def layer_forward(residual, weights, pieces, keys_live):
    w_in, w_out, w_up, w_down = weights
    bias_q, bias_v, bias_up, bias_out, bias_down, gain_one, shift_one, gain_two, shift_two = pieces
    bias_in = jnp.concatenate([bias_q, jnp.zeros_like(bias_q), bias_v]).reshape(1, -1)

    def mix(rows, live):
        (projected,) = rows_product(
            rows, *w_in, ("high",), ("low", "x"), [(3, BF)], plus, [bias_in]
        )
        return projected, attend(projected, live)

    def mix_out(mixed):
        return rows_product(mixed, *w_out, ("x", "high"), ("low",), [(1, F32)], same)[0]

    def feed(rows):
        return rows_product(
            rows,
            *w_up,
            ("high",),
            ("x", "low"),
            [(1, F32), (1, BF)],
            plus_gelu,
            [bias_up.reshape(1, -1)],
        )

    def feed_out(active):
        return rows_product(active, *w_down, ("x", "high"), ("low",), [(1, F32)], same)[0]

    own, across = collect(residual.astype(BF))
    own_qkv, own_mixed = mix(own, keys_live[0])
    other = complete(after(across, own_mixed))
    other_qkv, other_mixed = mix(other, keys_live[1])
    away = spread_first(mix_out(other_mixed))
    own_out = mix_out(after(own_mixed, away))
    first_in = residual + (spread_last(own_out, away) + bias_out)
    middle = layer_norm(first_in, gain_one, shift_one)
    own_mid, across = collect(middle.astype(BF))
    own_pre, own_act = feed(own_mid)
    other_mid = complete(after(across, own_act))
    other_pre, other_act = feed(other_mid)
    away = spread_first(feed_out(other_act))
    own_out = feed_out(after(own_act, away))
    second_in = middle + (spread_last(own_out, away) + bias_down)
    kept_values = (
        first_in,
        second_in,
        (own, other),
        (own_qkv, other_qkv),
        (own_mixed, other_mixed),
        (own_mid, other_mid),
        (own_pre, other_pre),
        (own_act, other_act),
    )
    return (layer_norm(second_in, gain_two, shift_two), kept_values)


def layer_backward(upstream, kept_values, weights, pieces, keys_live, dealt, emit):
    (
        first_in,
        second_in,
        gathered,
        qkv,
        mixed,
        spread_mid,
        hidden_pre,
        hidden_act,
    ) = kept_values
    w_in, w_out, w_up, w_down = weights
    gain_one, shift_one, gain_two, shift_two = pieces[5:]
    ranks, side = w_in[1]["x"][1], w_in[0].shape[-1]
    row_blocks, feed = w_in[1]["high"][1], w_up[1]["low"][1]
    d_second, d_gain_two, d_shift_two = norm_back(second_in, gain_two, shift_two, upstream)
    d_fed = d_second.astype(BF)

    def feed_back(rows, before):
        return rows_product(
            rows, *w_down, ("low",), ("x", "high"), [(1, BF)], times_gelu_slope, [before]
        )[0]

    def up_back(rows):
        return rows_product(rows, *w_up, ("x", "low"), ("high",), [(1, F32)], same)[0]

    own, across = collect(d_fed)
    own_pre = feed_back(own, hidden_pre[0])
    other = complete(after(across, own_pre))
    other_pre = feed_back(other, hidden_pre[1])
    away = spread_first(up_back(other_pre))
    own = after(own, away)
    parts = block_grads(hidden_act, (own, other), ranks, feed, row_blocks, side, True, dealt["down"])
    own_pre = emit("down", parts, own_pre)
    d_pre = (own_pre, other_pre)
    parts = block_grads(spread_mid, d_pre, ranks, row_blocks, feed, side, False, dealt["up"])
    own_pre = emit("up", parts, own_pre)
    d_middle = d_second + spread_last(up_back(own_pre), away)
    d_first, d_gain_one, d_shift_one = norm_back(first_in, gain_one, shift_one, d_middle)
    d_branch = d_first.astype(BF)

    def mix_back(rows, projected, live):
        (d_mixed,) = rows_product(rows, *w_out, ("low",), ("x", "high"), [(1, BF)], same)
        return attend(projected, live, d_mixed)

    def in_back(rows):
        return rows_product(rows, *w_in, ("low", "x"), ("high",), [(1, F32)], same)[0]

    own, across = collect(d_branch)
    own_qkv = mix_back(own, qkv[0], keys_live[0])
    other = complete(after(across, own_qkv))
    other_qkv = mix_back(other, qkv[1], keys_live[1])
    away = spread_first(in_back(other_qkv))
    own = after(own, away)
    parts = block_grads(mixed, (own, other), ranks, 1, row_blocks, side, True)
    own_qkv = emit("out", parts, own_qkv)
    d_qkv = (own_qkv, other_qkv)
    parts = block_grads(gathered, d_qkv, ranks, row_blocks, 3, side, False)
    own_qkv = emit("in", parts, own_qkv)
    d_residual = d_first + spread_last(in_back(own_qkv), away)
    bias_grads = (
        column_sum(*[member[0] for member in d_qkv]),
        column_sum(*[member[2] for member in d_qkv]),
        column_sum(*d_pre),
        column_sum(d_branch),
        column_sum(d_fed),
        d_gain_one,
        d_shift_one,
        d_gain_two,
        d_shift_two,
    )
    return d_residual, bias_grads


def precise(left, right, dims):
    return lax.dot_general(
        left, right, (dims, ((), ())), precision=PRECISE, preferred_element_type=F32
    )


def contrast_kernel(scale_ref, pairs_ref, pooled_ref, loss_ref, d_scale_ref, d_pooled_ref):
    pooled = pooled_ref[...]
    count = pooled.shape[0]
    norm = lax.rsqrt(jnp.sum(pooled * pooled, axis=-1, keepdims=True) + EPS_UNIT)
    unit = pooled * norm
    row_at = lax.broadcasted_iota(jnp.int32, (count, count), 0)
    column_at = lax.broadcasted_iota(jnp.int32, (count, count), 1)
    picks = (pairs_ref[...] == column_at).astype(F32)
    same_at = (row_at == column_at).astype(F32)
    scale = jnp.exp(scale_ref[...])
    partner = precise(picks, unit, ((1,), (0,)))
    logits = scale * precise(unit, partner, ((1,), (1,)))
    total = 0.0
    slope = -2.0 * same_at
    for axis in (1, 0):
        highest = jnp.max(logits, axis=axis, keepdims=True)
        grown = jnp.exp(logits - highest)
        each = jnp.sum(grown, axis=axis, keepdims=True)
        total = total + jnp.sum(highest + jnp.log(each), keepdims=True)
        slope = slope + grown / each
    total = total - 2.0 * jnp.sum(logits * same_at, keepdims=True)
    weight = 0.5 * CON_WEIGHT
    loss_ref[...] = weight * total
    slope = weight * slope
    d_scale_ref[...] = jnp.sum(slope * logits, keepdims=True)
    slope = slope * scale
    d_partner = precise(slope, unit, ((0,), (0,)))
    d_unit = precise(slope, partner, ((1,), (0,))) + precise(picks, d_partner, ((0,), (0,)))
    along = jnp.sum(d_unit * pooled, axis=-1, keepdims=True)
    d_pooled_ref[...] = norm * d_unit - pooled * (norm * norm * norm * along)


def contrast(pooled, log_scale, pair_index):
    loss, d_scale, d_pooled = pl.pallas_call(
        contrast_kernel,
        out_shape=[
            jax.ShapeDtypeStruct((1, 1), F32),
            jax.ShapeDtypeStruct((1, 1), F32),
            jax.ShapeDtypeStruct(pooled.shape, F32),
        ],
        compiler_params=wide(),
    )(log_scale.reshape(1, 1), pair_index.reshape(-1, 1), pooled)
    return loss[0, 0], d_scale[0, 0], d_pooled


def split_dot(left, right):
    total = None
    parts = []
    for operand in (left, right):
        if operand.dtype == BF:
            parts.append((operand,))
        else:
            high = operand.astype(BF)
            parts.append((high, (operand - high.astype(F32)).astype(BF)))
    for at, first in enumerate(parts[0]):
        for second in parts[1][: 2 - at]:
            term = dot_nn(first, second)
            total = term if total is None else total + term
    return total


def precondition(blocks, left_roots, right_roots, taken, owners):
    count, side = blocks.shape[0], blocks.shape[-1]
    rows = side // owners

    def kernel(slots_ref, block_ref, left_ref, right_ref, out_ref):
        block = block_ref[0]
        result = split_dot(split_dot(left_ref[0], block), right_ref[0])
        out_ref[:, 0, 0] = block.reshape(owners, rows, side)
        out_ref[:, 1, 0] = result.astype(BF).reshape(owners, rows, side)

    root_spec = pl.BlockSpec((1, side, side), lambda step, slots_ref: (slots_ref[step], 0, 0))
    return pl.pallas_call(
        kernel,
        grid_spec=pltpu.PrefetchScalarGridSpec(
            num_scalar_prefetch=1,
            grid=(count,),
            in_specs=[
                pl.BlockSpec((1, side, side), lambda step, slots_ref: (step, 0, 0)),
                root_spec,
                root_spec,
            ],
            out_specs=pl.BlockSpec(
                (owners, 2, 1, rows, side), lambda step, slots_ref: (0, 0, step, 0, 0)
            ),
        ),
        out_shape=jax.ShapeDtypeStruct((owners, 2, count, rows, side), BF),
        compiler_params=wide(),
        cost_estimate=pl.CostEstimate(
            flops=10 * count * side**3, bytes_accessed=14 * blocks.size, transcendentals=0
        ),
    )(jnp.array(taken, jnp.int32), blocks, left_roots, right_roots)


def shards(
    token_ids,
    labels,
    lengths,
    pair_index,
    embed_table,
    table_first,
    table_second,
    vectors,
    vector_first,
    vector_second,
    in_proj,
    out_proj,
    up_proj,
    down_proj,
    stats_left,
    stats_right,
    root_left,
    root_right,
):
    seq_dev, seq_slots = token_ids.shape
    layers = in_proj.shape[0]
    owners = lax.axis_size("dp")
    ranks = lax.axis_size("x")
    cores = lax.axis_size("core")
    devices = owners * ranks * cores
    owner_rank = lax.axis_index("dp")
    rank = lax.axis_index("x")
    core = lax.axis_index("core")
    device = (owner_rank * ranks + rank) * cores + core
    per_layer = 8 * D + FF
    tail_at = layers * per_layer
    block_size = in_proj.shape[-1]
    rows_per = in_proj.shape[-2]
    row_blocks = in_proj.shape[1]
    feed_blocks = up_proj.shape[2]
    slot_count = stats_left.shape[2]
    seqs = seq_dev // ranks
    group_rows = seqs * seq_slots
    local_rows = group_rows // cores

    def mine(values):
        return lax.dynamic_slice_in_dim(
            values.reshape(-1), rank * group_rows + core * local_rows, local_rows
        )

    my_rows = core * local_rows + jnp.arange(local_rows)
    my_sequence = rank * seqs + my_rows // seq_slots
    my_length = jnp.take(lengths, my_sequence)
    counted = (my_rows % seq_slots < my_length).astype(F32)
    my_labels = mine(labels).astype(F32)
    turned = (jnp.arange(seq_slots) + core * local_rows) % seq_slots
    keys_live = [
        (turned < lax.dynamic_index_in_dim(lengths, which, 0, keepdims=False))[None]
        for which in (rank, rank ^ 1)
    ]

    (attend_0, up_0, down_0), (attend_1, up_1, down_1) = [
        layer_rows(in_proj, out_proj, up_proj, down_proj, layer_no) for layer_no in range(layers)
    ]
    rows_here = [
        jnp.concatenate(members, axis=0)
        for members in ((attend_0, up_0), (attend_1, down_0), (up_1, down_1))
    ]
    rows_here[0], token_ids = lax.optimization_barrier((rows_here[0], token_ids))

    shard_rows = embed_table.shape[0]
    last_base = VOCAB - (devices - 1) * shard_rows
    places_last = last_base >= 0 and local_rows * cores == seq_slots
    all_ids = gather_small(token_ids).reshape(-1)
    if places_last:
        place_rows = from_last(
            [
                embed_table[last_base + at * local_rows : last_base + (at + 1) * local_rows].astype(BF)
                for at in range(cores)
            ]
        )
        hops = tree()
        all_ids, place_rows = lax.optimization_barrier((all_ids, place_rows))
    by_device = all_ids.reshape(devices, local_rows)
    holder = by_device // shard_rows
    earlier = jnp.arange(local_rows)[None, :] < jnp.arange(local_rows)[:, None]
    turn = jnp.sum(
        ((holder[:, :, None] == holder[:, None, :]) & earlier[None]).astype(jnp.int32), axis=2
    )
    rounds = jnp.max(turn) // ROW_SLOTS + 1
    own_index = by_device - device * shard_rows
    my_holder = lax.dynamic_index_in_dim(holder, device, 0, keepdims=False)
    my_turn = lax.dynamic_index_in_dim(turn, device, 0, keepdims=False)

    def plan(round_no):
        first = round_no * ROW_SLOTS
        here = (holder == device)[:, None, :] & (
            turn[:, None, :] - first == jnp.arange(ROW_SLOTS)[None, :, None]
        )
        row_of_slot = jnp.sum(jnp.where(here, own_index[:, None, :] + 1, 0), axis=2).reshape(-1)
        inside = (my_turn >= first) & (my_turn < first + ROW_SLOTS)
        my_slot = jnp.where(inside, my_holder * ROW_SLOTS + my_turn - first, -1)
        slot_of_token = (jnp.arange(devices * ROW_SLOTS)[:, None] == my_slot[None, :]).astype(BF)
        return row_of_slot, slot_of_token

    def exchange(filled):
        return lax.all_to_all(filled, EVERY, split_axis=0, concat_axis=0, tiled=True)

    def rows_to_send(round_no):
        rows = jnp.maximum(plan(round_no)[0] - 1, 0)
        return jnp.take(embed_table, rows, axis=0).astype(BF)

    def rows_reached(round_no, reached):
        return product_tn(plan(round_no)[1], reached)

    def rows_to_return(round_no, grads):
        return product(plan(round_no)[1], grads).astype(BF)

    def rows_returned(round_no, reached):
        row_of_slot = plan(round_no)[0]
        picker = (row_of_slot[None, :] == 1 + jnp.arange(shard_rows)[:, None]).astype(BF)
        return product(picker, reached)

    def full_rows():
        table = lax.all_gather(embed_table.astype(BF), "dp", axis=0, tiled=True)
        tensor_ranks = ranks * cores

        def lookup(row_index):
            block_at = row_index // shard_rows
            inside = block_at % tensor_ranks == rank * cores + core
            at_row = block_at // tensor_ranks * shard_rows + row_index % shard_rows
            picked = jnp.take(table, jnp.where(inside, at_row, 0), axis=0)
            return jnp.where(inside[:, None], picked, jnp.zeros((), BF))

        rows = lookup(token_ids.reshape(-1))
        rows = rows + lookup(VOCAB + jnp.arange(rows.shape[0]) % seq_slots)
        return lax.psum_scatter(rows, ("x", "core"), scatter_dimension=0, tiled=True).astype(F32)

    fetched = [fetch(rows) for rows in rows_here]
    if places_last:
        place_rows = spread_from(place_rows, hops[0])
        filled, place_rows = lax.optimization_barrier((rows_to_send(0), place_rows))
        for step in hops[1:]:
            place_rows = spread_from(place_rows, step)
        reached, fetched[0] = lax.optimization_barrier((exchange(filled), fetched[0]))
        token_rows = lax.fori_loop(
            1,
            rounds,
            lambda at, rows: rows + rows_reached(at, exchange(rows_to_send(at))),
            rows_reached(0, reached),
        )
        embedded = token_rows + both_halves(place_rows).astype(F32)
    else:
        embedded = full_rows()

    def by_rank(base_at, width):
        return lax.dynamic_slice_in_dim(vectors, base_at + (rank * cores + core) * width, width)

    head_width = D // (ranks * cores)
    feed_width = FF // (ranks * cores)

    def pieces_of(layer_no):
        base_at = layer_no * per_layer
        others = vectors[base_at + 2 * D + FF : base_at + per_layer].reshape(6, D)
        return (
            by_rank(base_at, head_width),
            by_rank(base_at + D, head_width),
            by_rank(base_at + 2 * D, feed_width),
        ) + tuple(others)

    gain_embed = vectors[tail_at : tail_at + D]
    shift_embed = vectors[tail_at + D : tail_at + 2 * D]
    head_weight = vectors[tail_at + 2 * D : tail_at + 3 * D]
    residual = layer_norm(embedded, gain_embed, shift_embed)
    kept_all = []
    weights_all = []
    first, middle, last = fetched
    placed_at = (
        (first, (first, 4), (middle, 4)),
        (middle, (last, 0), (last, row_blocks)),
    )
    for layer_no in range(layers):
        weights = named_layer(*placed_at[layer_no], row_blocks, feed_blocks)
        residual, kept_values = layer_forward(
            residual, weights, pieces_of(layer_no), keys_live
        )
        kept_all.append(kept_values)
        weights_all.append(weights)

    logits_tok = jnp.dot(residual, head_weight, precision=PRECISE) + vectors[tail_at + 3 * D]
    bce_part = jnp.sum(counted * (jax.nn.softplus(logits_tok) - my_labels * logits_tok))
    count_part = jnp.sum(counted)
    token_weight = counted / my_length.astype(F32)
    here_sequence = my_rows // seq_slots
    chooser = (here_sequence[None, :] == jnp.arange(seqs)[:, None]).astype(F32) * token_weight[None, :]
    pooled_here = jnp.dot(chooser, residual, precision=PRECISE)
    pooled = gather_small(pooled_here + from_peer(pooled_here, "core"), (("x", 1),))
    global_sequence = owner_rank * seq_dev + my_sequence

    scaled_con, d_scale, d_pooled = contrast(pooled, vectors[tail_at + 3 * D + 1], pair_index)
    d_logit = counted * (jax.nn.sigmoid(logits_tok) - my_labels)
    if seqs == 1:
        d_rows = lax.dynamic_slice_in_dim(d_pooled, owner_rank * seq_dev + rank, 1, axis=0)
    else:
        d_rows = jnp.take(d_pooled, global_sequence, axis=0)
    upstream = d_logit[:, None] * head_weight[None, :] + token_weight[:, None] * d_rows
    d_head_weight = jnp.dot(d_logit, residual, precision=PRECISE)
    d_head_bias = jnp.sum(d_logit)
    leader = (device == 0).astype(F32)

    counts = {
        "in": row_blocks * 3,
        "out": row_blocks,
        "up": row_blocks * feed_blocks,
        "down": feed_blocks * row_blocks,
    }
    starts = {}
    begin_at = 0
    for name in ("in", "out", "up", "down"):
        starts[name] = begin_at
        begin_at = begin_at + layers * counts[name]
    block_count = begin_at
    dealt = {
        name: owners if counts[name] % owners == 0 and starts[name] % owners == 0 else None
        for name in counts
    }
    ready = {}
    ready_slots = {}
    summed = {}
    sends = []
    halved = []

    def slot_parts(slot):
        if slot in ready_slots:
            array, at = ready_slots[slot]
            return array[:, :, at]
        numbers = range(slot * owners, (slot + 1) * owners)
        members = []
        at = 0
        while at < owners:
            number = numbers[at]
            if number >= block_count:
                members.append(jnp.zeros((owners - at, 1, block_size, block_size), BF))
                break
            array, offset = ready[number]
            span = 1
            while at + span < owners and ready.get(number + span, (None, 0))[0] is array:
                span = span + 1
            members.append(array[offset : offset + span])
            at = at + span
        return jnp.concatenate(members, axis=0)

    def once_there(slots, values):
        sums = jnp.stack([summed[slot] for slot in slots])
        values, sums = lax.optimization_barrier((values, sums))
        for at, slot in enumerate(slots):
            summed[slot] = sums[at]
        return values

    def sum_ready(next_in):
        taken = []
        for slot in range(slot_count):
            numbers = range(slot * owners, min((slot + 1) * owners, block_count))
            if slot not in summed and (
                slot in ready_slots or all(number in ready for number in numbers)
            ):
                taken.append(slot)
        if not taken:
            return next_in
        outgoing = jnp.concatenate([slot_parts(slot) for slot in taken], axis=1)
        next_in, outgoing = lax.optimization_barrier((next_in, outgoing))
        if len(sends) < 2:
            arrived = lax.psum_scatter(
                outgoing.reshape((-1,) + outgoing.shape[2:]), "dp", scatter_dimension=0, tiled=True
            )
        else:
            bits = (2,) * len(halving_steps())
            halved.append(halve(outgoing.reshape(bits + outgoing.shape[1:]), 0))
            sends.append(taken)
            return next_in
        for at, slot in enumerate(taken):
            summed[slot] = arrived[at]
        sends.append(taken)
        return next_in

    flat_stats = (slot_count, block_size, block_size)
    left_root = root_left.reshape(flat_stats)
    right_root = root_right.reshape(flat_stats)
    returned = [None] * slot_count

    def send_back(taken, next_in=None, wait=True):
        some = jnp.stack([summed[slot] for slot in taken])
        if rows_per % 16 == 0:
            outgoing = precondition(some, left_root, right_root, taken, owners)
        else:

            def roots(array):
                return jnp.stack([array[slot] for slot in taken])

            direction = jnp.einsum(
                "sij,sjk->sik",
                jnp.einsum(
                    "sij,sjk->sik", roots(left_root), some.astype(F32), precision=lax.Precision.HIGH
                ),
                roots(right_root),
                precision=lax.Precision.HIGH,
            )
            both = jnp.stack([some, direction.astype(BF)])
            outgoing = both.reshape(2, len(taken), owners, rows_per, block_size).transpose(
                2, 0, 1, 3, 4
            )
        if not wait:
            next_in, outgoing = lax.optimization_barrier((next_in, outgoing))
        back = lax.all_to_all(outgoing, "dp", split_axis=0, concat_axis=0, tiled=True)
        if next_in is not None and wait:
            next_in, back = lax.optimization_barrier((next_in, back))
        for at, slot in enumerate(taken):
            returned[slot] = (back, at)
        return next_in

    def emit_of(layer_no):
        def emit(name, value, next_in):
            next_in, value = lax.optimization_barrier((next_in, value))
            first = starts[name] + layer_no * counts[name]
            if dealt[name]:
                for at in range(counts[name] // owners):
                    ready_slots[first // owners + at] = (value, at)
            else:
                for at in range(counts[name]):
                    ready[first + at] = (value, at)
            if name == "down" and layer_no == 0 and sends:
                next_in = once_there(sends[0], next_in)
            if name == "up" or (name == "in" and layer_no == 0):
                next_in = sum_ready(next_in)
            if name == "out" and layer_no == 0 and len(sends) > 1:
                next_in = send_back(sends[0], next_in, False)
            return next_in

        return emit

    def placed(piece, width):
        row = jnp.zeros((ranks * cores * width,), F32)
        return lax.dynamic_update_slice(row, piece, ((rank * cores + core) * width,))

    bias_parts = [None] * layers

    def vector_rows_of(layer_no):
        grad_items = bias_parts[layer_no]
        return [
            placed(grad_items[0], head_width),
            placed(grad_items[1], head_width),
            placed(grad_items[2], feed_width),
        ] + list(grad_items[3:])

    for layer_no in reversed(range(layers)):
        upstream, bias_parts[layer_no] = layer_backward(
            upstream,
            kept_all[layer_no],
            weights_all[layer_no],
            pieces_of(layer_no),
            keys_live,
            dealt,
            emit_of(layer_no),
        )

    d_embed, d_gain_embed, d_shift_embed = norm_back(embedded, gain_embed, shift_embed, upstream)
    d_embed = d_embed.astype(BF)
    if returned[sends[0][0]] is not None:
        d_embed, back, halved = lax.optimization_barrier(
            (d_embed, returned[sends[0][0]][0], halved)
        )
        for at, slot in enumerate(sends[0]):
            returned[slot] = (back, at)
    last_step = len(halving_steps()) - 1
    halved = [halve(slots, 1) for slots in halved]
    if places_last:
        reached = exchange(rows_to_return(0, d_embed))
        if halved:
            before = sends[-2]
            sums = jnp.stack([summed[slot] for slot in before])
            reached, halved, sums = lax.optimization_barrier((reached, halved, sums))
            for at, slot in enumerate(before):
                summed[slot] = sums[at]
        table_shard = lax.fori_loop(
            1,
            rounds,
            lambda at, total: total + rows_returned(at, exchange(rows_to_return(at, d_embed))),
            rows_returned(0, reached),
        )
        place_grads = to_last(d_embed)
        table_shard = table_shard.at[last_base : last_base + seq_slots].add(
            jnp.where(device == devices - 1, place_grads, 0.0)
        )
    else:
        d_rows = lax.all_gather(d_embed, EVERY, axis=0, tiled=True)
        held = device * shard_rows + jnp.arange(shard_rows)
        all_places = VOCAB + jnp.arange(all_ids.shape[0]) % seq_slots
        picker = (all_ids[None, :] == held[:, None]).astype(BF) + (
            all_places[None, :] == held[:, None]
        ).astype(BF)
        table_shard = product(picker, d_rows)

    for slots in halved:
        for step in range(2, last_step + 1):
            slots = halve(slots, step)
        slots = send_back(sends[-2], slots, False)
        for at, slot in enumerate(sends[-1]):
            summed[slot] = slots[at]

    blocks_low = jnp.stack([summed[slot] for slot in range(slot_count)])
    blocks = blocks_low.astype(F32)
    squares = jnp.sum(table_shard * table_shard) + jnp.sum(blocks * blocks)
    for taken in sends:
        if returned[taken[0]] is None:
            squares = send_back(taken, squares, False)
    vector_rows = []
    for layer_no in range(layers):
        vector_rows = vector_rows + vector_rows_of(layer_no)
    scalars = jnp.stack([d_head_bias, leader * d_scale, bce_part, count_part, squares])
    totals = jnp.concatenate(vector_rows + [d_gain_embed, d_shift_embed, d_head_weight, scalars])
    totals = sum_over_all(totals)
    vector_total = totals[:-3]
    bce_total, count_total, square_total = totals[-3], totals[-2], totals[-1]
    grad_norm = jnp.sqrt(square_total + jnp.sum(vector_total * vector_total))
    factor = CLIP_NORM / jnp.maximum(grad_norm, CLIP_NORM)

    square_of = factor * factor * (1 - STAT_DECAY)
    new_left = STAT_DECAY * stats_left.reshape(blocks.shape) + square_of * jnp.einsum(
        "sij,skj->sik", blocks_low, blocks_low, preferred_element_type=F32
    )
    new_right = STAT_DECAY * stats_right.reshape(blocks.shape) + square_of * jnp.einsum(
        "sji,sjk->sik", blocks_low, blocks_low, preferred_element_type=F32
    )
    matrices = (in_proj, out_proj, up_proj, down_proj)
    new_weights = []
    clipped = []
    begin_at = 0
    rates = (RATE_MATRIX, RATE_OUT, RATE_MATRIX, RATE_MATRIX)
    for weight, rate in zip(matrices, rates):
        span_of = weight.size // (rows_per * block_size)
        numbers = range(begin_at, begin_at + span_of)
        both = []
        for kind in range(2):
            pieces = []
            for slot in range(numbers[0] // owners, numbers[-1] // owners + 1):
                back, at = returned[slot]
                low = max(numbers[0] - slot * owners, 0)
                high = min(numbers[-1] + 1 - slot * owners, owners)
                pieces.append(back[low:high, kind, at])
            both.append(jnp.concatenate(pieces, axis=0).reshape(weight.shape).astype(F32) * factor)
        clipped.append(both[0])
        new_weights.append(weight - rate * (both[1] + DECAY_MATRIX * weight))
        begin_at = begin_at + span_of
    clipped_vectors = vector_total * factor
    new_table, table_one, table_two = adamw(
        embed_table, table_first, table_second, table_shard * factor, RATE_TABLE, DECAY_TABLE
    )
    new_vectors, vector_one, vector_two = adamw(
        vectors, vector_first, vector_second, clipped_vectors, RATE_VECTOR, 0.0
    )
    loss = jnp.stack([bce_total, count_total, scaled_con])
    return (
        loss,
        grad_norm,
        new_weights[0],
        new_weights[1],
        new_weights[2],
        new_weights[3],
        clipped[0],
        clipped[1],
        clipped[2],
        clipped[3],
        new_left.reshape(stats_left.shape),
        new_right.reshape(stats_right.shape),
        new_table,
        table_one,
        table_two,
        new_vectors,
        vector_one,
        vector_two,
        clipped_vectors[:tail_at],
    )


def solution(mesh):
    owners, tensor_ranks = mesh.shape["dp"], mesh.shape["tensor"]
    split = Mesh(mesh.devices.reshape(owners, tensor_ranks // 2, 2), EVERY)
    both = ("x", "core")
    placed = (
        P("dp", None),
        P("dp", None),
        P("dp"),
        P(),
        P(EVERY, None),
        P(EVERY, None),
        P(EVERY, None),
        P(),
        P(),
        P(),
        P(None, None, None, both, "dp", None),
        P(None, both, None, "dp", None),
        P(None, None, both, "dp", None),
        P(None, both, None, "dp", None),
        P(both, "dp", None, None, None),
        P(both, "dp", None, None, None),
        P(both, "dp", None, None, None),
        P(both, "dp", None, None, None),
    )
    matrices = placed[10:14]
    return jax.shard_map(
        shards,
        mesh=split,
        in_specs=placed,
        out_specs=(P(), P())
        + matrices
        + matrices
        + placed[14:16]
        + placed[4:7]
        + (P(), P(), P(), P()),
        check_vma=False,
    )
```
